128 devices in a mesh: space: 16 (over z, y), mp: 8 (over x, core).
Axes of the slice: x: 4, y: 4, z: 4, core: 2. Of those that a mesh axis runs over, the one named last changes fastest.
Arguments:
- points: bfloat16 [32768, 512], P('space'), may hold values from -6 to 6
- cotangent: bfloat16 [32768, 512], P('space'), may hold values from -6 to 6
- cell_counts: int32 [2048], P('space'), may hold values from 8 to 16
- norm_gain: float32 [512], replicated, may hold values from 0.1 to 1.9
- w_qkv: bfloat16 [512, 1536], P(None, 'mp'), as said below
- w_proj: bfloat16 [512, 512], P('mp'), may hold values from -0.25 to 0.25
Outputs:
- grad_points: bfloat16 [32768, 512], P('space', 'mp')
- grad_qkv: float32 [512, 1536], P('space', 'mp')
- grad_proj: float32 [512, 512], P('mp', 'space')
The draws below stay inside these ranges and needn't reach their ends.
Inputs may be any that keep to these rules, and one draw needn't show every extreme that they name: `w_qkv`: columns ordered by head, then query, key, value, then the 16 channels of a head.
All inputs are finite; a program needn't handle non-finite values.
Results may differ from the reference program's by a relative error of at most 0.025.
The reference program's roundings to bfloat16 on the way count: a program that leaves them out, or rounds other values in their place, can miss the bound.
Values may be sent and summed in bfloat16 or wider, within the bound.
No kernel may reach another device: no remote copies, remote signals or barrier semaphores. Data moves between devices by JAX's collectives and lax.ppermute only.
A program may use at most 128 MiB of HBM per device.

```python
import jax
import jax.numpy as jnp
from jax import lax

D = 512
H = 32
PATCH = 1024
NCELLS = 2048
N_PTS = 32768
N_SPACE = 16
N_MP = 8


def draw_w_qkv(key, part):
    key = jax.random.fold_in(key, 11)
    base = jax.random.normal(key, (D, 3 * D), jnp.float32) * D ** (-0.5)
    return base.astype(jnp.bfloat16)


def plant(entries, own_key, low, largest):
    index_at = [jax.random.randint(jax.random.fold_in(own_key, axis), (), 0, length) for axis, length in enumerate(entries.shape)]
    main_axis = entries.shape.index(max(entries.shape))
    next_to = index_at[:main_axis] + [(index_at[main_axis] + 1) % entries.shape[main_axis]] + index_at[main_axis + 1:]
    return entries.at[tuple(index_at)].set(low).at[tuple(next_to)].set(largest)


def steps_of(stream_key, dims, shards, smallest, high):
    def one(dim, blocks):
        heights = jax.random.uniform(jax.random.fold_in(jax.random.fold_in(stream_key, 6), dim), (blocks,), jnp.float32, smallest / len(shards), high / len(shards))
        return jnp.repeat(jnp.exp(heights), dims[dim] // blocks).reshape((-1,) + (1,) * (len(dims) - dim - 1))

    loudness = one(*shards[0])
    for cut in shards[1:]:
        loudness = loudness * one(*cut)
    return loudness


def gaussian(key, extent, width, reach, cuts=(), held_as=jnp.bfloat16):
    loudness = steps_of(key, extent, cuts, -0.22, 0.18) if cuts else 1.0
    array = jax.random.normal(key, extent, jnp.float32) * width * loudness
    return jnp.minimum(jnp.maximum(array, -reach), reach).astype(held_as)


def setup_inputs(seed: int = 0) -> dict:
    arg_keys = jax.random.split(jax.random.key(seed), 7)
    points = gaussian(arg_keys[0], (N_PTS, D), 1.0, 6.0, ((0, 16),))
    cotangent = gaussian(arg_keys[1], (N_PTS, D), 1.0, 6.0, ((0, 16),))
    cell_counts = plant(jax.random.randint(arg_keys[2], (NCELLS,), 8, 17), jax.random.fold_in(arg_keys[2], 1), 8, 16).astype(jnp.int32)
    norm_gain = jnp.clip(1.0 + 0.18 * jax.random.normal(arg_keys[3], (D,), jnp.float32), 0.1, 1.9)
    w_qkv = draw_w_qkv(jax.random.fold_in(arg_keys[6], 71), 0)
    w_proj = gaussian(arg_keys[5], (D, D), D ** -0.5, 0.25, ((0, 8),))
    return dict(points=points, cotangent=cotangent, cell_counts=cell_counts, norm_gain=norm_gain, w_qkv=w_qkv, w_proj=w_proj)


EPS = 1e-05
MASKED = -1e+30

def norm_rows(matrix, gain_vec):
    as_f32 = matrix.astype(jnp.float32)
    center = as_f32 - lax.optimization_barrier(jnp.mean(as_f32, axis=-1, keepdims=True))
    spread = lax.rsqrt(lax.optimization_barrier(jnp.mean(center * center, axis=-1, keepdims=True)) + EPS)
    normed = center * spread
    return (normed, spread, (normed * gain_vec).astype(jnp.bfloat16))

def patch_grads(inputs):
    query_rows, key_rows, value_rows, up_rows, key_bias = inputs
    attn_scale = query_rows.shape[-1] ** (-0.5)
    query_wide = query_rows.astype(jnp.float32)
    key_wide = key_rows.astype(jnp.float32)
    value_wide = value_rows.astype(jnp.float32)
    up_wide = up_rows.astype(jnp.float32)
    scores = jnp.einsum('hqe,hke->hqk', query_wide, key_wide) * attn_scale + key_bias[None, None, :]
    row_max = lax.optimization_barrier(jnp.max(scores, axis=-1, keepdims=True))
    exp_scores = jnp.exp(scores - row_max)
    prob_wide = exp_scores / lax.optimization_barrier(jnp.sum(exp_scores, axis=-1, keepdims=True))
    probs_low = prob_wide.astype(jnp.bfloat16)
    attended = jnp.einsum('hqk,hke->hqe', probs_low.astype(jnp.float32), value_wide).astype(jnp.bfloat16)
    dprob = jnp.einsum('hqe,hke->hqk', up_wide, value_wide)
    row_delta = lax.optimization_barrier(jnp.sum(prob_wide * dprob, axis=-1, keepdims=True))
    dscore = (prob_wide * (dprob - row_delta) * attn_scale).astype(jnp.bfloat16)
    dscore_wide = dscore.astype(jnp.float32)
    grad_q = jnp.einsum('hqk,hke->hqe', dscore_wide, key_wide).astype(jnp.bfloat16)
    grad_k = jnp.einsum('hqk,hqe->hke', dscore_wide, query_wide).astype(jnp.bfloat16)
    grad_v = jnp.einsum('hqk,hqe->hke', probs_low.astype(jnp.float32), up_wide).astype(jnp.bfloat16)
    return (attended, grad_q, grad_k, grad_v)

def reference(points, cotangent, cell_counts, norm_gain, w_qkv, w_proj):
    n_total = points.shape[0]
    dev_rows = n_total // N_SPACE
    feat_width = points.shape[1]
    head_size = feat_width // H
    counts = lax.optimization_barrier(jnp.sum(cell_counts.reshape(N_SPACE, -1), axis=1, dtype=jnp.int32))
    starts = jnp.cumsum(counts, dtype=jnp.int32) - counts
    slot_ids = jnp.arange(dev_rows, dtype=jnp.int32)
    position = starts[:, None] + slot_ids[None, :]
    is_alive = slot_ids[None, :] < counts[:, None]
    target = jnp.where(is_alive, position, n_total).reshape(-1).astype(jnp.int32)
    packed_x = jnp.zeros_like(points).at[target].set(points, mode='drop')
    packed_dy = jnp.zeros_like(cotangent).at[target].set(cotangent, mode='drop')
    filled = jnp.sum(counts, dtype=jnp.int32)
    key_bias = jnp.where(jnp.arange(n_total, dtype=jnp.int32) < filled, 0.0, MASKED).astype(jnp.float32)
    normed, spread, normed_low = norm_rows(packed_x, norm_gain)
    proj_qkv = jnp.dot(normed_low, w_qkv, preferred_element_type=jnp.float32).astype(jnp.bfloat16)
    upstream = jnp.dot(packed_dy, w_proj.T, preferred_element_type=jnp.float32).astype(jnp.bfloat16)
    n_patch = n_total // PATCH
    arranged = proj_qkv.reshape(n_patch, PATCH, H, 3, head_size).transpose(0, 3, 2, 1, 4)
    up_heads = upstream.reshape(n_patch, PATCH, H, head_size).transpose(0, 2, 1, 3)
    attended, grad_q, grad_k, grad_v = lax.map(patch_grads, (arranged[:, 0], arranged[:, 1], arranged[:, 2], up_heads, key_bias.reshape(n_patch, PATCH)))
    attended_rows = attended.transpose(0, 2, 1, 3).reshape(n_total, feat_width)
    dqkv = jnp.stack([grad_q, grad_k, grad_v], axis=2)
    dqkv = dqkv.transpose(0, 3, 1, 2, 4).reshape(n_total, 3 * feat_width)
    grad_proj = jnp.dot(attended_rows.T, packed_dy, preferred_element_type=jnp.float32)
    grad_qkv = jnp.dot(normed_low.T, dqkv, preferred_element_type=jnp.float32)
    group_cols = 3 * feat_width // N_MP
    dunit = jnp.zeros((n_total, feat_width), jnp.float32)
    for member in range(N_MP):
        du_term = jnp.dot(dqkv[:, member * group_cols:(member + 1) * group_cols], w_qkv[:, member * group_cols:(member + 1) * group_cols].T, preferred_element_type=jnp.float32)
        dunit = dunit + lax.optimization_barrier(du_term.astype(jnp.bfloat16)).astype(jnp.float32)
    scaled = dunit * norm_gain
    dnorm = spread * (scaled - lax.optimization_barrier(jnp.mean(scaled, axis=-1, keepdims=True)) - normed * lax.optimization_barrier(jnp.mean(scaled * normed, axis=-1, keepdims=True)))
    dpacked = (packed_dy.astype(jnp.float32) + dnorm).astype(jnp.bfloat16)
    gathered = jnp.take(dpacked, jnp.clip(position, 0, n_total - 1).reshape(-1).astype(jnp.int32), axis=0)
    grad_points = jnp.where(is_alive.reshape(-1)[:, None], gathered, jnp.zeros((), jnp.bfloat16))
    return (grad_points, grad_qkv, grad_proj)
```

```python
import functools

import jax
import jax.numpy as jnp
from jax import lax
from jax.experimental import pallas as pl
from jax.experimental.pallas import tpu as pltpu
from jax.sharding import PartitionSpec as P

H = 32
PATCH = 1024
EPS = 1e-05
MASKED = -1e30
HEAD = 16
GROUP = 64
LANES = 256
BLOCK = 256
SHIFT = 128
MIB = 1024 * 1024

BF = jnp.bfloat16
F32 = jnp.float32
NT = (((1,), (1,)), ((), ()))
TN = (((0,), (0,)), ((), ()))


def dot(a, b):
    return jnp.dot(a, b, preferred_element_type=F32)


def dot_nt(a, b):
    return lax.dot_general(a, b, NT, preferred_element_type=F32)


def dot_tn(a, b):
    return lax.dot_general(a, b, TN, preferred_element_type=F32)


def iota(shape, axis):
    return lax.broadcasted_iota(jnp.int32, shape, axis)


def onehot(mask):
    return jnp.where(mask, 1.0, 0.0).astype(BF)


def split(value):
    high = value.astype(BF)
    return high, (value - high.astype(F32)).astype(BF)


def project_kernel(
    sc_ref, x_ref, dy_ref, gain_ref, wqkv_ref, wproj_ref, spread_ref,
    qkvu_ref, unit_ref, own_ref, stat_ref, wide_ref, wg_ref, wup_ref,
):
    rows = x_ref.shape[0]
    width = x_ref.shape[1]
    gain = gain_ref[...]

    @pl.when(pl.program_id(0) == 0)
    def _():
        wide = dot(wqkv_ref[...], spread_ref[...]).astype(BF)
        wide_ref[...] = wide
        lane = iota((LANES, GROUP), 0)
        part = iota((LANES, GROUP), 1)
        up = onehot(lane == (part // HEAD) * GROUP + 3 * HEAD + part % HEAD)
        wup_ref[...] = dot(up, wproj_ref[...]).astype(BF)
        gain_high, gain_low = split(jnp.broadcast_to(gain, (16, width)))
        wg = dot(gain_high, wide) + dot(gain_low, wide)
        wg_high, wg_low = split(wg)
        row = iota((16, LANES), 0)
        zero = jnp.zeros((16, LANES), F32)
        wg_ref[...] = jnp.where(
            row == 0, wg_high.astype(F32), jnp.where(row == 1, wg_low.astype(F32), zero)
        ).astype(BF)

    x_low = x_ref[...]
    x = x_low.astype(F32)
    mean = jnp.mean(x, axis=-1, keepdims=True)
    center = x - mean
    spread = lax.rsqrt(jnp.mean(center * center, axis=-1, keepdims=True) + EPS)
    unit = (center * spread * gain).astype(BF)
    unit_ref[...] = unit
    dy = dy_ref[...]
    qkvu_ref[...] = (dot(unit, wide_ref[...]) + dot_nt(dy, wup_ref[...])).astype(BF)
    own_cols = own_ref.shape[0] // 2
    pick = onehot(
        iota((own_cols, width), 1) == iota((own_cols, width), 0) + sc_ref[4] * own_cols
    )
    own_ref[:own_cols, :] = dot_nt(pick, x_low).astype(BF)
    own_ref[own_cols:, :] = dot_nt(pick, dy).astype(BF)
    both = jnp.where(iota((rows, 128), 1) < 4, mean, spread)
    stat_ref[...] = both.T[:8, :]


def shift_rows(src_ref, total, first, low, high):
    base = jnp.clip((first // SHIFT) * SHIFT, 0, total - 2 * SHIFT)
    base = pl.multiple_of(base, SHIFT)
    row = iota((SHIFT, 2 * SHIFT), 0) + first
    col = iota((SHIFT, 2 * SHIFT), 1) + base
    pick = onehot((row == col) & (row >= low) & (row < high))
    return dot(pick, src_ref[pl.ds(base, 2 * SHIFT), :])


def attend_kernel(
    spanning, sc_ref, own_ref, next_ref, *rest
):
    if spanning:
        out_ref, out_next_ref = rest[:2]
        rest = rest[2:]
    else:
        out_ref = rest[0]
        rest = rest[1:]
    x_ref, keys_ref, moved_ref, flip_ref, score_ref, pair_ref, right_ref, sum_ref, turn_ref, done_ref = rest
    slots = own_ref.shape[0]
    head_len = sc_ref[0]
    count = sc_ref[1]
    n_patch = sc_ref[2]
    tail_len = sc_ref[3]

    def work():
        first = head_len + (PATCH * (n_patch - 1) if spanning else 0)

        def gather(i, carry):
            start = pl.multiple_of(i * SHIFT, SHIFT)
            piece = shift_rows(own_ref, slots, first + start, 0, count)
            if spanning:
                piece = piece + shift_rows(next_ref, PATCH, first + start - count, 0, tail_len)
            x_ref[pl.ds(start, SHIFT), :] = piece.astype(BF)
            return carry

        lax.fori_loop(0, PATCH // SHIFT, gather, 0)
        x = x_ref[...]
        if spanning:
            valid = count - first + tail_len
            row = iota((PATCH, LANES), 0)
            lane = iota((PATCH, LANES), 1)
            bias = jnp.where(row < valid, 0.0, MASKED)
            keys_ref[...] = jnp.where(lane == 3 * HEAD, bias, x.astype(F32)).astype(BF)
        lhs_ref = keys_ref if spanning else x_ref
        src = iota((LANES, LANES), 0)
        dst = iota((LANES, LANES), 1)
        sub = dst & (GROUP - 1)
        is_k = (sub >= HEAD) & (sub < 2 * HEAD)
        is_v = (sub >= 2 * HEAD) & (sub < 3 * HEAD)
        is_q = sub < HEAD
        is_u = sub >= 3 * HEAD
        move = onehot((is_k & (src == dst - HEAD)) | (is_v & (src == dst + HEAD)))
        moved_ref[...] = dot(x, move).astype(BF)
        scale = HEAD ** (-0.5)
        flip = jnp.where(src == dst, jnp.where(is_q | is_u, scale, 1.0), 0.0).astype(BF)
        flip_ref[...] = dot_nt(flip, x).astype(BF)
        sum_ref[...] = jnp.zeros_like(sum_ref)
        turn_ref[...] = jnp.zeros_like(turn_ref)

        def placed(piece, at):
            parts = []
            if at:
                parts.append(jnp.zeros((at, BLOCK), BF))
            parts.append(piece)
            if at + HEAD < LANES:
                parts.append(jnp.zeros((LANES - at - HEAD, BLOCK), BF))
            return jnp.concatenate(parts, axis=0)

        ones_row = onehot(
            (iota((LANES, BLOCK), 0) == 3 * HEAD)
        )

        def block(step, carry):
            start = pl.multiple_of(step * BLOCK, BLOCK)
            here = pl.ds(start, BLOCK)
            tops = []
            for h in range(4):
                at = h * GROUP
                right = placed(flip_ref[at : at + HEAD, here], at + HEAD)
                if spanning:
                    right = right + ones_row
                scores = dot(lhs_ref[...], right)
                score_ref[h] = scores
                tops.append(jnp.max(scores, axis=0, keepdims=True))
            for h in range(4):
                at = h * GROUP
                exps = jnp.exp(score_ref[h] - tops[h])
                inverse = 1.0 / jnp.sum(exps, axis=0, keepdims=True)
                score_ref[h] = exps
                probs = score_ref[h] * inverse
                low = probs.astype(BF)
                pair_ref[:, 2 * h * BLOCK : (2 * h + 1) * BLOCK] = low
                attended = dot(flip_ref[at + 2 * HEAD : at + 3 * HEAD, :], low)
                turn_ref[at + 3 * HEAD : at + 4 * HEAD, here] = attended
                up = flip_ref[at + 3 * HEAD : at + 4 * HEAD, here]
                delta = jnp.sum(up.astype(F32) * attended, axis=0, keepdims=True)
                dprob = dot(lhs_ref[...], placed(up, at + 2 * HEAD))
                dscore = (score_ref[h] * inverse * (dprob - delta)).astype(BF)
                pair_ref[:, (2 * h + 1) * BLOCK : (2 * h + 2) * BLOCK] = dscore
                grad_q = dot(flip_ref[at + HEAD : at + 2 * HEAD, :], dscore)
                turn_ref[at : at + HEAD, here] = grad_q
            moved = moved_ref[here, :]
            lane = iota((BLOCK, LANES), 1)
            zero = jnp.zeros((BLOCK, LANES), BF)
            for h in range(4):
                at = h * GROUP
                in_k = (lane >= at + HEAD) & (lane < at + 2 * HEAD)
                in_v = (lane >= at + 2 * HEAD) & (lane < at + 3 * HEAD)
                right_ref[2 * h * BLOCK : (2 * h + 1) * BLOCK, :] = jnp.where(in_v, moved, zero)
                right_ref[(2 * h + 1) * BLOCK : (2 * h + 2) * BLOCK, :] = jnp.where(in_k, moved, zero)
            sum_ref[...] += dot(pair_ref[...], right_ref[...])
            return carry

        lax.fori_loop(0, PATCH // BLOCK, block, 0)
        done_ref[...] = (sum_ref[...] + turn_ref[...].T).astype(BF)

        def scatter(i, carry):
            start = pl.multiple_of(i * SHIFT, SHIFT)
            piece = shift_rows(done_ref, PATCH, start - first, 0, jnp.minimum(PATCH, count - first))
            out_ref[pl.ds(start, SHIFT), :] = piece.astype(BF)
            return carry

        lax.fori_loop(0, slots // SHIFT, scatter, 0)
        if spanning:
            def scatter_next(i, carry):
                start = pl.multiple_of(i * SHIFT, SHIFT)
                piece = shift_rows(
                    done_ref, PATCH, start + count - first, 0, count - first + tail_len
                )
                out_next_ref[pl.ds(start, SHIFT), :] = piece.astype(BF)
                return carry

            lax.fori_loop(0, PATCH // SHIFT, scatter_next, 0)

    if spanning:
        work()
    else:
        pl.when(n_patch == 2)(work)

        @pl.when(n_patch < 2)
        def _():
            out_ref[...] = jnp.zeros_like(out_ref)


def weight_kernel(
    sc_ref, one_ref, two_ref, got_ref, unit_ref, dy_ref, qkvu_ref, wide_ref, wg_ref,
    keep_ref, send_ref, grads_ref, turned_ref, gu_ref, gy_ref,
):
    step = pl.program_id(0)
    steps = pl.num_programs(0)
    rows = one_ref.shape[0]
    core = sc_ref[5]
    cols = wide_ref.shape[0] // 8

    @pl.when(step == 0)
    def _():
        gu_ref[...] = jnp.zeros_like(gu_ref)
        gy_ref[...] = jnp.zeros_like(gy_ref)
        for side in range(2):
            for x in range(4):
                from_row = pl.multiple_of((2 * x + (core ^ side)) * cols, cols)
                to_row = (side * 4 + x) * cols
                turned_ref[to_row : to_row + cols, :] = wide_ref[pl.ds(from_row, cols), :]

    got = jnp.where(step < PATCH // rows, got_ref[...].astype(F32), 0.0)
    total = (one_ref[...].astype(F32) + two_ref[...].astype(F32) + got).astype(BF)
    gu_ref[...] += dot_tn(unit_ref[...], total)
    gy_ref[...] += dot_tn(dy_ref[...], total)
    du = dot_nt(turned_ref[...], total).astype(BF)
    half = 4 * cols
    keep_ref[:half, :] = du[:half]
    send_ref[:half, :] = du[half:]
    lane = iota((rows, LANES), 1) & (GROUP - 1)
    product = jnp.where(lane < 3 * HEAD, total.astype(F32) * qkvu_ref[...].astype(F32), 0.0)
    high, low = split(product)
    ones = jnp.ones((16, LANES), BF)
    second = (dot_nt(ones, high) + dot_nt(ones, low))[:1]
    first_rows = dot_nt(wg_ref[...], total)
    first = first_rows[:1] + first_rows[1:2]
    stats = pack_stats(first, second, rows)
    keep_ref[half:, :] = stats
    send_ref[half:, :] = stats

    @pl.when(step == steps - 1)
    def _():
        lane = iota(gu_ref.shape, 1) & (GROUP - 1)
        grads_ref[...] = jnp.where(lane < 3 * HEAD, gu_ref[...], gy_ref[...]).astype(BF)


def pack_stats(first, second, rows):
    row = iota((16, rows), 0)
    first_high = first.astype(BF).astype(F32)
    second_high = second.astype(BF).astype(F32)
    return jnp.where(
        row == 0,
        first_high,
        jnp.where(
            row == 1,
            first - first_high,
            jnp.where(row == 2, second_high, jnp.where(row == 3, second - second_high, 0.0)),
        ),
    ).astype(BF)


def pair_kernel(sc_ref, keep_ref, got_ref, out0_ref, out1_ref, out2_ref, out3_ref):
    x = sc_ref[6]
    rows = keep_ref.shape[1]
    half = keep_ref.shape[0] - 16
    cols = half // 4
    stats = keep_ref[half:, :].astype(F32) + got_ref[half:, :].astype(F32)
    packed = pack_stats(stats[0:1] + stats[1:2], stats[2:3] + stats[3:4], rows)
    for d, out_ref in enumerate((out0_ref, out1_ref, out2_ref, out3_ref)):
        at = pl.ds(pl.multiple_of(((x + d) % 4) * cols, cols), cols)
        out_ref[:cols, :] = (keep_ref[at, :].astype(F32) + got_ref[at, :].astype(F32)).astype(BF)
        out_ref[cols:, :] = packed


def finish_kernel(
    sc_ref, a_ref, b_ref, c_ref, d_ref, own_ref, stat_ref, gain_ref, grads_ref,
    points_ref, qkv_ref, proj_ref,
):
    step = pl.program_id(0)
    rows = a_ref.shape[1]
    cols = own_ref.shape[0] // 2
    width = gain_ref.shape[0]
    parts = [ref[...].astype(F32) for ref in (a_ref, b_ref, c_ref, d_ref)]
    total = (parts[0] + parts[1]) + (parts[2] + parts[3])
    gain = gain_ref[pl.ds(pl.multiple_of(sc_ref[4] * cols, cols), cols), :]
    mean = stat_ref[0:1, :]
    spread = stat_ref[4:5, :]
    normed = (own_ref[:cols, :].astype(F32) - mean) * spread
    first = (total[cols : cols + 1] + total[cols + 1 : cols + 2]) * (1.0 / width)
    second = (total[cols + 2 : cols + 3] + total[cols + 3 : cols + 4]) * (1.0 / width)
    dnorm = spread * (total[:cols] * gain - first - normed * second)
    out = own_ref[cols:, :].astype(F32) + dnorm
    slot = iota((cols, rows), 1) + step * rows
    out = jnp.where(slot < sc_ref[1], out, 0.0)
    points_ref[...] = out.T.astype(BF)

    @pl.when(step == 0)
    def _():
        grads = jnp.sum(grads_ref[...].astype(F32), axis=0)
        qkv_ref[...] = jnp.concatenate(
            [grads[:, h * GROUP : h * GROUP + 3 * HEAD] for h in range(4)], axis=1
        )
        proj = jnp.concatenate(
            [grads[:, h * GROUP + 3 * HEAD : (h + 1) * GROUP] for h in range(4)], axis=1
        )
        proj_ref[...] = proj.T


def whole(shape):
    return pl.BlockSpec(shape, lambda *_: (0,) * len(shape))


def call(kernel, sc, args, grid, in_specs, out_specs, out_shape, scratch, limit=48):
    return pl.pallas_call(
        kernel,
        grid_spec=pltpu.PrefetchScalarGridSpec(
            num_scalar_prefetch=1,
            grid=grid,
            in_specs=in_specs,
            out_specs=out_specs,
            scratch_shapes=scratch,
        ),
        out_shape=out_shape,
        compiler_params=pltpu.CompilerParams(vmem_limit_bytes=limit * MIB),
    )(sc, *args)


def project(sc, points, cotangent, gain, w_qkv, w_proj, spread):
    slots, width = points.shape
    cols = width // 8
    rows = 256
    shape = jax.ShapeDtypeStruct
    return call(
        project_kernel,
        sc,
        (points, cotangent, gain, w_qkv, w_proj, spread),
        (slots // rows,),
        [
            pl.BlockSpec((rows, width), lambda i, s: (i, 0)),
            pl.BlockSpec((rows, width), lambda i, s: (i, 0)),
            whole(gain.shape),
            whole(w_qkv.shape),
            whole(w_proj.shape),
            whole(spread.shape),
        ],
        [
            pl.BlockSpec((rows, LANES), lambda i, s: (i, 0)),
            pl.BlockSpec((rows, width), lambda i, s: (i, 0)),
            pl.BlockSpec((2 * cols, rows), lambda i, s: (0, i)),
            pl.BlockSpec((8, rows), lambda i, s: (0, i)),
            whole((width, LANES)),
            whole((16, LANES)),
        ],
        [
            shape((slots, LANES), BF),
            shape((slots, width), BF),
            shape((2 * cols, slots), BF),
            shape((8, slots), F32),
            shape((width, LANES), BF),
            shape((16, LANES), BF),
        ],
        [pltpu.VMEM((LANES, width), BF)],
    )


def attend(spanning, sc, own, following):
    slots = own.shape[0]
    shape = jax.ShapeDtypeStruct
    args = (own, following) if spanning else (own, own)
    outs = [shape((slots, LANES), BF)] + ([shape((PATCH, LANES), BF)] if spanning else [])
    result = call(
        functools.partial(attend_kernel, spanning),
        sc,
        args,
        (1,),
        [whole((slots, LANES)), whole((PATCH, LANES))],
        [whole(o.shape) for o in outs],
        outs,
        [
            pltpu.VMEM((PATCH, LANES), BF),
            pltpu.VMEM((PATCH, LANES), BF),
            pltpu.VMEM((PATCH, LANES), BF),
            pltpu.VMEM((LANES, PATCH), BF),
            pltpu.VMEM((4, PATCH, BLOCK), F32),
            pltpu.VMEM((PATCH, 8 * BLOCK), BF),
            pltpu.VMEM((8 * BLOCK, LANES), BF),
            pltpu.VMEM((PATCH, LANES), F32),
            pltpu.VMEM((LANES, PATCH), F32),
            pltpu.VMEM((PATCH, LANES), BF),
        ],
    )
    return result


def weights(sc, one, two, got, unit, dy, qkvu, wide, wg):
    slots, width = unit.shape
    rows = 256
    half = width // 2 + 16
    shape = jax.ShapeDtypeStruct
    by_rows = lambda i, s: (i, 0)
    last = PATCH // rows - 1
    return call(
        weight_kernel,
        sc,
        (one, two, got, unit, dy, qkvu, wide, wg),
        (slots // rows,),
        [
            pl.BlockSpec((rows, LANES), by_rows),
            pl.BlockSpec((rows, LANES), by_rows),
            pl.BlockSpec((rows, LANES), lambda i, s: (jnp.minimum(i, last), 0)),
            pl.BlockSpec((rows, width), by_rows),
            pl.BlockSpec((rows, width), by_rows),
            pl.BlockSpec((rows, LANES), by_rows),
            whole(wide.shape),
            whole(wg.shape),
        ],
        [
            pl.BlockSpec((half, rows), lambda i, s: (0, i)),
            pl.BlockSpec((half, rows), lambda i, s: (0, i)),
            whole((width, LANES)),
        ],
        [
            shape((half, slots), BF),
            shape((half, slots), BF),
            shape((width, LANES), BF),
        ],
        [
            pltpu.VMEM((width, LANES), BF),
            pltpu.VMEM((width, LANES), F32),
            pltpu.VMEM((width, LANES), F32),
        ],
    )


def pair_sum(sc, keep, got):
    total, slots = keep.shape
    cols = (total - 16) // 4 + 16
    rows = 512
    shape = jax.ShapeDtypeStruct((cols, slots), BF)
    spec = pl.BlockSpec((total, rows), lambda i, s: (0, i))
    out = pl.BlockSpec((cols, rows), lambda i, s: (0, i))
    return call(
        pair_kernel, sc, (keep, got), (slots // rows,), [spec] * 2, [out] * 4, [shape] * 4, []
    )


def finish(sc, parts, own, stat, gain_col, grads):
    cols, slots = own.shape
    cols //= 2
    n_space, weight_rows = grads.shape[:2]
    rows = 512
    shape = jax.ShapeDtypeStruct
    by_lanes = lambda i, s: (0, i)
    return call(
        finish_kernel,
        sc,
        (*parts, own, stat, gain_col, grads),
        (slots // rows,),
        [pl.BlockSpec((cols + 16, rows), by_lanes)] * 4
        + [
            pl.BlockSpec((2 * cols, rows), by_lanes),
            pl.BlockSpec((8, rows), by_lanes),
            whole(gain_col.shape),
            whole(grads.shape),
        ],
        [
            pl.BlockSpec((rows, cols), lambda i, s: (i, 0)),
            whole((weight_rows, 3 * GROUP)),
            whole((GROUP, weight_rows)),
        ],
        [
            shape((slots, cols), BF),
            shape((weight_rows, 3 * GROUP), F32),
            shape((GROUP, weight_rows), F32),
        ],
        [],
    )


def prefix(part, axis):
    size = lax.axis_size(axis)
    state = part
    step = 1
    while step < size:
        route = [(i, i + step) for i in range(size - step)]
        state = state + lax.ppermute(state, axis, route)
        step *= 2
    return state - part


def spread_matrix():
    column = jnp.arange(3 * GROUP)
    target = (column // (3 * HEAD)) * GROUP + column % (3 * HEAD)
    return (target[:, None] == jnp.arange(LANES)[None, :]).astype(BF)


def on_device(points, cotangent, cell_counts, norm_gain, w_qkv, w_proj):
    slots, width = points.shape
    n_space = lax.axis_size("space")
    n_mp = lax.axis_size("mp")
    place = lax.axis_index("space")
    member = lax.axis_index("mp")
    live = jnp.sum(cell_counts, dtype=jnp.int32)
    start = prefix(live.reshape(1), "space")[0]
    zero = jnp.zeros((), jnp.int32)
    where_i_am = jnp.stack([zero, zero, zero, zero, member, member % 2, member // 2, zero])
    qkvu, unit, own, stat, wide, wg = project(
        where_i_am, points, cotangent, norm_gain.reshape(1, width), w_qkv, w_proj, spread_matrix()
    )
    back = [(i + 1, i) for i in range(n_space - 1)]
    onward = [(i, i + 1) for i in range(n_space - 1)]
    following = lax.ppermute(qkvu[:PATCH], "space", back)
    head_len = (PATCH - start % PATCH) % PATCH
    tail_len = jnp.where(place == n_space - 1, 0, (PATCH - (start + live) % PATCH) % PATCH)
    n_patch = (live - head_len + PATCH - 1) // PATCH
    sc = jnp.stack(
        [head_len, live, n_patch, tail_len, member, member % 2, member // 2, zero]
    ).astype(jnp.int32)
    one, spill = attend(True, sc, qkvu, following)
    got = lax.ppermute(spill, "space", onward)
    two = attend(False, sc, qkvu, qkvu)[0]
    keep, send, grads = weights(sc, one, two, got, unit, cotangent, qkvu, wide, wg)
    swap = [(i, i ^ 1) for i in range(n_mp)]
    other = lax.ppermute(send, "mp", swap)
    grads = lax.all_to_all(
        grads.reshape(n_space, width // n_space, LANES), "space", 0, 0
    )
    parts = pair_sum(sc, keep, other)
    n_x = n_mp // 2
    received = [parts[0]]
    for d in range(1, n_x):
        route = [(i, (i + 2 * d) % n_mp) for i in range(n_mp)]
        received.append(lax.ppermute(parts[d], "mp", route))
    return tuple(finish(sc, received, own, stat, norm_gain.reshape(width, 1), grads))


def solution(mesh):
    return jax.shard_map(
        on_device,
        mesh=mesh,
        in_specs=(
            P("space", None),
            P("space", None),
            P("space"),
            P(),
            P(None, "mp"),
            P("mp", None),
        ),
        out_specs=(P("space", "mp"), P("space", "mp"), P("mp", "space")),
        check_vma=False,
    )
```

```python
import functools

import jax
import jax.numpy as jnp
from jax import lax
from jax.experimental import pallas as pl
from jax.experimental.pallas import tpu as pltpu
from jax.sharding import PartitionSpec as P

H = 32
PATCH = 1024
EPS = 1e-05
MASKED = -1e30
HEAD = 16
GROUP = 64
LANES = 256
PAIR = 128
BLOCK = 256
SHIFT = 128
MIB = 1024 * 1024
LOG2E = 1.4426950408889634
SAFE = 40.0

BF = jnp.bfloat16
F32 = jnp.float32
NT = (((1,), (1,)), ((), ()))
TN = (((0,), (0,)), ((), ()))


def dot(a, b):
    return jnp.dot(a, b, preferred_element_type=F32)


def dot_nt(a, b):
    return lax.dot_general(a, b, NT, preferred_element_type=F32)


def dot_tn(a, b):
    return lax.dot_general(a, b, TN, preferred_element_type=F32)


def iota(shape, axis):
    return lax.broadcasted_iota(jnp.int32, shape, axis)


def onehot(mask):
    return jnp.where(mask, 1.0, 0.0).astype(BF)


def split(value):
    high = value.astype(BF)
    return high, (value - high.astype(F32)).astype(BF)


def project_kernel(lead, sc_ref, x_ref, dy_ref, gain_ref, *rest):
    if lead:
        wqkv_ref, wproj_ref, spread_ref = rest[:3]
        outs = rest[4:]
        wide_ref, side_ref, wg_ref = outs[5:8]
    else:
        wide_ref, side_ref = rest[:2]
        outs = rest[8:]
    one_ref, two_ref, unit_ref, own_ref, stat_ref = outs[:5]
    rows, width = x_ref.shape
    cols = own_ref.shape[0] // 2
    gain = gain_ref[...]

    if lead:
        @pl.when(pl.program_id(0) == 0)
        def _():
            wide = dot_tn(wqkv_ref[...], spread_ref[...]).astype(BF)
            wide_ref[...] = wide
            part = iota((GROUP, LANES), 0)
            lane = iota((GROUP, LANES), 1)
            up = onehot(lane == (part // HEAD) * GROUP + 3 * HEAD + part % HEAD)
            side_ref[:, :LANES] = dot_tn(wproj_ref[...], up).astype(BF)
            row = iota((width, cols), 0)
            col = iota((width, cols), 1)
            pick = onehot(row == col + sc_ref[4] * cols)
            none = jnp.zeros((width, cols), BF)
            side_ref[:, LANES:] = jnp.concatenate([none, pick, pick, none], axis=1)
            gain_high, gain_low = split(jnp.broadcast_to(gain, (16, width)))
            wg = dot(gain_high, wide) + dot(gain_low, wide)
            wg_high, wg_low = split(wg)
            row = iota((16, LANES), 0)
            wg_ref[...] = jnp.where(
                row == 0, wg_high.astype(F32), jnp.where(row == 1, wg_low.astype(F32), 0.0)
            ).astype(BF)

    x_low = x_ref[...]
    x = x_low.astype(F32)
    mean = jnp.mean(x, axis=-1, keepdims=True)
    center = x - mean
    spread = lax.rsqrt(jnp.mean(center * center, axis=-1, keepdims=True) + EPS)
    unit = (center * spread * gain).astype(BF)
    unit_ref[...] = unit
    from_dy = dot(dy_ref[...], side_ref[:, : LANES + PAIR])
    qkvu = (dot(unit, wide_ref[...]) + from_dy[:, :LANES]).astype(BF)
    one_ref[...] = qkvu[:, :PAIR]
    two_ref[...] = qkvu[:, PAIR:]
    own = dot(x_low, side_ref[:, LANES + PAIR :]) + from_dy[:, LANES:]
    own_ref[...] = own.T.astype(BF)
    both = jnp.where(iota((rows, 128), 1) < 4, mean, spread)
    stat_ref[...] = both.T[:8, :]


def shift_rows(src_ref, total, first, low, high):
    base = jnp.clip((first // SHIFT) * SHIFT, 0, total - 2 * SHIFT)
    base = pl.multiple_of(base, SHIFT)
    row = iota((SHIFT, 2 * SHIFT), 0) + first
    col = iota((SHIFT, 2 * SHIFT), 1) + base
    pick = onehot((row == col) & (row >= low) & (row < high))
    return dot(pick, src_ref[pl.ds(base, 2 * SHIFT), :])


def attend_kernel(spanning, extra_args, sc_ref, own_ref, *rest):
    if spanning:
        next_ref = rest[0]
        out_ref, out_next_ref = rest[1 + extra_args : 3 + extra_args]
        rest = rest[3 + extra_args :]
    else:
        out_ref = rest[extra_args]
        rest = rest[1 + extra_args :]
    (x_ref, left_ref, flip_ref, value_ref, top_ref, exp_ref, low_ref, grad_ref, right_ref, sum_ref,
     turn_ref, done_ref) = rest
    slots = own_ref.shape[0]
    head_len = sc_ref[0]
    count = sc_ref[1]
    n_patch = sc_ref[2]
    tail_len = sc_ref[3]
    scale = HEAD ** (-0.5)

    def work():
        first = head_len + (PATCH * (n_patch - 1) if spanning else 0)

        def gather(i, carry):
            start = pl.multiple_of(i * SHIFT, SHIFT)
            piece = shift_rows(own_ref, slots, first + start, 0, count)
            if spanning:
                piece = piece + shift_rows(next_ref, PATCH, first + start - count, 0, tail_len)
            x_ref[pl.ds(start, SHIFT), :] = piece.astype(BF)
            return carry

        lax.fori_loop(0, PATCH // SHIFT, gather, 0, unroll=True)
        x = x_ref[...]
        src = iota((PAIR, PAIR), 0)
        dst = iota((PAIR, PAIR), 1)
        sub = dst & (GROUP - 1)
        keys = sub < 2 * HEAD
        move = onehot(
            ((sub < HEAD) & (src == dst + HEAD))
            | ((sub >= HEAD) & (sub < 3 * HEAD) & (src == dst))
        )
        lane = iota((PATCH, PAIR), 1) & (GROUP - 1)
        fixed = jnp.where((lane > 3 * HEAD) & (lane < 3 * HEAD + 4), 1.0, 0.0)
        if spanning:
            valid = count - first + tail_len
            row = iota((PATCH, PAIR), 0)
            fixed = jnp.where((lane == 3 * HEAD) & (row >= valid), MASKED, fixed)
        left_ref[...] = (dot(x, move) + fixed).astype(BF)
        flip = dot_nt(onehot(src == dst), x)
        flip_ref[...] = flip.astype(BF)
        square = flip * flip
        bounded = True
        for h in range(2):
            at = h * GROUP
            value_ref[h, :HEAD, :] = flip_ref[at + 2 * HEAD : at + 3 * HEAD, :]
            value_ref[h, HEAD:, :] = jnp.ones((HEAD, PATCH), BF)
            most_q = jnp.max(jnp.sum(square[at : at + HEAD], axis=0))
            most_k = jnp.max(jnp.sum(square[at + HEAD : at + 2 * HEAD], axis=0))
            bounded &= most_q * most_k * scale * scale <= SAFE * SAFE
        sum_ref[...] = jnp.zeros_like(sum_ref)
        turn_ref[...] = jnp.zeros_like(turn_ref)
        right_ref[...] = jnp.zeros_like(right_ref)
        top_ref[...] = jnp.zeros_like(top_ref)
        row = iota((HEAD, BLOCK), 0)

        def placed(pieces, h):
            zero = jnp.zeros((GROUP, BLOCK), BF)
            group = jnp.concatenate(pieces, axis=0)
            return jnp.concatenate([group, zero] if h % 2 == 0 else [zero, group], axis=0)

        nothing = jnp.zeros((HEAD, BLOCK), BF)

        def score_right(h, here, top):
            query = flip_ref[h * GROUP : h * GROUP + HEAD, here].astype(F32) * (scale * LOG2E)
            high, low = split(query)
            if top is None:
                extra = jnp.where(row == 0, 1.0, 0.0)
            else:
                top_high = top.astype(BF).astype(F32)
                top_mid = (top - top_high).astype(BF).astype(F32)
                top_low = top - top_high - top_mid
                extra = jnp.where(
                    row == 0,
                    1.0,
                    jnp.where(
                        row == 1,
                        -top_high,
                        jnp.where(row == 2, -top_mid, jnp.where(row == 3, -top_low, 0.0)),
                    ),
                )
            return placed([high, low, nothing, extra.astype(BF)], h)

        def block(step, carry):
            here = [
                pl.ds(pl.multiple_of((step * 2 + t // 2) * BLOCK, BLOCK), BLOCK) for t in range(4)
            ]

            @pl.when(jnp.logical_not(bounded))
            def _():
                for t in range(4):
                    scores = dot(left_ref[...], score_right(t % 2, here[t], None))
                    top_ref[t : t + 1, :] = jnp.max(scores, axis=0, keepdims=True)

            inverses = [None] * 4
            rights = [None] * 4
            spans = [slice(t * BLOCK, (t + 1) * BLOCK) for t in range(4)]

            def stage_exp(t):
                scores = dot(left_ref[...], score_right(t % 2, here[t], top_ref[t : t + 1, :]))
                exps = jnp.exp2(scores)
                exp_ref[t] = exps
                low_ref[:, spans[t]] = exps.astype(BF)

            def stage_sum(t):
                at = (t % 2) * GROUP
                result = dot(value_ref[t % 2], low_ref[:, spans[t]])
                inverse = 1.0 / result[HEAD : HEAD + 1]
                inverses[t] = inverse
                attended = result[:HEAD] * inverse
                turn_ref[at + 3 * HEAD : at + 4 * HEAD, here[t]] = attended
                up = flip_ref[at + 3 * HEAD : at + 4 * HEAD, here[t]].astype(F32)
                scaled = up * scale
                delta = jnp.sum(scaled * attended, axis=0, keepdims=True)
                delta_high = delta.astype(BF).astype(F32)
                extra = jnp.where(
                    row == 1, -delta_high, jnp.where(row == 2, delta_high - delta, 0.0)
                ).astype(BF)
                rights[t] = placed([nothing, nothing, scaled.astype(BF), extra], t % 2)
                query = flip_ref[at : at + HEAD, here[t]].astype(F32)
                right_ref[at + 2 * HEAD : at + 3 * HEAD, spans[t]] = (up * inverse).astype(BF)
                right_ref[
                    at + HEAD : at + 2 * HEAD, (4 + t) * BLOCK : (5 + t) * BLOCK
                ] = (query * inverse).astype(BF)

            def stage_grad(t):
                dprob = dot(left_ref[...], rights[t])
                grad_ref[:, spans[t]] = (exp_ref[t] * dprob).astype(BF)

            def stage_query(t):
                at = (t % 2) * GROUP
                result = dot(flip_ref[at + HEAD : at + 2 * HEAD, :], grad_ref[:, spans[t]])
                turn_ref[at : at + HEAD, here[t]] = result * inverses[t]

            for stage in (stage_exp, stage_sum, stage_grad, stage_query):
                for t in range(4):
                    stage(t)
            sum_ref[...] += dot_nt(low_ref[...], right_ref[:, : 4 * BLOCK]) + dot_nt(
                grad_ref[...], right_ref[:, 4 * BLOCK :]
            )
            return carry

        lax.fori_loop(0, PATCH // (2 * BLOCK), block, 0)
        done_ref[...] = (sum_ref[...] + turn_ref[...].T).astype(BF)

        def scatter(i, carry):
            start = pl.multiple_of(i * SHIFT, SHIFT)
            piece = shift_rows(done_ref, PATCH, start - first, 0, jnp.minimum(PATCH, count - first))
            out_ref[pl.ds(start, SHIFT), :] = piece.astype(BF)
            return carry

        lax.fori_loop(0, slots // SHIFT, scatter, 0, unroll=True)
        if spanning:
            def scatter_next(i, carry):
                start = pl.multiple_of(i * SHIFT, SHIFT)
                piece = shift_rows(
                    done_ref, PATCH, start + count - first, 0, count - first + tail_len
                )
                out_next_ref[pl.ds(start, SHIFT), :] = piece.astype(BF)
                return carry

            lax.fori_loop(0, PATCH // SHIFT, scatter_next, 0, unroll=True)

    if spanning:
        work()
    else:
        pl.when(n_patch == 2)(work)

        @pl.when(n_patch < 2)
        def _():
            out_ref[...] = jnp.zeros_like(out_ref)


def product_kernel(
    sc_ref, a_ref, b_ref, c_ref, d_ref, e_ref, f_ref, one_ref, two_ref, wide_ref, wg_ref,
    keep_ref, send_ref, total_ref, turned_ref,
):
    step = pl.program_id(0)
    rows = a_ref.shape[0]
    core = sc_ref[5]
    cols = wide_ref.shape[0] // 8

    @pl.when(step == 0)
    def _():
        for side in range(2):
            for x in range(4):
                from_row = pl.multiple_of((2 * x + (core ^ side)) * cols, cols)
                to_row = (side * 4 + x) * cols
                turned_ref[to_row : to_row + cols, :] = wide_ref[pl.ds(from_row, cols), :]

    here = step < PATCH // rows
    sums = []
    for refs in ((a_ref, c_ref, e_ref), (b_ref, d_ref, f_ref)):
        got = jnp.where(here, refs[2][...].astype(F32), 0.0)
        sums.append(refs[0][...].astype(F32) + refs[1][...].astype(F32) + got)
    wide_total = jnp.concatenate(sums, axis=1)
    total = wide_total.astype(BF)
    total_ref[...] = total
    du = dot_nt(turned_ref[...], total).astype(BF)
    half = 4 * cols
    keep_ref[:half, :] = du[:half]
    send_ref[:half, :] = du[half:]
    lane = iota((rows, LANES), 1) & (GROUP - 1)
    qkvu = jnp.concatenate([one_ref[...], two_ref[...]], axis=1).astype(F32)
    product = jnp.where(lane < 3 * HEAD, wide_total * qkvu, 0.0)
    high, low = split(product)
    ones = jnp.ones((16, LANES), BF)
    second = (dot_nt(ones, high) + dot_nt(ones, low))[:1]
    first_rows = dot_nt(wg_ref[...], total)
    first = first_rows[:1] + first_rows[1:2]
    stats = pack_stats(first, second, rows)
    keep_ref[half:, :] = stats
    send_ref[half:, :] = stats


def weight_kernel(sc_ref, total_ref, unit_ref, dy_ref, after_ref, grads_ref, gu_ref, gy_ref):
    step = pl.program_id(0)

    @pl.when(step == 0)
    def _():
        gu_ref[...] = jnp.zeros_like(gu_ref)
        gy_ref[...] = jnp.zeros_like(gy_ref)

    total = total_ref[...]
    gu_ref[...] += dot_tn(total, unit_ref[...])
    gy_ref[...] += dot_tn(total, dy_ref[...])

    @pl.when(step == pl.num_programs(0) - 1)
    def _():
        row = iota(gu_ref.shape, 0) & (GROUP - 1)
        grads_ref[...] = jnp.where(row < 3 * HEAD, gu_ref[...], gy_ref[...]).T.astype(BF)


def pack_stats(first, second, rows):
    row = iota((16, rows), 0)
    first_high = first.astype(BF).astype(F32)
    second_high = second.astype(BF).astype(F32)
    return jnp.where(
        row == 0,
        first_high,
        jnp.where(
            row == 1,
            first - first_high,
            jnp.where(row == 2, second_high, jnp.where(row == 3, second - second_high, 0.0)),
        ),
    ).astype(BF)


def pair_kernel(sc_ref, keep_ref, got_ref, after_ref, out0_ref, out1_ref, out2_ref, out3_ref):
    x = sc_ref[6]
    rows = keep_ref.shape[1]
    half = keep_ref.shape[0] - 16
    cols = half // 4
    stats = keep_ref[half:, :].astype(F32) + got_ref[half:, :].astype(F32)
    packed = pack_stats(stats[0:1] + stats[1:2], stats[2:3] + stats[3:4], rows)
    for d, out_ref in enumerate((out0_ref, out1_ref, out2_ref, out3_ref)):
        at = pl.ds(pl.multiple_of(((x + d) % 4) * cols, cols), cols)
        out_ref[:cols, :] = (keep_ref[at, :].astype(F32) + got_ref[at, :].astype(F32)).astype(BF)
        out_ref[cols:, :] = packed


def finish_kernel(
    sc_ref, a_ref, b_ref, c_ref, d_ref, own_ref, stat_ref, gain_ref, grads_ref,
    points_ref, qkv_ref, proj_ref,
):
    step = pl.program_id(0)
    rows = a_ref.shape[1]
    cols = own_ref.shape[0] // 2
    width = gain_ref.shape[1]
    parts = [ref[...].astype(F32) for ref in (a_ref, b_ref, c_ref, d_ref)]
    total = (parts[0] + parts[1]) + (parts[2] + parts[3])
    mine = iota((cols, width), 1) == iota((cols, width), 0) + sc_ref[4] * cols
    gain = jnp.sum(jnp.where(mine, gain_ref[...], 0.0), axis=1, keepdims=True)
    mean = stat_ref[0:1, :]
    spread = stat_ref[4:5, :]
    normed = (own_ref[:cols, :].astype(F32) - mean) * spread
    first = (total[cols : cols + 1] + total[cols + 1 : cols + 2]) * (1.0 / width)
    second = (total[cols + 2 : cols + 3] + total[cols + 3 : cols + 4]) * (1.0 / width)
    dnorm = spread * (total[:cols] * gain - first - normed * second)
    out = own_ref[cols:, :].astype(F32) + dnorm
    slot = iota((cols, rows), 1) + step * rows
    points_ref[...] = jnp.where(slot < sc_ref[1], out, 0.0).astype(BF)

    @pl.when(step == 0)
    def _():
        grads = jnp.sum(grads_ref[...].astype(F32), axis=0)
        qkv_ref[...] = jnp.concatenate(
            [grads[:, h * GROUP : h * GROUP + 3 * HEAD] for h in range(4)], axis=1
        )
        proj_ref[...] = jnp.concatenate(
            [grads[:, h * GROUP + 3 * HEAD : (h + 1) * GROUP] for h in range(4)], axis=1
        )


def whole(shape):
    return pl.BlockSpec(shape, lambda *_: (0,) * len(shape))


ANY = pl.BlockSpec(memory_space=pl.ANY)
shape = jax.ShapeDtypeStruct


def call(kernel, sc, args, grid, in_specs, out_specs, out_shape, scratch, limit, micros, aliases={}):
    return pl.pallas_call(
        kernel,
        grid_spec=pltpu.PrefetchScalarGridSpec(
            num_scalar_prefetch=1,
            grid=grid,
            in_specs=in_specs,
            out_specs=out_specs,
            scratch_shapes=scratch,
        ),
        out_shape=out_shape,
        input_output_aliases=aliases,
        cost_estimate=pl.CostEstimate(
            flops=int(micros * 1.1e9), bytes_accessed=0, transcendentals=0
        ),
        compiler_params=pltpu.CompilerParams(vmem_limit_bytes=limit * MIB),
    )(sc, *args)


def project(sc, points, cotangent, gain, w_qkv, w_proj, spread, after):
    slots, width = points.shape
    cols = width // 8
    rows = 256
    steps = slots // (2 * rows)
    outs = [
        shape((slots, PAIR), BF),
        shape((slots, PAIR), BF),
        shape((slots, width), BF),
        shape((2 * cols, slots), BF),
        shape((8, slots), F32),
    ]
    extra = [shape((width, LANES), BF), shape((width, LANES + 2 * PAIR), BF), shape((16, LANES), BF)]

    def specs(offset):
        down = lambda i, s: (i + offset, 0)
        across = lambda i, s: (0, i + offset)
        return (
            [pl.BlockSpec((rows, width), down)] * 2 + [whole(gain.shape)],
            [pl.BlockSpec((rows, PAIR), down)] * 2
            + [
                pl.BlockSpec((rows, width), down),
                pl.BlockSpec((2 * cols, rows), across),
                pl.BlockSpec((8, rows), across),
            ],
        )

    ins, out_specs = specs(0)
    results = call(
        functools.partial(project_kernel, True),
        sc,
        (points, cotangent, gain, w_qkv, w_proj, spread, after[0]),
        (steps,),
        ins + [whole(w_qkv.shape), whole(w_proj.shape), whole(spread.shape), ANY],
        out_specs + [whole(e.shape) for e in extra],
        outs + extra,
        [],
        16,
        4.5,
    )
    ins, out_specs = specs(steps)
    again = call(
        functools.partial(project_kernel, False),
        sc,
        (points, cotangent, gain, results[5], results[6], *results[:5], after[1]),
        (steps,),
        ins + [whole(e.shape) for e in extra[:2]] + [ANY] * 6,
        out_specs,
        outs,
        [],
        16,
        4.0,
        {6 + i: i for i in range(5)},
    )
    return (*again, results[5], results[7])


def attend(spanning, sc, own, following, after):
    slots = own.shape[0]
    args = ((own, following) if spanning else (own,)) + tuple(after)
    outs = [shape((slots, PAIR), BF)] + ([shape((PATCH, PAIR), BF)] if spanning else [])
    return call(
        functools.partial(attend_kernel, spanning, len(after)),
        sc,
        args,
        (1,),
        [whole((slots, PAIR))] + ([whole((PATCH, PAIR))] if spanning else []) + [ANY] * len(after),
        [whole(o.shape) for o in outs],
        outs,
        [
            pltpu.VMEM((PATCH, PAIR), BF),
            pltpu.VMEM((PATCH, PAIR), BF),
            pltpu.VMEM((PAIR, PATCH), BF),
            pltpu.VMEM((2, 2 * HEAD, PATCH), BF),
            pltpu.VMEM((8, BLOCK), F32),
            pltpu.VMEM((4, PATCH, BLOCK), F32),
            pltpu.VMEM((PATCH, 4 * BLOCK), BF),
            pltpu.VMEM((PATCH, 4 * BLOCK), BF),
            pltpu.VMEM((PAIR, 8 * BLOCK), BF),
            pltpu.VMEM((PATCH, PAIR), F32),
            pltpu.VMEM((PAIR, PATCH), F32),
            pltpu.VMEM((PATCH, PAIR), BF),
        ],
        24,
        7.5,
    )


def products(sc, ones, twos, gots, heads, wide, wg):
    slots = ones[0].shape[0]
    width = wide.shape[0]
    rows = 256
    half = width // 2 + 16
    last = PATCH // rows - 1
    down = pl.BlockSpec((rows, PAIR), lambda i, s: (i, 0))
    first = pl.BlockSpec((rows, PAIR), lambda i, s: (jnp.minimum(i, last), 0))
    across = pl.BlockSpec((half, rows), lambda i, s: (0, i))
    return call(
        product_kernel,
        sc,
        (*ones, *twos, *gots, *heads, wide, wg),
        (slots // rows,),
        [down] * 4 + [first] * 2 + [down] * 2 + [whole(wide.shape), whole(wg.shape)],
        [across, across, pl.BlockSpec((rows, LANES), lambda i, s: (i, 0))],
        [shape((half, slots), BF), shape((half, slots), BF), shape((slots, LANES), BF)],
        [pltpu.VMEM((width, LANES), BF)],
        16,
        4.0,
    )


def weights(sc, total, unit, dy, after):
    slots, width = unit.shape
    rows = 512
    down = lambda i, s: (i, 0)
    return call(
        weight_kernel,
        sc,
        (total, unit, dy, after),
        (slots // rows,),
        [
            pl.BlockSpec((rows, LANES), down),
            pl.BlockSpec((rows, width), down),
            pl.BlockSpec((rows, width), down),
            ANY,
        ],
        [whole((width, LANES))],
        [shape((width, LANES), BF)],
        [pltpu.VMEM((LANES, width), F32), pltpu.VMEM((LANES, width), F32)],
        16,
        4.0,
    )[0]


def pair_sum(sc, keep, got, after):
    total, slots = keep.shape
    cols = (total - 16) // 4 + 16
    rows = 512
    spec = pl.BlockSpec((total, rows), lambda i, s: (0, i))
    out = pl.BlockSpec((cols, rows), lambda i, s: (0, i))
    return call(
        pair_kernel,
        sc,
        (keep, got, after),
        (slots // rows,),
        [spec] * 2 + [ANY],
        [out] * 4,
        [shape((cols, slots), BF)] * 4,
        [],
        16,
        2.3,
    )


def finish(sc, parts, own, stat, gain, grads):
    cols, slots = own.shape
    cols //= 2
    weight_rows = grads.shape[1]
    rows = 512
    across = lambda i, s: (0, i)
    points, qkv, proj = call(
        finish_kernel,
        sc,
        (*parts, own, stat, gain, grads),
        (slots // rows,),
        [pl.BlockSpec((cols + 16, rows), across)] * 4
        + [
            pl.BlockSpec((2 * cols, rows), across),
            pl.BlockSpec((8, rows), across),
            whole(gain.shape),
            whole(grads.shape),
        ],
        [
            pl.BlockSpec((cols, rows), across),
            whole((weight_rows, 3 * GROUP)),
            whole((weight_rows, GROUP)),
        ],
        [
            shape((cols, slots), BF),
            shape((weight_rows, 3 * GROUP), F32),
            shape((weight_rows, GROUP), F32),
        ],
        [],
        16,
        2.3,
    )
    return points.T, qkv, proj.T


def spread_matrix():
    column = jnp.arange(3 * GROUP)
    target = (column // (3 * HEAD)) * GROUP + column % (3 * HEAD)
    return (target[:, None] == jnp.arange(LANES)[None, :]).astype(BF)


def on_device(points, cotangent, cell_counts, norm_gain, w_qkv, w_proj):
    slots, width = points.shape
    n_space = lax.axis_size("space")
    n_mp = lax.axis_size("mp")
    place = lax.axis_index("space")
    member = lax.axis_index("mp")
    live = jnp.sum(cell_counts, dtype=jnp.int32)
    states = [live.reshape(1)]
    step = 1
    while step < n_space:
        route = [(i, i + step) for i in range(n_space - step)]
        states.append(states[-1] + lax.ppermute(states[-1], "space", route))
        step *= 2
    start = states[-1][0] - live
    zero = jnp.zeros((), jnp.int32)
    where_i_am = jnp.stack([zero, zero, zero, zero, member, member % 2, member // 2, zero])
    gain = norm_gain.reshape(1, width)
    one, two, unit, own, stat, wide, wg = project(
        where_i_am, points, cotangent, gain, w_qkv.T, w_proj, spread_matrix(), states[:2]
    )
    head_len = (PATCH - start % PATCH) % PATCH
    tail_len = jnp.where(place == n_space - 1, 0, (PATCH - (start + live) % PATCH) % PATCH)
    n_patch = (live - head_len + PATCH - 1) // PATCH
    sc = jnp.stack(
        [head_len, live, n_patch, tail_len, member, member % 2, member // 2, zero]
    ).astype(jnp.int32)
    back = [(i + 1, i) for i in range(n_space - 1)]
    onward = [(i, i + 1) for i in range(n_space - 1)]
    at = jnp.minimum(start, 0)
    following = [
        lax.ppermute(lax.dynamic_slice(rows, (at, zero), (PATCH, PAIR)), "space", back)
        for rows in (one, two)
    ]
    local_a = attend(False, sc, one, None, [])[0]
    mine_a, spill_a = attend(True, sc, one, following[0], [local_a])
    got_a = lax.ppermute(spill_a, "space", onward)
    mine_b, spill_b = attend(True, sc, two, following[1], [mine_a])
    got_b = lax.ppermute(spill_b, "space", onward)
    local_b = attend(False, sc, two, None, [mine_b])[0]
    keep, send, total = products(
        sc, (mine_a, mine_b), (local_a, local_b), (got_a, got_b), (one, two), wide, wg
    )
    swap = [(i, i ^ 1) for i in range(n_mp)]
    other = lax.ppermute(send, "mp", swap)
    grads = weights(sc, total, unit, cotangent, keep)
    gathered = lax.all_to_all(
        grads.reshape(n_space, width // n_space, LANES), "space", 0, 0
    )
    parts = pair_sum(sc, keep, other, grads)
    received = [parts[0]]
    for d in range(1, n_mp // 2):
        route = [(i, (i + 2 * d) % n_mp) for i in range(n_mp)]
        received.append(lax.ppermute(parts[d], "mp", route))
    return finish(sc, received, own, stat, gain, gathered)


def solution(mesh):
    return jax.shard_map(
        on_device,
        mesh=mesh,
        in_specs=(
            P("space", None),
            P("space", None),
            P("space"),
            P(),
            P(None, "mp"),
            P("mp", None),
        ),
        out_specs=(P("space", "mp"), P("space", "mp"), P("mp", "space")),
        check_vma=False,
    )
```

```python
import functools

import jax
import jax.numpy as jnp
from jax import lax
from jax.experimental import pallas as pl
from jax.experimental.pallas import tpu as pltpu
from jax.sharding import PartitionSpec as P

H = 32
PATCH = 1024
EPS = 1e-05
MASKED = -1e30
HEAD = 16
GROUP = 64
LANES = 256
PAIR = 128
BLOCK = 256
SHIFT = 128
MIB = 1024 * 1024
FULL = 60.5
LOG2E = 1.4426950408889634
SAFE = 40.0

BF = jnp.bfloat16
F32 = jnp.float32
NT = (((1,), (1,)), ((), ()))
TN = (((0,), (0,)), ((), ()))


def dot(a, b):
    return jnp.dot(a, b, preferred_element_type=F32)


def dot_nt(a, b):
    return lax.dot_general(a, b, NT, preferred_element_type=F32)


def dot_tn(a, b):
    return lax.dot_general(a, b, TN, preferred_element_type=F32)


def iota(shape, axis):
    return lax.broadcasted_iota(jnp.int32, shape, axis)


def onehot(mask):
    return jnp.where(mask, 1.0, 0.0).astype(BF)


def split(value):
    high = value.astype(BF)
    return high, (value - high.astype(F32)).astype(BF)


def project_kernel(
    x_hbm, dy_hbm, gain_hbm, wqkv_hbm, wproj_hbm,
    one_hbm, two_hbm, unit_hbm, head_hbm, own_ref, stat_ref, wide_ref, wg_ref,
    x_ref, dy_ref, gain_ref, wqkv_ref, wproj_ref, side_ref, qkvu_ref, unit_ref,
    row_sems, sems, out_sems,
):
    slots, width = x_ref.shape
    cols = own_ref.shape[0] // 2
    chunks = slots // BLOCK

    def rows_copy(i, which):
        src, dst = ((x_hbm, x_ref), (dy_hbm, dy_ref))[which]
        at = pl.ds(pl.multiple_of(i * BLOCK, BLOCK), BLOCK)
        return pltpu.make_async_copy(src.at[at], dst.at[at], row_sems.at[which, i])

    def out_copy(i, which):
        at = pl.ds(pl.multiple_of(i * BLOCK, BLOCK), BLOCK)
        src, dst = (
            (qkvu_ref.at[at, :PAIR], one_hbm),
            (qkvu_ref.at[at, PAIR:], two_hbm),
            (unit_ref.at[at], unit_hbm),
            (qkvu_ref.at[at], head_hbm),
        )[which]
        return pltpu.make_async_copy(src, dst.at[at], out_sems.at[which, i])

    pairs = ((wqkv_hbm, wqkv_ref), (wproj_hbm, wproj_ref), (gain_hbm, gain_ref))
    small = [pltpu.make_async_copy(src, dst, sems.at[i]) for i, (src, dst) in enumerate(pairs)]
    for copy in small:
        copy.start()
    for i in range(chunks):
        rows_copy(i, 0).start()
        rows_copy(i, 1).start()
    row = iota((width, cols), 0)
    col = iota((width, cols), 1)
    pick = onehot(row == col + lax.axis_index("mp") * cols)
    none = jnp.zeros((width, cols), BF)
    side_ref[:, LANES:] = jnp.concatenate([none, pick, pick, none], axis=1)
    for copy in small:
        copy.wait()
    gain = gain_ref[...]
    col = iota((3 * GROUP, LANES), 0)
    lane = iota((3 * GROUP, LANES), 1)
    head = sum(jnp.where(col >= 3 * HEAD * h, HEAD, 0) for h in range(1, 4))
    wide = dot_tn(wqkv_ref[...], onehot(lane == col + head)).astype(BF)
    wide_ref[...] = wide
    part = iota((GROUP, LANES), 0)
    lane = iota((GROUP, LANES), 1)
    head = sum(jnp.where(part >= HEAD * h, GROUP - HEAD, 0) for h in range(1, 4))
    up = onehot(lane == part + head + 3 * HEAD)
    side_ref[:, :LANES] = dot_tn(wproj_ref[...], up).astype(BF)
    gain_high, gain_low = split(jnp.broadcast_to(gain, (16, width)))
    wg_high, wg_low = split(dot(gain_high, wide) + dot(gain_low, wide))
    row = iota((16, LANES), 0)
    wg_ref[...] = jnp.where(
        row == 0, wg_high.astype(F32), jnp.where(row == 1, wg_low.astype(F32), 0.0)
    ).astype(BF)

    for i in range(chunks):
        rows_copy(i, 0).wait()
        rows_copy(i, 1).wait()
        at = slice(i * BLOCK, (i + 1) * BLOCK)
        x_low = x_ref[at, :]
        x = x_low.astype(F32)
        mean = jnp.mean(x, axis=-1, keepdims=True)
        center = x - mean
        spread = lax.rsqrt(jnp.mean(center * center, axis=-1, keepdims=True) + EPS)
        unit = (center * spread * gain).astype(BF)
        unit_ref[at, :] = unit
        from_dy = dot(dy_ref[at, :], side_ref[:, : LANES + PAIR])
        qkvu_ref[at, :] = (dot(unit, wide_ref[...]) + from_dy[:, :LANES]).astype(BF)
        for which in range(4 if i < PATCH // BLOCK else 3):
            out_copy(i, which).start()
        own = dot(x_low, side_ref[:, LANES + PAIR :]) + from_dy[:, LANES:]
        own_ref[:, at] = own.T.astype(BF)
        both = jnp.where(iota((BLOCK, 128), 1) < 4, mean, spread)
        stat_ref[:, at] = both.T[:8, :]
    for i in range(chunks):
        for which in range(4 if i < PATCH // BLOCK else 3):
            out_copy(i, which).wait()


def place_in_row(counts_ref):
    place = lax.axis_index("space")
    n_space = counts_ref.shape[0]
    start = jnp.int32(0)
    for i in range(n_space):
        start = start + jnp.where(i < place, counts_ref[i, 0, 0], 0)
    count = counts_ref[place, 0, 0]
    head_len = (PATCH - start % PATCH) % PATCH
    tail_len = jnp.where(place == n_space - 1, 0, (PATCH - (start + count) % PATCH) % PATCH)
    n_patch = (count - head_len + PATCH - 1) // PATCH
    return count, head_len, tail_len, n_patch


MARGIN = 2 * SHIFT


def shifter(first):
    part = first & (SHIFT - 1)
    pick = onehot(iota((SHIFT, 2 * SHIFT), 1) == iota((SHIFT, 2 * SHIFT), 0) + part)

    def block(src_ref, start):
        rows = src_ref.shape[0]
        base = jnp.clip(first - part + start + MARGIN, 0, rows - MARGIN)
        return dot(pick, src_ref[pl.ds(pl.multiple_of(base, SHIFT), 2 * SHIFT), :])

    return block


def padded(dst_ref, src_ref, limit, at):
    rows, width = src_ref.shape
    cols = slice(at, at + width)
    none = jnp.zeros((MARGIN, width), BF)
    dst_ref[:MARGIN, cols] = none
    dst_ref[MARGIN + rows :, cols] = none
    kept = iota(src_ref.shape, 0) < limit
    dst_ref[MARGIN : MARGIN + rows, cols] = jnp.where(
        kept, src_ref[...].astype(F32), 0.0
    ).astype(BF)


def attend_kernel(spanning, pairs, counts_ref, *rest):
    own_refs = rest[:pairs]
    if spanning:
        next_ref = rest[pairs]
        out_ref, out_next_ref = rest[pairs + 2 : pairs + 4]
        rest = rest[pairs + 4 :]
    else:
        out_ref = rest[pairs + 1]
        rest = rest[pairs + 2 :]
    (x_ref, left_ref, flip_ref, value_ref, top_ref, exp_ref, low_ref, grad_ref, turn_ref,
     done_ref, own_pad_ref, next_pad_ref) = rest
    slots = own_refs[0].shape[0]
    lanes = pairs * PAIR
    count, head_len, tail_len, n_patch = place_in_row(counts_ref)
    scale = HEAD ** (-0.5)

    def work():
        first = head_len + (PATCH * (n_patch - 1) if spanning else 0)

        for p in range(pairs):
            padded(own_pad_ref, own_refs[p], count, p * PAIR)
        from_own = shifter(first)
        if spanning:
            padded(next_pad_ref, next_ref, tail_len, 0)
            from_next = shifter(first - count)
        for start in range(0, PATCH, SHIFT):
            piece = from_own(own_pad_ref, start)
            if spanning:
                piece = piece + from_next(next_pad_ref, start)
            x_ref[start : start + SHIFT, :] = piece.astype(BF)
        x = x_ref[...]
        src = iota((lanes, lanes), 0)
        dst = iota((lanes, lanes), 1)
        sub = dst & (GROUP - 1)
        keys = sub < 2 * HEAD
        move = onehot(
            ((sub < HEAD) & (src == dst + HEAD))
            | ((sub >= HEAD) & (sub < 3 * HEAD) & (src == dst))
        )
        lane = iota((PATCH, lanes), 1) & (GROUP - 1)
        fixed = jnp.where((lane > 3 * HEAD) & (lane < 3 * HEAD + 4), 1.0, 0.0)
        if spanning:
            valid = count - first + tail_len
            row = iota((PATCH, lanes), 0)
            fixed = jnp.where((lane == 3 * HEAD) & (row >= valid), MASKED, fixed)
        left_ref[...] = (dot(x, move) + fixed).astype(BF)
        flip = dot_nt(onehot(src == dst), x)
        flip_ref[...] = flip.astype(BF)
        square = flip * flip
        bounded = True
        for h in range(2 * pairs):
            at = h * GROUP
            value_ref[h, :HEAD, :] = flip_ref[at + 2 * HEAD : at + 3 * HEAD, :]
            value_ref[h, HEAD:, :] = jnp.ones((HEAD, PATCH), BF)
            most_q = jnp.max(jnp.sum(square[at : at + HEAD], axis=0))
            most_k = jnp.max(jnp.sum(square[at + HEAD : at + 2 * HEAD], axis=0))
            bounded &= most_q * most_k * scale * scale <= SAFE * SAFE
        turn_ref[...] = jnp.zeros_like(turn_ref)
        top_ref[...] = jnp.zeros_like(top_ref)
        row = iota((HEAD, BLOCK), 0)

        def placed(pieces, h):
            zero = jnp.zeros((GROUP, BLOCK), BF)
            group = jnp.concatenate(pieces, axis=0)
            return jnp.concatenate([group, zero] if h % 2 == 0 else [zero, group], axis=0)

        nothing = jnp.zeros((HEAD, BLOCK), BF)

        def score_right(h, here, top):
            query = flip_ref[h * GROUP : h * GROUP + HEAD, here].astype(F32) * (scale * LOG2E)
            high, low = split(query)
            if top is None:
                extra = jnp.where(row == 0, 1.0, 0.0)
            else:
                top_high = top.astype(BF).astype(F32)
                top_mid = (top - top_high).astype(BF).astype(F32)
                top_low = top - top_high - top_mid
                extra = jnp.where(
                    row == 0,
                    1.0,
                    jnp.where(
                        row == 1,
                        -top_high,
                        jnp.where(row == 2, -top_mid, jnp.where(row == 3, -top_low, 0.0)),
                    ),
                )
            return placed([high, low, nothing, extra.astype(BF)], h)

        def block(pair, step, carry):
            left = left_ref.at[:, pair * PAIR : (pair + 1) * PAIR]
            here = [
                pl.ds(pl.multiple_of((step * 2 + t // 2) * BLOCK, BLOCK), BLOCK) for t in range(4)
            ]

            @pl.when(jnp.logical_not(bounded))
            def _():
                for t in range(4):
                    scores = dot(left[...], score_right(pair * 2 + t % 2, here[t], None))
                    top_ref[t : t + 1, :] = jnp.max(scores, axis=0, keepdims=True)

            inverses = [None] * 4
            rights = [None] * 4
            spans = [
                slice((t % 2 * 2 + t // 2) * BLOCK, (t % 2 * 2 + t // 2 + 1) * BLOCK)
                for t in range(4)
            ]
            ups = [None] * 4
            queries = [None] * 4

            def stage_exp(t):
                scores = dot(left[...], score_right(pair * 2 + t % 2, here[t], top_ref[t : t + 1, :]))
                exps = jnp.exp2(scores)
                exp_ref[t] = exps
                low_ref[:, spans[t]] = exps.astype(BF)

            def stage_sum(t):
                at = (pair * 2 + t % 2) * GROUP
                result = dot(value_ref[pair * 2 + t % 2], low_ref[:, spans[t]])
                inverse = 1.0 / result[HEAD : HEAD + 1]
                inverses[t] = inverse
                attended = result[:HEAD] * inverse
                turn_ref[at + 3 * HEAD : at + 4 * HEAD, here[t]] = attended
                up = flip_ref[at + 3 * HEAD : at + 4 * HEAD, here[t]].astype(F32)
                scaled = up * scale
                delta = jnp.sum(scaled * attended, axis=0, keepdims=True)
                delta_high = delta.astype(BF).astype(F32)
                extra = jnp.where(
                    row == 1, -delta_high, jnp.where(row == 2, delta_high - delta, 0.0)
                ).astype(BF)
                rights[t] = placed([nothing, nothing, scaled.astype(BF), extra], t % 2)
                query = flip_ref[at : at + HEAD, here[t]].astype(F32)
                ups[t] = (up * inverse).astype(BF)
                queries[t] = (query * inverse).astype(BF)

            def stage_grad(t):
                dprob = dot(left[...], rights[t])
                grad_ref[:, spans[t]] = (exp_ref[t] * dprob).astype(BF)

            def stage_query(t):
                at = (pair * 2 + t % 2) * GROUP
                result = dot(flip_ref[at + HEAD : at + 2 * HEAD, :], grad_ref[:, spans[t]])
                turn_ref[at : at + HEAD, here[t]] = result * inverses[t]

            for stage in (stage_exp, stage_sum, stage_grad, stage_query):
                for t in range(4):
                    stage(t)
            for h in range(2):
                at = (pair * 2 + h) * GROUP
                both = slice(2 * h * BLOCK, 2 * (h + 1) * BLOCK)
                turn_ref[at + 2 * HEAD : at + 3 * HEAD, :] += dot_nt(
                    jnp.concatenate([ups[h], ups[h + 2]], axis=1), low_ref[:, both]
                )
                turn_ref[at + HEAD : at + 2 * HEAD, :] += dot_nt(
                    jnp.concatenate([queries[h], queries[h + 2]], axis=1), grad_ref[:, both]
                )
            return carry

        for pair in range(pairs):
            lax.fori_loop(0, PATCH // (2 * BLOCK), functools.partial(block, pair), 0)
        done_ref[:MARGIN, :] = jnp.zeros((MARGIN, lanes), BF)
        done_ref[MARGIN + PATCH :, :] = jnp.zeros((MARGIN, lanes), BF)
        done_ref[MARGIN : MARGIN + PATCH, :] = turn_ref[...].T.astype(BF)
        row = iota((SHIFT, lanes), 0)
        to_own = shifter(-first)
        for start in range(0, slots, SHIFT):
            piece = to_own(done_ref, start)
            out_ref[start : start + SHIFT, :] = jnp.where(
                row < count - start, piece, 0.0
            ).astype(BF)
        if spanning:
            to_next = shifter(count - first)
            for start in range(0, PATCH, SHIFT):
                piece = to_next(done_ref, start)
                out_next_ref[start : start + SHIFT, :] = jnp.where(
                    row < tail_len - start, piece, 0.0
                ).astype(BF)

    if spanning:
        work()
    else:
        pl.when(n_patch == 2)(work)

        @pl.when(n_patch < 2)
        def _():
            out_ref[...] = jnp.zeros_like(out_ref)


def product_kernel(
    mine_ref, a_ref, b_ref, got_ref, one_ref, two_ref, wide_ref, wg_ref,
    keep_ref, send_ref, total_ref, turned_ref,
):
    step = pl.program_id(0)
    rows = a_ref.shape[0]
    core = lax.axis_index("mp") % 2
    cols = wide_ref.shape[0] // 8

    @pl.when(step == 0)
    def _():
        for side in range(2):
            for x in range(4):
                from_row = pl.multiple_of((2 * x + (core ^ side)) * cols, cols)
                to_row = (side * 4 + x) * cols
                turned_ref[to_row : to_row + cols, :] = wide_ref[pl.ds(from_row, cols), :]

    got = jnp.where(step < PATCH // rows, got_ref[...].astype(F32), 0.0)
    local = jnp.concatenate([a_ref[...], b_ref[...]], axis=1)
    wide_total = mine_ref[...].astype(F32) + local.astype(F32) + got
    total = wide_total.astype(BF)
    total_ref[...] = total
    du = dot_nt(turned_ref[...], total).astype(BF)
    half = 4 * cols
    keep_ref[:half, :] = du[:half]
    send_ref[:half, :] = du[half:]
    lane = iota((rows, LANES), 1) & (GROUP - 1)
    qkvu = jnp.concatenate([one_ref[...], two_ref[...]], axis=1).astype(F32)
    product = jnp.where(lane < 3 * HEAD, wide_total * qkvu, 0.0)
    high, low = split(product)
    ones = jnp.ones((16, LANES), BF)
    second = (dot_nt(ones, high) + dot_nt(ones, low))[:1]
    first_rows = dot_nt(wg_ref[...], total)
    first = first_rows[:1] + first_rows[1:2]
    stats = pack_stats(first, second, rows)
    keep_ref[half:, :] = stats
    send_ref[half:, :] = stats


def weight_kernel(total_ref, unit_ref, dy_ref, after_ref, grads_ref, gu_ref, gy_ref):
    step = pl.program_id(0)

    @pl.when(step == 0)
    def _():
        gu_ref[...] = jnp.zeros_like(gu_ref)
        gy_ref[...] = jnp.zeros_like(gy_ref)

    total = total_ref[...]
    gu_ref[...] += dot_tn(total, unit_ref[...])
    gy_ref[...] += dot_tn(total, dy_ref[...])

    @pl.when(step == pl.num_programs(0) - 1)
    def _():
        row = iota(gu_ref.shape, 0) & (GROUP - 1)
        grads_ref[...] = jnp.where(row < 3 * HEAD, gu_ref[...], gy_ref[...]).T.astype(BF)


def pack_stats(first, second, rows):
    row = iota((16, rows), 0)
    first_high = first.astype(BF).astype(F32)
    second_high = second.astype(BF).astype(F32)
    return jnp.where(
        row == 0,
        first_high,
        jnp.where(
            row == 1,
            first - first_high,
            jnp.where(row == 2, second_high, jnp.where(row == 3, second - second_high, 0.0)),
        ),
    ).astype(BF)


def pair_kernel(keep_ref, got_ref, after_ref, out0_ref, out1_ref, out2_ref, out3_ref):
    x = lax.axis_index("mp") // 2
    rows = keep_ref.shape[1]
    half = keep_ref.shape[0] - 16
    cols = half // 4
    stats = keep_ref[half:, :].astype(F32) + got_ref[half:, :].astype(F32)
    packed = pack_stats(stats[0:1] + stats[1:2], stats[2:3] + stats[3:4], rows).astype(F32)
    folded = jnp.concatenate(
        [packed[i : i + 1, j : j + 128] for i in range(4) for j in range(0, rows, 128)], axis=0
    ).astype(BF)
    for d, out_ref in enumerate((out0_ref, out1_ref, out2_ref, out3_ref)):
        at = pl.ds(pl.multiple_of(((x + d) % 4) * cols, cols), cols)
        both = keep_ref[at, :].astype(F32) + got_ref[at, :].astype(F32)
        out_ref[:, :rows] = both.astype(BF)
        out_ref[:, rows:] = folded


def finish_kernel(
    counts_ref, a_ref, b_ref, c_ref, d_ref, own_ref, stat_ref, gain_ref, grads_ref,
    points_ref, qkv_ref, proj_ref,
):
    rows = a_ref.shape[1] - 128
    cols = own_ref.shape[0] // 2
    width = gain_ref.shape[1]
    parts = [ref[...].astype(F32) for ref in (a_ref, b_ref, c_ref, d_ref)]
    total = (parts[0] + parts[1]) + (parts[2] + parts[3])
    folded = total[:, rows:]
    total = total[:, :rows]
    each = rows // 128
    firsts = (folded[:each] + folded[each : 2 * each]) * (1.0 / width)
    seconds = (folded[2 * each : 3 * each] + folded[3 * each : 4 * each]) * (1.0 / width)
    first = jnp.concatenate([firsts[i : i + 1] for i in range(each)], axis=1)
    second = jnp.concatenate([seconds[i : i + 1] for i in range(each)], axis=1)
    mine = iota((cols, width), 1) == iota((cols, width), 0) + lax.axis_index("mp") * cols
    gain = jnp.sum(jnp.where(mine, gain_ref[...], 0.0), axis=1, keepdims=True)
    mean = stat_ref[0:1, :]
    spread = stat_ref[4:5, :]
    normed = (own_ref[:cols, :].astype(F32) - mean) * spread
    dnorm = spread * (total * gain - first - normed * second)
    out = own_ref[cols:, :].astype(F32) + dnorm
    slot = iota((cols, rows), 1)
    points_ref[...] = jnp.where(slot < counts_ref[lax.axis_index("space"), 0, 0], out, 0.0).astype(BF)

    grads = jnp.sum(grads_ref[...].astype(F32), axis=0)
    qkv_ref[...] = jnp.concatenate(
        [grads[:, h * GROUP : h * GROUP + 3 * HEAD] for h in range(4)], axis=1
    )
    proj_ref[...] = jnp.concatenate(
        [grads[:, h * GROUP + 3 * HEAD : (h + 1) * GROUP] for h in range(4)], axis=1
    )


def whole(shape):
    return pl.BlockSpec(shape, lambda *_: (0,) * len(shape))


ANY = pl.BlockSpec(memory_space=pl.ANY)
shape = jax.ShapeDtypeStruct


SMEM = pl.BlockSpec(memory_space=pltpu.SMEM)


def call(kernel, args, grid, in_specs, out_specs, out_shape, scratch, limit, micros, aliases={}):
    return pl.pallas_call(
        kernel,
        grid=grid,
        in_specs=in_specs,
        out_specs=out_specs,
        scratch_shapes=scratch,
        out_shape=out_shape,
        input_output_aliases=aliases,
        cost_estimate=pl.CostEstimate(
            flops=int(micros * 1.1e9), bytes_accessed=0, transcendentals=0
        ),
        compiler_params=pltpu.CompilerParams(vmem_limit_bytes=int(limit * MIB)),
    )(*args)


def project(points, cotangent, gain, w_qkv, w_proj):
    slots, width = points.shape
    cols = width // 8
    chunks = slots // BLOCK
    outs = [
        shape((slots, PAIR), BF),
        shape((slots, PAIR), BF),
        shape((slots, width), BF),
        shape((PATCH, LANES), BF),
        shape((2 * cols, slots), BF),
        shape((8, slots), F32),
        shape((width, LANES), BF),
        shape((16, LANES), BF),
    ]
    return call(
        project_kernel,
        (points, cotangent, gain, w_qkv, w_proj),
        (1,),
        [ANY] * 5,
        [ANY] * 4 + [whole(o.shape) for o in outs[4:]],
        outs,
        [
            pltpu.VMEM((slots, width), BF),
            pltpu.VMEM((slots, width), BF),
            pltpu.VMEM(gain.shape, F32),
            pltpu.VMEM(w_qkv.shape, BF),
            pltpu.VMEM(w_proj.shape, BF),
            pltpu.VMEM((width, LANES + 2 * PAIR), BF),
            pltpu.VMEM((slots, LANES), BF),
            pltpu.VMEM((slots, width), BF),
            pltpu.SemaphoreType.DMA((2, chunks)),
            pltpu.SemaphoreType.DMA((3,)),
            pltpu.SemaphoreType.DMA((4, chunks)),
        ],
        FULL,
        6.5,
    )


def count_kernel(cells_ref, out_ref):
    total = jnp.sum(cells_ref[...].astype(F32), axis=1, keepdims=True).astype(jnp.int32)
    out_ref[...] = jnp.broadcast_to(total.reshape(1, 1, 1), out_ref.shape)


def count(cells, n_space):
    out = shape((n_space, 1, 128), jnp.int32)
    cells = cells.reshape(1, -1)
    return call(
        count_kernel, (cells,), (1,), [whole(cells.shape)], whole(out.shape), out, [], 1, 0.5
    )


def attend(spanning, counts, owns, following, after):
    slots = owns[0].shape[0]
    pairs = len(owns)
    lanes = pairs * PAIR
    outs = [shape((slots, lanes), BF)] + ([shape((PATCH, lanes), BF)] if spanning else [])
    args = (*owns, following) if spanning else tuple(owns)
    return call(
        functools.partial(attend_kernel, spanning, pairs),
        (counts, *args, after),
        (1,),
        [SMEM] + [whole(a.shape) for a in args] + [ANY],
        [whole(o.shape) for o in outs],
        outs,
        [
            pltpu.VMEM((PATCH, lanes), BF),
            pltpu.VMEM((PATCH, lanes), BF),
            pltpu.VMEM((lanes, PATCH), BF),
            pltpu.VMEM((2 * pairs, 2 * HEAD, PATCH), BF),
            pltpu.VMEM((8, BLOCK), F32),
            pltpu.VMEM((4, PATCH, BLOCK), F32),
            pltpu.VMEM((PATCH, 4 * BLOCK), BF),
            pltpu.VMEM((PATCH, 4 * BLOCK), BF),
            pltpu.VMEM((lanes, PATCH), F32),
            pltpu.VMEM((PATCH + 2 * MARGIN, lanes), BF),
            pltpu.VMEM((slots + 2 * MARGIN, lanes), BF),
            pltpu.VMEM((PATCH + 2 * MARGIN, lanes), BF),
        ],
        24,
        7.5 * pairs,
    )


def products(mine, locals_, got, heads, wide, wg):
    slots = mine.shape[0]
    width = wide.shape[0]
    rows = 256
    half = width // 2 + 16
    last = PATCH // rows - 1
    down = pl.BlockSpec((rows, PAIR), lambda i: (i, 0))
    full = pl.BlockSpec((rows, LANES), lambda i: (i, 0))
    first = pl.BlockSpec((rows, LANES), lambda i: (jnp.minimum(i, last), 0))
    across = pl.BlockSpec((half, rows), lambda i: (0, i))
    return call(
        product_kernel,
        (mine, *locals_, got, *heads, wide, wg),
        (slots // rows,),
        [full, down, down, first, down, down] + [whole(wide.shape), whole(wg.shape)],
        [across, across, pl.BlockSpec((rows, LANES), lambda i: (i, 0))],
        [shape((half, slots), BF), shape((half, slots), BF), shape((slots, LANES), BF)],
        [pltpu.VMEM((width, LANES), BF)],
        24,
        4.0,
    )


def weights(total, unit, dy, after):
    slots, width = unit.shape
    rows = 512
    down = lambda i: (i, 0)
    return call(
        weight_kernel,
        (total, unit, dy, after),
        (slots // rows,),
        [
            pl.BlockSpec((rows, LANES), down),
            pl.BlockSpec((rows, width), down),
            pl.BlockSpec((rows, width), down),
            ANY,
        ],
        [whole((width, LANES))],
        [shape((width, LANES), BF)],
        [pltpu.VMEM((LANES, width), F32), pltpu.VMEM((LANES, width), F32)],
        24,
        4.0,
    )[0]


def pair_sum(keep, got, after):
    total, slots = keep.shape
    out = shape(((total - 16) // 4, slots + 128), BF)
    return call(
        pair_kernel,
        (keep, got, after),
        (1,),
        [whole(keep.shape)] * 2 + [ANY],
        [whole(out.shape)] * 4,
        [out] * 4,
        [],
        24,
        2.3,
    )


def finish(counts, parts, own, stat, gain, grads):
    cols, slots = own.shape
    rows = grads.shape[1]
    outs = [
        shape((cols // 2, slots), BF),
        shape((rows, 3 * GROUP), F32),
        shape((rows, GROUP), F32),
    ]
    args = (*parts, own, stat, gain, grads)
    points, qkv, proj = call(
        finish_kernel,
        (counts, *args),
        (1,),
        [SMEM] + [whole(a.shape) for a in args],
        [whole(o.shape) for o in outs],
        outs,
        [],
        24,
        2.3,
    )
    return points.T, qkv, proj.T


def on_device(points, cotangent, cell_counts, norm_gain, w_qkv, w_proj):
    slots, width = points.shape
    n_space = lax.axis_size("space")
    n_mp = lax.axis_size("mp")
    counts = lax.all_to_all(count(cell_counts, n_space), "space", 0, 0)
    gain = norm_gain.reshape(1, width)
    one, two, unit, head, own, stat, wide, wg = project(
        points, cotangent, gain, w_qkv.T, w_proj
    )
    back = [(i + 1, i) for i in range(n_space - 1)]
    onward = [(i, i + 1) for i in range(n_space - 1)]
    following = lax.ppermute(head, "space", back)
    local_a = attend(False, counts, (one,), None, wg)[0]
    mine, spill = attend(True, counts, (one, two), following, local_a)
    got = lax.ppermute(spill, "space", onward)
    local_b = attend(False, counts, (two,), None, mine)[0]
    keep, send, total = products(mine, (local_a, local_b), got, (one, two), wide, wg)
    swap = [(i, i ^ 1) for i in range(n_mp)]
    other = lax.ppermute(send, "mp", swap)
    grads = weights(total, unit, cotangent, keep)
    gathered = lax.all_to_all(
        grads.reshape(n_space, width // n_space, LANES), "space", 0, 0
    )
    parts = pair_sum(keep, other, grads)
    received = [parts[0]]
    for d in range(1, n_mp // 2):
        route = [(i, (i + 2 * d) % n_mp) for i in range(n_mp)]
        received.append(lax.ppermute(parts[d], "mp", route))
    return finish(counts, received, own, stat, gain, gathered)


def solution(mesh):
    return jax.shard_map(
        on_device,
        mesh=mesh,
        in_specs=(
            P("space", None),
            P("space", None),
            P("space"),
            P(),
            P(None, "mp"),
            P("mp", None),
        ),
        out_specs=(P("space", "mp"), P("space", "mp"), P("mp", "space")),
        check_vma=False,
    )
```

```python
import functools

import jax
import jax.numpy as jnp
from jax import lax
from jax.experimental import pallas as pl
from jax.experimental.pallas import tpu as pltpu
from jax.sharding import PartitionSpec as P

H = 32
PATCH = 1024
EPS = 1e-05
MASKED = -1e30
HEAD = 16
GROUP = 64
LANES = 256
PAIR = 128
BLOCK = 256
SHIFT = 128
CHUNK = 512
MIB = 1024 * 1024
FULL = 60.5
LOG2E = 1.4426950408889634
SAFE = 40.0

BF = jnp.bfloat16
F32 = jnp.float32
NT = (((1,), (1,)), ((), ()))
TN = (((0,), (0,)), ((), ()))


def dot(a, b):
    return jnp.dot(a, b, preferred_element_type=F32)


def dot_nt(a, b):
    return lax.dot_general(a, b, NT, preferred_element_type=F32)


def dot_tn(a, b):
    return lax.dot_general(a, b, TN, preferred_element_type=F32)


def iota(shape, axis):
    return lax.broadcasted_iota(jnp.int32, shape, axis)


def onehot(mask):
    return jnp.where(mask, 1.0, 0.0).astype(BF)


def split(value):
    high = value.astype(BF)
    return high, (value - high.astype(F32)).astype(BF)


def project_kernel(lead, x_hbm, dy_hbm, gain_hbm, *rest):
    if lead:
        wqkv_hbm, wproj_hbm = rest[:2]
        one_hbm, two_hbm, unit_hbm, own_hbm, stat_hbm, head_hbm = rest[2:8]
        wide_ref, side_ref, wg_ref = rest[8:11]
        wqkv_ref, wproj_ref = rest[11:13]
        rest = rest[13:]
        pairs = ((wqkv_hbm, wqkv_ref), (wproj_hbm, wproj_ref))
    else:
        wide_hbm, side_hbm = rest[:2]
        one_hbm, two_hbm, unit_hbm, own_hbm, stat_hbm = rest[8:13]
        wide_ref, side_ref = rest[13:15]
        rest = rest[15:]
        pairs = ((wide_hbm, wide_ref), (side_hbm, side_ref))
    x_ref, dy_ref, gain_ref, qkvu_ref, unit_ref, own_ref, stat_ref, row_sems, sems, out_sems = rest
    half, width = x_ref.shape
    cols = own_ref.shape[0] // 2
    chunks = half // CHUNK
    base = 0 if lead else half

    def rows_copy(i, which):
        src, dst = ((x_hbm, x_ref), (dy_hbm, dy_ref))[which]
        return pltpu.make_async_copy(
            src.at[pl.ds(base + i * CHUNK, CHUNK)],
            dst.at[pl.ds(i * CHUNK, CHUNK)],
            row_sems.at[which, i],
        )

    def out_copy(i, which):
        at = pl.ds(i * CHUNK, CHUNK)
        to = pl.ds(base + i * CHUNK, CHUNK)
        if which == 0:
            src, dst = qkvu_ref.at[at, :PAIR], one_hbm.at[to]
        elif which == 1:
            src, dst = qkvu_ref.at[at, PAIR:], two_hbm.at[to]
        elif which == 2:
            src, dst = unit_ref.at[at], unit_hbm.at[to]
        elif which == 3:
            src, dst = own_ref.at[:, at], own_hbm.at[:, to]
        elif which == 4:
            src, dst = stat_ref.at[:, at], stat_hbm.at[:, to]
        else:
            src, dst = qkvu_ref.at[at], head_hbm.at[to]
        return pltpu.make_async_copy(src, dst, out_sems.at[which, i])

    pairs = (*pairs, (gain_hbm, gain_ref))
    small = [pltpu.make_async_copy(src, dst, sems.at[i]) for i, (src, dst) in enumerate(pairs)]
    for copy in small:
        copy.start()
    for i in range(chunks):
        rows_copy(i, 0).start()
        rows_copy(i, 1).start()
    if lead:
        row = iota((width, cols), 0)
        col = iota((width, cols), 1)
        pick = onehot(row == col + lax.axis_index("mp") * cols)
        none = jnp.zeros((width, cols), BF)
        side_ref[:, LANES:] = jnp.concatenate([none, pick, pick, none], axis=1)
    for copy in small:
        copy.wait()
    gain = gain_ref[...]
    if lead:
        col = iota((3 * GROUP, LANES), 0)
        lane = iota((3 * GROUP, LANES), 1)
        head = sum(jnp.where(col >= 3 * HEAD * h, HEAD, 0) for h in range(1, 4))
        wide = dot_tn(wqkv_ref[...], onehot(lane == col + head)).astype(BF)
        wide_ref[...] = wide
        part = iota((GROUP, LANES), 0)
        lane = iota((GROUP, LANES), 1)
        head = sum(jnp.where(part >= HEAD * h, GROUP - HEAD, 0) for h in range(1, 4))
        up = onehot(lane == part + head + 3 * HEAD)
        side_ref[:, :LANES] = dot_tn(wproj_ref[...], up).astype(BF)
        gain_high, gain_low = split(jnp.broadcast_to(gain, (16, width)))
        wg_high, wg_low = split(dot(gain_high, wide) + dot(gain_low, wide))
        row = iota((16, LANES), 0)
        wg_ref[...] = jnp.where(
            row == 0, wg_high.astype(F32), jnp.where(row == 1, wg_low.astype(F32), 0.0)
        ).astype(BF)

    copies = []
    for i in range(chunks):
        rows_copy(i, 0).wait()
        rows_copy(i, 1).wait()
        at = slice(i * CHUNK, (i + 1) * CHUNK)
        x_low = x_ref[at, :]
        x = x_low.astype(F32)
        mean = jnp.mean(x, axis=-1, keepdims=True)
        center = x - mean
        spread = lax.rsqrt(jnp.mean(center * center, axis=-1, keepdims=True) + EPS)
        unit = (center * spread * gain).astype(BF)
        unit_ref[at, :] = unit
        from_dy = dot(dy_ref[at, :], side_ref[:, : LANES + PAIR])
        qkvu_ref[at, :] = (dot(unit, wide_ref[...]) + from_dy[:, :LANES]).astype(BF)
        own = dot(x_low, side_ref[:, LANES + PAIR :]) + from_dy[:, LANES:]
        own_ref[:, at] = own.T.astype(BF)
        both = jnp.where(iota((CHUNK, 128), 1) < 4, mean, spread)
        stat_ref[:, at] = both.T[:8, :]
        for which in range(6 if lead else 5):
            copies.append(out_copy(i, which))
            copies[-1].start()
    for copy in copies:
        copy.wait()


def place_in_row(counts_ref):
    place = lax.axis_index("space")
    n_space = counts_ref.shape[0]
    start = jnp.int32(0)
    for i in range(n_space):
        start = start + jnp.where(i < place, counts_ref[i, 0, 0], 0)
    count = counts_ref[place, 0, 0]
    head_len = (PATCH - start % PATCH) % PATCH
    tail_len = jnp.where(place == n_space - 1, 0, (PATCH - (start + count) % PATCH) % PATCH)
    n_patch = (count - head_len + PATCH - 1) // PATCH
    return count, head_len, tail_len, n_patch


MARGIN = 2 * SHIFT


def shifter(first):
    part = first & (SHIFT - 1)
    pick = onehot(iota((SHIFT, 2 * SHIFT), 1) == iota((SHIFT, 2 * SHIFT), 0) + part)

    def block(src_ref, start):
        rows = src_ref.shape[0]
        base = jnp.clip(first - part + start + MARGIN, 0, rows - MARGIN)
        return dot(pick, src_ref[pl.ds(pl.multiple_of(base, SHIFT), 2 * SHIFT), :])

    return block


def padded(dst_ref, src_ref, limit, at):
    rows, width = src_ref.shape
    cols = slice(at, at + width)
    none = jnp.zeros((MARGIN, width), BF)
    dst_ref[:MARGIN, cols] = none
    dst_ref[MARGIN + rows :, cols] = none
    kept = iota(src_ref.shape, 0) < limit
    dst_ref[MARGIN : MARGIN + rows, cols] = jnp.where(
        kept, src_ref[...].astype(F32), 0.0
    ).astype(BF)


def attend_kernel(spanning, pairs, counts_ref, *rest):
    own_refs = rest[:pairs]
    if spanning:
        next_ref = rest[pairs]
        out_ref, out_next_ref = rest[pairs + 2 : pairs + 4]
        rest = rest[pairs + 4 :]
    else:
        out_ref = rest[pairs + 1]
        rest = rest[pairs + 2 :]
    (x_ref, left_ref, flip_ref, value_ref, top_ref, exp_ref, low_ref, grad_ref, turn_ref,
     done_ref, own_pad_ref, next_pad_ref) = rest
    slots = own_refs[0].shape[0]
    lanes = pairs * PAIR
    count, head_len, tail_len, n_patch = place_in_row(counts_ref)
    scale = HEAD ** (-0.5)

    def work():
        first = head_len + (PATCH * (n_patch - 1) if spanning else 0)

        for p in range(pairs):
            padded(own_pad_ref, own_refs[p], count, p * PAIR)
        from_own = shifter(first)
        if spanning:
            padded(next_pad_ref, next_ref, tail_len, 0)
            from_next = shifter(first - count)
        for start in range(0, PATCH, SHIFT):
            piece = from_own(own_pad_ref, start)
            if spanning:
                piece = piece + from_next(next_pad_ref, start)
            x_ref[start : start + SHIFT, :] = piece.astype(BF)
        x = x_ref[...]
        src = iota((lanes, lanes), 0)
        dst = iota((lanes, lanes), 1)
        sub = dst & (GROUP - 1)
        keys = sub < 2 * HEAD
        move = onehot(
            ((sub < HEAD) & (src == dst + HEAD))
            | ((sub >= HEAD) & (sub < 3 * HEAD) & (src == dst))
        )
        lane = iota((PATCH, lanes), 1) & (GROUP - 1)
        fixed = jnp.where((lane > 3 * HEAD) & (lane < 3 * HEAD + 4), 1.0, 0.0)
        if spanning:
            valid = count - first + tail_len
            row = iota((PATCH, lanes), 0)
            fixed = jnp.where((lane == 3 * HEAD) & (row >= valid), MASKED, fixed)
        left_ref[...] = (dot(x, move) + fixed).astype(BF)
        flip = dot_nt(onehot(src == dst), x)
        flip_ref[...] = flip.astype(BF)
        square = flip * flip
        bounded = True
        for h in range(2 * pairs):
            at = h * GROUP
            value_ref[h, :HEAD, :] = flip_ref[at + 2 * HEAD : at + 3 * HEAD, :]
            value_ref[h, HEAD:, :] = jnp.ones((HEAD, PATCH), BF)
            most_q = jnp.max(jnp.sum(square[at : at + HEAD], axis=0))
            most_k = jnp.max(jnp.sum(square[at + HEAD : at + 2 * HEAD], axis=0))
            bounded &= most_q * most_k * scale * scale <= SAFE * SAFE
        turn_ref[...] = jnp.zeros_like(turn_ref)
        top_ref[...] = jnp.zeros_like(top_ref)
        row = iota((HEAD, BLOCK), 0)

        def placed(pieces, h):
            zero = jnp.zeros((GROUP, BLOCK), BF)
            group = jnp.concatenate(pieces, axis=0)
            return jnp.concatenate([group, zero] if h % 2 == 0 else [zero, group], axis=0)

        nothing = jnp.zeros((HEAD, BLOCK), BF)

        def score_right(h, here, top):
            query = flip_ref[h * GROUP : h * GROUP + HEAD, here].astype(F32) * (scale * LOG2E)
            high, low = split(query)
            if top is None:
                extra = jnp.where(row == 0, 1.0, 0.0)
            else:
                top_high = top.astype(BF).astype(F32)
                top_mid = (top - top_high).astype(BF).astype(F32)
                top_low = top - top_high - top_mid
                extra = jnp.where(
                    row == 0,
                    1.0,
                    jnp.where(
                        row == 1,
                        -top_high,
                        jnp.where(row == 2, -top_mid, jnp.where(row == 3, -top_low, 0.0)),
                    ),
                )
            return placed([high, low, nothing, extra.astype(BF)], h)

        def block(pair, step, carry):
            left = left_ref.at[:, pair * PAIR : (pair + 1) * PAIR]
            here = [
                pl.ds(pl.multiple_of((step * 2 + t // 2) * BLOCK, BLOCK), BLOCK) for t in range(4)
            ]

            @pl.when(jnp.logical_not(bounded))
            def _():
                for t in range(4):
                    scores = dot(left[...], score_right(pair * 2 + t % 2, here[t], None))
                    top_ref[t : t + 1, :] = jnp.max(scores, axis=0, keepdims=True)

            inverses = [None] * 4
            rights = [None] * 4
            spans = [
                slice((t % 2 * 2 + t // 2) * BLOCK, (t % 2 * 2 + t // 2 + 1) * BLOCK)
                for t in range(4)
            ]
            ups = [None] * 4
            queries = [None] * 4

            def stage_exp(t):
                scores = dot(left[...], score_right(pair * 2 + t % 2, here[t], top_ref[t : t + 1, :]))
                exps = jnp.exp2(scores)
                exp_ref[t] = exps
                low_ref[:, spans[t]] = exps.astype(BF)

            def stage_sum(t):
                at = (pair * 2 + t % 2) * GROUP
                result = dot(value_ref[pair * 2 + t % 2], low_ref[:, spans[t]])
                inverse = 1.0 / result[HEAD : HEAD + 1]
                inverses[t] = inverse
                attended = result[:HEAD] * inverse
                turn_ref[at + 3 * HEAD : at + 4 * HEAD, here[t]] = attended
                up = flip_ref[at + 3 * HEAD : at + 4 * HEAD, here[t]].astype(F32)
                scaled = up * scale
                delta = jnp.sum(scaled * attended, axis=0, keepdims=True)
                delta_high = delta.astype(BF).astype(F32)
                extra = jnp.where(
                    row == 1, -delta_high, jnp.where(row == 2, delta_high - delta, 0.0)
                ).astype(BF)
                rights[t] = placed([nothing, nothing, scaled.astype(BF), extra], t % 2)
                query = flip_ref[at : at + HEAD, here[t]].astype(F32)
                ups[t] = (up * inverse).astype(BF)
                queries[t] = (query * inverse).astype(BF)

            def stage_grad(t):
                dprob = dot(left[...], rights[t])
                grad_ref[:, spans[t]] = (exp_ref[t] * dprob).astype(BF)

            def stage_query(t):
                at = (pair * 2 + t % 2) * GROUP
                result = dot(flip_ref[at + HEAD : at + 2 * HEAD, :], grad_ref[:, spans[t]])
                turn_ref[at : at + HEAD, here[t]] = result * inverses[t]

            for stage in (stage_exp, stage_sum, stage_grad, stage_query):
                for t in range(4):
                    stage(t)
            for h in range(2):
                at = (pair * 2 + h) * GROUP
                both = slice(2 * h * BLOCK, 2 * (h + 1) * BLOCK)
                turn_ref[at + 2 * HEAD : at + 3 * HEAD, :] += dot_nt(
                    jnp.concatenate([ups[h], ups[h + 2]], axis=1), low_ref[:, both]
                )
                turn_ref[at + HEAD : at + 2 * HEAD, :] += dot_nt(
                    jnp.concatenate([queries[h], queries[h + 2]], axis=1), grad_ref[:, both]
                )
            return carry

        for pair in range(pairs):
            lax.fori_loop(0, PATCH // (2 * BLOCK), functools.partial(block, pair), 0)
        done_ref[:MARGIN, :] = jnp.zeros((MARGIN, lanes), BF)
        done_ref[MARGIN + PATCH :, :] = jnp.zeros((MARGIN, lanes), BF)
        done_ref[MARGIN : MARGIN + PATCH, :] = turn_ref[...].T.astype(BF)
        row = iota((SHIFT, lanes), 0)
        to_own = shifter(-first)
        for start in range(0, slots, SHIFT):
            piece = to_own(done_ref, start)
            out_ref[start : start + SHIFT, :] = jnp.where(
                row < count - start, piece, 0.0
            ).astype(BF)
        if spanning:
            to_next = shifter(count - first)
            for start in range(0, PATCH, SHIFT):
                piece = to_next(done_ref, start)
                out_next_ref[start : start + SHIFT, :] = jnp.where(
                    row < tail_len - start, piece, 0.0
                ).astype(BF)

    if spanning:
        work()
    else:
        pl.when(n_patch == 2)(work)

        @pl.when(n_patch < 2)
        def _():
            out_ref[...] = jnp.zeros_like(out_ref)


def product_kernel(
    mine_ref, a_ref, b_ref, got_ref, one_ref, two_ref, wide_ref, wg_ref,
    keep_ref, send_ref, total_ref, turned_ref,
):
    step = pl.program_id(0)
    rows = a_ref.shape[0]
    core = lax.axis_index("mp") % 2
    cols = wide_ref.shape[0] // 8

    @pl.when(step == 0)
    def _():
        for side in range(2):
            for x in range(4):
                from_row = pl.multiple_of((2 * x + (core ^ side)) * cols, cols)
                to_row = (side * 4 + x) * cols
                turned_ref[to_row : to_row + cols, :] = wide_ref[pl.ds(from_row, cols), :]

    got = jnp.where(step < PATCH // rows, got_ref[...].astype(F32), 0.0)
    local = jnp.concatenate([a_ref[...], b_ref[...]], axis=1)
    wide_total = mine_ref[...].astype(F32) + local.astype(F32) + got
    total = wide_total.astype(BF)
    total_ref[...] = total
    du = dot_nt(turned_ref[...], total).astype(BF)
    half = 4 * cols
    keep_ref[:half, :] = du[:half]
    send_ref[:half, :] = du[half:]
    lane = iota((rows, LANES), 1) & (GROUP - 1)
    qkvu = jnp.concatenate([one_ref[...], two_ref[...]], axis=1).astype(F32)
    product = jnp.where(lane < 3 * HEAD, wide_total * qkvu, 0.0)
    high, low = split(product)
    ones = jnp.ones((16, LANES), BF)
    second = (dot_nt(ones, high) + dot_nt(ones, low))[:1]
    first_rows = dot_nt(wg_ref[...], total)
    first = first_rows[:1] + first_rows[1:2]
    stats = pack_stats(first, second, rows)
    keep_ref[half:, :] = stats
    send_ref[half:, :] = stats


def weight_kernel(total_ref, unit_ref, dy_ref, after_ref, grads_ref, gu_ref, gy_ref):
    step = pl.program_id(0)

    @pl.when(step == 0)
    def _():
        gu_ref[...] = jnp.zeros_like(gu_ref)
        gy_ref[...] = jnp.zeros_like(gy_ref)

    total = total_ref[...]
    gu_ref[...] += dot_tn(total, unit_ref[...])
    gy_ref[...] += dot_tn(total, dy_ref[...])

    @pl.when(step == pl.num_programs(0) - 1)
    def _():
        row = iota(gu_ref.shape, 0) & (GROUP - 1)
        grads_ref[...] = jnp.where(row < 3 * HEAD, gu_ref[...], gy_ref[...]).T.astype(BF)


def pack_stats(first, second, rows):
    row = iota((16, rows), 0)
    first_high = first.astype(BF).astype(F32)
    second_high = second.astype(BF).astype(F32)
    return jnp.where(
        row == 0,
        first_high,
        jnp.where(
            row == 1,
            first - first_high,
            jnp.where(row == 2, second_high, jnp.where(row == 3, second - second_high, 0.0)),
        ),
    ).astype(BF)


def pair_kernel(keep_ref, got_ref, after_ref, out0_ref, out1_ref, out2_ref, out3_ref):
    x = lax.axis_index("mp") // 2
    rows = keep_ref.shape[1]
    half = keep_ref.shape[0] - 16
    cols = half // 4
    stats = keep_ref[half:, :].astype(F32) + got_ref[half:, :].astype(F32)
    packed = pack_stats(stats[0:1] + stats[1:2], stats[2:3] + stats[3:4], rows).astype(F32)
    folded = jnp.concatenate(
        [packed[i : i + 1, j : j + 128] for i in range(4) for j in range(0, rows, 128)], axis=0
    ).astype(BF)
    for d, out_ref in enumerate((out0_ref, out1_ref, out2_ref, out3_ref)):
        at = pl.ds(pl.multiple_of(((x + d) % 4) * cols, cols), cols)
        both = keep_ref[at, :].astype(F32) + got_ref[at, :].astype(F32)
        out_ref[:, :rows] = both.astype(BF)
        out_ref[:, rows:] = folded


def finish_kernel(
    counts_ref, a_ref, b_ref, c_ref, d_ref, own_ref, stat_ref, gain_ref, grads_ref,
    points_ref, qkv_ref, proj_ref,
):
    rows = a_ref.shape[1] - 128
    cols = own_ref.shape[0] // 2
    width = gain_ref.shape[1]
    parts = [ref[...].astype(F32) for ref in (a_ref, b_ref, c_ref, d_ref)]
    total = (parts[0] + parts[1]) + (parts[2] + parts[3])
    folded = total[:, rows:]
    total = total[:, :rows]
    each = rows // 128
    firsts = (folded[:each] + folded[each : 2 * each]) * (1.0 / width)
    seconds = (folded[2 * each : 3 * each] + folded[3 * each : 4 * each]) * (1.0 / width)
    first = jnp.concatenate([firsts[i : i + 1] for i in range(each)], axis=1)
    second = jnp.concatenate([seconds[i : i + 1] for i in range(each)], axis=1)
    mine = iota((cols, width), 1) == iota((cols, width), 0) + lax.axis_index("mp") * cols
    gain = jnp.sum(jnp.where(mine, gain_ref[...], 0.0), axis=1, keepdims=True)
    mean = stat_ref[0:1, :]
    spread = stat_ref[4:5, :]
    normed = (own_ref[:cols, :].astype(F32) - mean) * spread
    dnorm = spread * (total * gain - first - normed * second)
    out = own_ref[cols:, :].astype(F32) + dnorm
    slot = iota((cols, rows), 1)
    points_ref[...] = jnp.where(slot < counts_ref[lax.axis_index("space"), 0, 0], out, 0.0).astype(BF)

    grads = jnp.sum(grads_ref[...].astype(F32), axis=0)
    qkv_ref[...] = jnp.concatenate(
        [grads[:, h * GROUP : h * GROUP + 3 * HEAD] for h in range(4)], axis=1
    )
    proj_ref[...] = jnp.concatenate(
        [grads[:, h * GROUP + 3 * HEAD : (h + 1) * GROUP] for h in range(4)], axis=1
    )


def whole(shape):
    return pl.BlockSpec(shape, lambda *_: (0,) * len(shape))


ANY = pl.BlockSpec(memory_space=pl.ANY)
shape = jax.ShapeDtypeStruct


SMEM = pl.BlockSpec(memory_space=pltpu.SMEM)


def call(kernel, args, grid, in_specs, out_specs, out_shape, scratch, limit, micros, aliases={}):
    return pl.pallas_call(
        kernel,
        grid=grid,
        in_specs=in_specs,
        out_specs=out_specs,
        scratch_shapes=scratch,
        out_shape=out_shape,
        input_output_aliases=aliases,
        cost_estimate=pl.CostEstimate(
            flops=int(micros * 1.1e9), bytes_accessed=0, transcendentals=0
        ),
        compiler_params=pltpu.CompilerParams(vmem_limit_bytes=int(limit * MIB)),
    )(*args)


def project(points, cotangent, gain, w_qkv, w_proj):
    slots, width = points.shape
    cols = width // 8
    half = slots // 2
    chunks = half // CHUNK
    outs = [
        shape((slots, PAIR), BF),
        shape((slots, PAIR), BF),
        shape((slots, width), BF),
        shape((2 * cols, slots), BF),
        shape((8, slots), F32),
    ]
    head = shape((half, LANES), BF)
    extra = [shape((width, LANES), BF), shape((width, LANES + 2 * PAIR), BF), shape((16, LANES), BF)]
    scratch = [
        pltpu.VMEM((half, width), BF),
        pltpu.VMEM((half, width), BF),
        pltpu.VMEM(gain.shape, F32),
        pltpu.VMEM((half, LANES), BF),
        pltpu.VMEM((half, width), BF),
        pltpu.VMEM((2 * cols, half), BF),
        pltpu.VMEM((8, half), F32),
        pltpu.SemaphoreType.DMA((2, chunks)),
        pltpu.SemaphoreType.DMA((3,)),
        pltpu.SemaphoreType.DMA((6, chunks)),
    ]
    results = call(
        functools.partial(project_kernel, True),
        (points, cotangent, gain, w_qkv, w_proj),
        (1,),
        [ANY] * 5,
        [ANY] * 6 + [whole(e.shape) for e in extra],
        outs + [head] + extra,
        [pltpu.VMEM(w_qkv.shape, BF), pltpu.VMEM(w_proj.shape, BF)] + scratch,
        FULL,
        4.5,
    )
    head, wide, side, wg = results[5:]
    again = call(
        functools.partial(project_kernel, False),
        (points, cotangent, gain, wide, side, *results[:5], head),
        (1,),
        [ANY] * 11,
        [ANY] * 5,
        outs,
        [pltpu.VMEM(e.shape, BF) for e in extra[:2]] + scratch,
        FULL,
        3.0,
        {5 + i: i for i in range(5)},
    )
    return (*again, head, wide, wg)


def count_kernel(cells_ref, out_ref):
    total = jnp.sum(cells_ref[...].astype(F32), axis=1, keepdims=True).astype(jnp.int32)
    out_ref[...] = jnp.broadcast_to(total.reshape(1, 1, 1), out_ref.shape)


def count(cells, n_space):
    out = shape((n_space, 1, 128), jnp.int32)
    cells = cells.reshape(1, -1)
    return call(
        count_kernel, (cells,), (1,), [whole(cells.shape)], whole(out.shape), out, [], 1, 0.5
    )


def attend(spanning, counts, owns, following, after):
    slots = owns[0].shape[0]
    pairs = len(owns)
    lanes = pairs * PAIR
    outs = [shape((slots, lanes), BF)] + ([shape((PATCH, lanes), BF)] if spanning else [])
    args = (*owns, following) if spanning else tuple(owns)
    return call(
        functools.partial(attend_kernel, spanning, pairs),
        (counts, *args, after),
        (1,),
        [SMEM] + [whole(a.shape) for a in args] + [ANY],
        [whole(o.shape) for o in outs],
        outs,
        [
            pltpu.VMEM((PATCH, lanes), BF),
            pltpu.VMEM((PATCH, lanes), BF),
            pltpu.VMEM((lanes, PATCH), BF),
            pltpu.VMEM((2 * pairs, 2 * HEAD, PATCH), BF),
            pltpu.VMEM((8, BLOCK), F32),
            pltpu.VMEM((4, PATCH, BLOCK), F32),
            pltpu.VMEM((PATCH, 4 * BLOCK), BF),
            pltpu.VMEM((PATCH, 4 * BLOCK), BF),
            pltpu.VMEM((lanes, PATCH), F32),
            pltpu.VMEM((PATCH + 2 * MARGIN, lanes), BF),
            pltpu.VMEM((slots + 2 * MARGIN, lanes), BF),
            pltpu.VMEM((PATCH + 2 * MARGIN, lanes), BF),
        ],
        24,
        7.5 * pairs,
    )


def products(mine, locals_, got, heads, wide, wg):
    slots = mine.shape[0]
    width = wide.shape[0]
    rows = 256
    half = width // 2 + 16
    last = PATCH // rows - 1
    down = pl.BlockSpec((rows, PAIR), lambda i: (i, 0))
    full = pl.BlockSpec((rows, LANES), lambda i: (i, 0))
    first = pl.BlockSpec((rows, LANES), lambda i: (jnp.minimum(i, last), 0))
    across = pl.BlockSpec((half, rows), lambda i: (0, i))
    return call(
        product_kernel,
        (mine, *locals_, got, *heads, wide, wg),
        (slots // rows,),
        [full, down, down, first, down, down] + [whole(wide.shape), whole(wg.shape)],
        [across, across, pl.BlockSpec((rows, LANES), lambda i: (i, 0))],
        [shape((half, slots), BF), shape((half, slots), BF), shape((slots, LANES), BF)],
        [pltpu.VMEM((width, LANES), BF)],
        24,
        4.0,
    )


def weights(total, unit, dy, after):
    slots, width = unit.shape
    rows = 512
    down = lambda i: (i, 0)
    return call(
        weight_kernel,
        (total, unit, dy, after),
        (slots // rows,),
        [
            pl.BlockSpec((rows, LANES), down),
            pl.BlockSpec((rows, width), down),
            pl.BlockSpec((rows, width), down),
            ANY,
        ],
        [whole((width, LANES))],
        [shape((width, LANES), BF)],
        [pltpu.VMEM((LANES, width), F32), pltpu.VMEM((LANES, width), F32)],
        24,
        4.0,
    )[0]


def pair_sum(keep, got, after):
    total, slots = keep.shape
    out = shape(((total - 16) // 4, slots + 128), BF)
    return call(
        pair_kernel,
        (keep, got, after),
        (1,),
        [whole(keep.shape)] * 2 + [ANY],
        [whole(out.shape)] * 4,
        [out] * 4,
        [],
        24,
        2.3,
    )


def finish(counts, parts, own, stat, gain, grads):
    cols, slots = own.shape
    rows = grads.shape[1]
    outs = [
        shape((cols // 2, slots), BF),
        shape((rows, 3 * GROUP), F32),
        shape((rows, GROUP), F32),
    ]
    args = (*parts, own, stat, gain, grads)
    points, qkv, proj = call(
        finish_kernel,
        (counts, *args),
        (1,),
        [SMEM] + [whole(a.shape) for a in args],
        [whole(o.shape) for o in outs],
        outs,
        [],
        24,
        2.3,
    )
    return points.T, qkv, proj.T


def on_device(points, cotangent, cell_counts, norm_gain, w_qkv, w_proj):
    slots, width = points.shape
    n_space = lax.axis_size("space")
    n_mp = lax.axis_size("mp")
    counts = lax.all_to_all(count(cell_counts, n_space), "space", 0, 0)
    gain = norm_gain.reshape(1, width)
    one, two, unit, own, stat, head, wide, wg = project(
        points, cotangent, gain, w_qkv.T, w_proj
    )
    back = [(i + 1, i) for i in range(n_space - 1)]
    onward = [(i, i + 1) for i in range(n_space - 1)]
    following = lax.ppermute(head, "space", back)
    local_a = attend(False, counts, (one,), None, one)[0]
    mine, spill = attend(True, counts, (one, two), following, local_a)
    got = lax.ppermute(spill, "space", onward)
    local_b = attend(False, counts, (two,), None, mine)[0]
    keep, send, total = products(mine, (local_a, local_b), got, (one, two), wide, wg)
    swap = [(i, i ^ 1) for i in range(n_mp)]
    other = lax.ppermute(send, "mp", swap)
    grads = weights(total, unit, cotangent, keep)
    gathered = lax.all_to_all(
        grads.reshape(n_space, width // n_space, LANES), "space", 0, 0
    )
    parts = pair_sum(keep, other, grads)
    received = [parts[0]]
    for d in range(1, n_mp // 2):
        route = [(i, (i + 2 * d) % n_mp) for i in range(n_mp)]
        received.append(lax.ppermute(parts[d], "mp", route))
    return finish(counts, received, own, stat, gain, gathered)


def solution(mesh):
    return jax.shard_map(
        on_device,
        mesh=mesh,
        in_specs=(
            P("space", None),
            P("space", None),
            P("space"),
            P(),
            P(None, "mp"),
            P("mp", None),
        ),
        out_specs=(P("space", "mp"), P("space", "mp"), P("mp", "space")),
        check_vma=False,
    )
```

```python
import functools

import jax
import jax.numpy as jnp
from jax import lax
from jax.experimental import pallas as pl
from jax.experimental.pallas import tpu as pltpu
from jax.sharding import PartitionSpec as P

H = 32
PATCH = 1024
EPS = 1e-05
MASKED = -1e30
HEAD = 16
GROUP = 64
LANES = 256
PAIR = 128
BLOCK = 256
SHIFT = 128
CHUNK = 512
MIB = 1024 * 1024
FULL = 60.5
LOG2E = 1.4426950408889634
SAFE = 40.0

BF = jnp.bfloat16
F32 = jnp.float32
NT = (((1,), (1,)), ((), ()))
TN = (((0,), (0,)), ((), ()))


def dot(a, b):
    return jnp.dot(a, b, preferred_element_type=F32)


def dot_nt(a, b):
    return lax.dot_general(a, b, NT, preferred_element_type=F32)


def dot_tn(a, b):
    return lax.dot_general(a, b, TN, preferred_element_type=F32)


def iota(shape, axis):
    return lax.broadcasted_iota(jnp.int32, shape, axis)


def onehot(mask):
    return jnp.where(mask, 1.0, 0.0).astype(BF)


def split(value):
    high = value.astype(BF)
    return high, (value - high.astype(F32)).astype(BF)


def project_rows(lead, x_hbm, dy_hbm, gain_hbm, *rest):
    if lead:
        wqkv_hbm, wproj_hbm = rest[:2]
        one_hbm, two_hbm, unit_hbm, own_hbm, stat_hbm, head_hbm = rest[2:8]
        wide_ref, side_ref, wg_ref = rest[8:11]
        wqkv_ref, wproj_ref = rest[11:13]
        rest = rest[13:]
        pairs = ((wqkv_hbm, wqkv_ref), (wproj_hbm, wproj_ref))
    else:
        wide_hbm, side_hbm = rest[:2]
        one_hbm, two_hbm, unit_hbm, own_hbm, stat_hbm = rest[7:12]
        wide_ref, side_ref = rest[12:14]
        rest = rest[14:]
        pairs = ((wide_hbm, wide_ref), (side_hbm, side_ref))
    x_ref, dy_ref, gain_ref, qkvu_ref, unit_ref, own_ref, stat_ref, row_sems, sems, out_sems = rest
    half, width = x_ref.shape
    cols = own_ref.shape[0] // 2
    chunks = half // CHUNK
    base = 0 if lead else half

    def rows_copy(i, which):
        src, dst = ((x_hbm, x_ref), (dy_hbm, dy_ref))[which]
        return pltpu.make_async_copy(
            src.at[pl.ds(base + i * CHUNK, CHUNK)],
            dst.at[pl.ds(i * CHUNK, CHUNK)],
            row_sems.at[which, i],
        )

    def out_copy(i, which):
        at = pl.ds(i * CHUNK, CHUNK)
        to = pl.ds(base + i * CHUNK, CHUNK)
        if which == 0:
            src, dst = qkvu_ref.at[at, :PAIR], one_hbm.at[to]
        elif which == 1:
            src, dst = qkvu_ref.at[at, PAIR:], two_hbm.at[to]
        elif which == 2:
            src, dst = unit_ref.at[at], unit_hbm.at[to]
        elif which == 3:
            src, dst = own_ref.at[:, at], own_hbm.at[:, to]
        elif which == 4:
            src, dst = stat_ref.at[:, at], stat_hbm.at[:, to]
        else:
            src, dst = qkvu_ref.at[at], head_hbm.at[to]
        return pltpu.make_async_copy(src, dst, out_sems.at[which, i])

    pairs = (*pairs, (gain_hbm, gain_ref))
    small = [pltpu.make_async_copy(src, dst, sems.at[i]) for i, (src, dst) in enumerate(pairs)]
    for copy in small:
        copy.start()
    for i in range(chunks):
        rows_copy(i, 0).start()
        rows_copy(i, 1).start()
    if lead:
        row = iota((width, cols), 0)
        col = iota((width, cols), 1)
        pick = onehot(row == col + lax.axis_index("mp") * cols)
        none = jnp.zeros((width, cols), BF)
        side_ref[:, LANES:] = jnp.concatenate([none, pick, pick, none], axis=1)
    for copy in small:
        copy.wait()
    gain = gain_ref[...]
    if lead:
        col = iota((3 * GROUP, LANES), 0)
        lane = iota((3 * GROUP, LANES), 1)
        head = sum(jnp.where(col >= 3 * HEAD * h, HEAD, 0) for h in range(1, 4))
        wide = dot_tn(wqkv_ref[...], onehot(lane == col + head)).astype(BF)
        wide_ref[...] = wide
        part = iota((GROUP, LANES), 0)
        lane = iota((GROUP, LANES), 1)
        head = sum(jnp.where(part >= HEAD * h, GROUP - HEAD, 0) for h in range(1, 4))
        up = onehot(lane == part + head + 3 * HEAD)
        side_ref[:, :LANES] = dot_tn(wproj_ref[...], up).astype(BF)
        gain_high, gain_low = split(jnp.broadcast_to(gain, (16, width)))
        wg_high, wg_low = split(dot(gain_high, wide) + dot(gain_low, wide))
        row = iota((16, LANES), 0)
        wg_ref[...] = jnp.where(
            row == 0, wg_high.astype(F32), jnp.where(row == 1, wg_low.astype(F32), 0.0)
        ).astype(BF)

    copies = []
    for i in range(chunks):
        rows_copy(i, 0).wait()
        rows_copy(i, 1).wait()
        at = slice(i * CHUNK, (i + 1) * CHUNK)
        x_low = x_ref[at, :]
        x = x_low.astype(F32)
        mean = jnp.mean(x, axis=-1, keepdims=True)
        center = x - mean
        spread = lax.rsqrt(jnp.mean(center * center, axis=-1, keepdims=True) + EPS)
        unit = (center * spread * gain).astype(BF)
        unit_ref[at, :] = unit
        from_dy = dot(dy_ref[at, :], side_ref[:, : LANES + PAIR])
        qkvu_ref[at, :] = (dot(unit, wide_ref[...]) + from_dy[:, :LANES]).astype(BF)
        own = dot(x_low, side_ref[:, LANES + PAIR :]) + from_dy[:, LANES:]
        own_ref[:, at] = own.T.astype(BF)
        both = jnp.where(iota((CHUNK, 128), 1) < 4, mean, spread)
        stat_ref[:, at] = both.T[:8, :]
        for which in range(6 if lead else 5):
            copies.append(out_copy(i, which))
            copies[-1].start()
    return copies


def project_kernel(*refs):
    for copy in project_rows(True, *refs):
        copy.wait()


def front_kernel(
    counts_ref, x_hbm, dy_hbm, gain_hbm, wide_hbm, side_hbm, head_hbm, *rest
):
    carried, outs, local_ref = rest[:5], rest[5:10], rest[10]
    (wide_ref, side_ref, *project_scratch) = rest[11:23]
    first_ref, first_sem = rest[23:25]
    half = head_hbm.shape[0]
    lower = pltpu.make_async_copy(head_hbm.at[:, :PAIR], first_ref.at[pl.ds(0, half)], first_sem.at[0])
    lower.start()
    copies = project_rows(
        False, x_hbm, dy_hbm, gain_hbm, wide_hbm, side_hbm, *carried, *outs,
        wide_ref, side_ref, *project_scratch,
    )
    qkvu_ref = project_scratch[3]
    first_ref[half:, :] = qkvu_ref[:, :PAIR]
    lower.wait()
    attend_kernel(False, 1, counts_ref, first_ref, None, local_ref, *rest[25:])
    for copy in copies:
        copy.wait()


def place_in_row(counts_ref):
    place = lax.axis_index("space")
    n_space = counts_ref.shape[0]
    start = jnp.int32(0)
    for i in range(n_space):
        start = start + jnp.where(i < place, counts_ref[i, 0, 0], 0)
    count = counts_ref[place, 0, 0]
    head_len = (PATCH - start % PATCH) % PATCH
    tail_len = jnp.where(place == n_space - 1, 0, (PATCH - (start + count) % PATCH) % PATCH)
    n_patch = (count - head_len + PATCH - 1) // PATCH
    return count, head_len, tail_len, n_patch


MARGIN = 2 * SHIFT


def shifter(first):
    part = first & (SHIFT - 1)
    pick = onehot(iota((SHIFT, 2 * SHIFT), 1) == iota((SHIFT, 2 * SHIFT), 0) + part)

    def block(src_ref, start):
        rows = src_ref.shape[0]
        base = jnp.clip(first - part + start + MARGIN, 0, rows - MARGIN)
        return dot(pick, src_ref[pl.ds(pl.multiple_of(base, SHIFT), 2 * SHIFT), :])

    return block


def padded(dst_ref, src_ref, limit, at):
    rows, width = src_ref.shape
    cols = slice(at, at + width)
    none = jnp.zeros((MARGIN, width), BF)
    dst_ref[:MARGIN, cols] = none
    dst_ref[MARGIN + rows :, cols] = none
    kept = iota(src_ref.shape, 0) < limit
    dst_ref[MARGIN : MARGIN + rows, cols] = jnp.where(
        kept, src_ref[...].astype(F32), 0.0
    ).astype(BF)


def attend_kernel(spanning, pairs, counts_ref, *rest):
    own_refs = rest[:pairs]
    if spanning:
        next_ref = rest[pairs]
        out_ref, out_next_ref = rest[pairs + 2 : pairs + 4]
        rest = rest[pairs + 4 :]
    else:
        out_ref = rest[pairs + 1]
        rest = rest[pairs + 2 :]
    (x_ref, left_ref, flip_ref, value_ref, top_ref, exp_ref, low_ref, grad_ref, turn_ref,
     done_ref, own_pad_ref, next_pad_ref) = rest
    slots = own_refs[0].shape[0]
    lanes = pairs * PAIR
    count, head_len, tail_len, n_patch = place_in_row(counts_ref)
    scale = HEAD ** (-0.5)

    def work():
        first = head_len + (PATCH * (n_patch - 1) if spanning else 0)

        for p in range(pairs):
            padded(own_pad_ref, own_refs[p], count, p * PAIR)
        from_own = shifter(first)
        if spanning:
            padded(next_pad_ref, next_ref, tail_len, 0)
            from_next = shifter(first - count)
        for start in range(0, PATCH, SHIFT):
            piece = from_own(own_pad_ref, start)
            if spanning:
                piece = piece + from_next(next_pad_ref, start)
            x_ref[start : start + SHIFT, :] = piece.astype(BF)
        x = x_ref[...]
        src = iota((lanes, lanes), 0)
        dst = iota((lanes, lanes), 1)
        sub = dst & (GROUP - 1)
        keys = sub < 2 * HEAD
        move = onehot(
            ((sub < HEAD) & (src == dst + HEAD))
            | ((sub >= HEAD) & (sub < 3 * HEAD) & (src == dst))
        )
        lane = iota((PATCH, lanes), 1) & (GROUP - 1)
        fixed = jnp.where((lane > 3 * HEAD) & (lane < 3 * HEAD + 4), 1.0, 0.0)
        if spanning:
            valid = count - first + tail_len
            row = iota((PATCH, lanes), 0)
            fixed = jnp.where((lane == 3 * HEAD) & (row >= valid), MASKED, fixed)
        left_ref[...] = (dot(x, move) + fixed).astype(BF)
        flip = dot_nt(onehot(src == dst), x)
        flip_ref[...] = flip.astype(BF)
        square = flip * flip
        most = jnp.zeros((1, 1), F32)
        for h in range(2 * pairs):
            at = h * GROUP
            value_ref[h, :HEAD, :] = flip_ref[at + 2 * HEAD : at + 3 * HEAD, :]
            value_ref[h, HEAD:, :] = jnp.ones((HEAD, PATCH), BF)
            most_q = jnp.sum(square[at : at + HEAD], axis=0, keepdims=True)
            most_k = jnp.sum(square[at + HEAD : at + 2 * HEAD], axis=0, keepdims=True)
            both = jnp.max(most_q, axis=1, keepdims=True) * jnp.max(most_k, axis=1, keepdims=True)
            most = jnp.maximum(most, both)
        bounded = jnp.max(most) * scale * scale <= SAFE * SAFE
        turn_ref[...] = jnp.zeros_like(turn_ref)
        top_ref[...] = jnp.zeros_like(top_ref)
        row = iota((HEAD, BLOCK), 0)

        def placed(pieces, h):
            zero = jnp.zeros((GROUP, BLOCK), BF)
            group = jnp.concatenate(pieces, axis=0)
            return jnp.concatenate([group, zero] if h % 2 == 0 else [zero, group], axis=0)

        nothing = jnp.zeros((HEAD, BLOCK), BF)

        def score_right(h, here, top):
            query = flip_ref[h * GROUP : h * GROUP + HEAD, here].astype(F32) * (scale * LOG2E)
            high, low = split(query)
            if top is None:
                extra = jnp.where(row == 0, 1.0, 0.0)
            else:
                top_high = top.astype(BF).astype(F32)
                top_mid = (top - top_high).astype(BF).astype(F32)
                top_low = top - top_high - top_mid
                extra = jnp.where(
                    row == 0,
                    1.0,
                    jnp.where(
                        row == 1,
                        -top_high,
                        jnp.where(row == 2, -top_mid, jnp.where(row == 3, -top_low, 0.0)),
                    ),
                )
            return placed([high, low, nothing, extra.astype(BF)], h)

        def block(pair, step, carry):
            left = left_ref.at[:, pair * PAIR : (pair + 1) * PAIR]
            here = [
                pl.ds(pl.multiple_of((step * 2 + t // 2) * BLOCK, BLOCK), BLOCK) for t in range(4)
            ]

            @pl.when(jnp.logical_not(bounded))
            def _():
                for t in range(4):
                    scores = dot(left[...], score_right(pair * 2 + t % 2, here[t], None))
                    top_ref[t : t + 1, :] = jnp.max(scores, axis=0, keepdims=True)

            inverses = [None] * 4
            rights = [None] * 4
            spans = [
                slice((t % 2 * 2 + t // 2) * BLOCK, (t % 2 * 2 + t // 2 + 1) * BLOCK)
                for t in range(4)
            ]
            ups = [None] * 4
            queries = [None] * 4

            def stage_exp(t):
                scores = dot(left[...], score_right(pair * 2 + t % 2, here[t], top_ref[t : t + 1, :]))
                exps = jnp.exp2(scores)
                exp_ref[t] = exps
                low_ref[:, spans[t]] = exps.astype(BF)

            def stage_sum(t):
                at = (pair * 2 + t % 2) * GROUP
                result = dot(value_ref[pair * 2 + t % 2], low_ref[:, spans[t]])
                inverse = 1.0 / result[HEAD : HEAD + 1]
                inverses[t] = inverse
                attended = result[:HEAD] * inverse
                turn_ref[at + 3 * HEAD : at + 4 * HEAD, here[t]] = attended
                up = flip_ref[at + 3 * HEAD : at + 4 * HEAD, here[t]].astype(F32)
                scaled = up * scale
                delta = jnp.sum(scaled * attended, axis=0, keepdims=True)
                delta_high = delta.astype(BF).astype(F32)
                extra = jnp.where(
                    row == 1, -delta_high, jnp.where(row == 2, delta_high - delta, 0.0)
                ).astype(BF)
                rights[t] = placed([nothing, nothing, scaled.astype(BF), extra], t % 2)
                query = flip_ref[at : at + HEAD, here[t]].astype(F32)
                ups[t] = (up * inverse).astype(BF)
                queries[t] = (query * inverse).astype(BF)

            def stage_grad(t):
                dprob = dot(left[...], rights[t])
                grad_ref[:, spans[t]] = (exp_ref[t] * dprob).astype(BF)

            def stage_query(t):
                at = (pair * 2 + t % 2) * GROUP
                result = dot(flip_ref[at + HEAD : at + 2 * HEAD, :], grad_ref[:, spans[t]])
                turn_ref[at : at + HEAD, here[t]] = result * inverses[t]

            for stage in (stage_exp, stage_sum, stage_grad, stage_query):
                for t in range(4):
                    stage(t)
            for h in range(2):
                at = (pair * 2 + h) * GROUP
                both = slice(2 * h * BLOCK, 2 * (h + 1) * BLOCK)
                turn_ref[at + 2 * HEAD : at + 3 * HEAD, :] += dot_nt(
                    jnp.concatenate([ups[h], ups[h + 2]], axis=1), low_ref[:, both]
                )
                turn_ref[at + HEAD : at + 2 * HEAD, :] += dot_nt(
                    jnp.concatenate([queries[h], queries[h + 2]], axis=1), grad_ref[:, both]
                )
            return carry

        for pair in range(pairs):
            lax.fori_loop(0, PATCH // (2 * BLOCK), functools.partial(block, pair), 0)
        done_ref[:MARGIN, :] = jnp.zeros((MARGIN, lanes), BF)
        done_ref[MARGIN + PATCH :, :] = jnp.zeros((MARGIN, lanes), BF)
        done_ref[MARGIN : MARGIN + PATCH, :] = turn_ref[...].T.astype(BF)
        row = iota((SHIFT, lanes), 0)
        to_own = shifter(-first)
        for start in range(0, slots, SHIFT):
            piece = to_own(done_ref, start)
            out_ref[start : start + SHIFT, :] = jnp.where(
                row < count - start, piece, 0.0
            ).astype(BF)
        if spanning:
            to_next = shifter(count - first)
            for start in range(0, PATCH, SHIFT):
                piece = to_next(done_ref, start)
                out_next_ref[start : start + SHIFT, :] = jnp.where(
                    row < tail_len - start, piece, 0.0
                ).astype(BF)

    if spanning:
        work()
    else:
        pl.when(n_patch == 2)(work)

        @pl.when(n_patch < 2)
        def _():
            out_ref[...] = jnp.zeros_like(out_ref)


def product_kernel(lower, mine_ref, a_ref, b_ref, one_ref, two_ref, wide_ref, wg_ref, *rest):
    if lower:
        got_ref = rest[0]
        rest = rest[4:]
    keep_ref, send_ref, total_ref, turned_ref = rest
    step = pl.program_id(0)
    rows = a_ref.shape[0]
    core = lax.axis_index("mp") % 2
    cols = wide_ref.shape[0] // 8

    @pl.when(step == 0)
    def _():
        for side in range(2):
            for x in range(4):
                from_row = pl.multiple_of((2 * x + (core ^ side)) * cols, cols)
                to_row = (side * 4 + x) * cols
                turned_ref[to_row : to_row + cols, :] = wide_ref[pl.ds(from_row, cols), :]

    local = jnp.concatenate([a_ref[...], b_ref[...]], axis=1)
    wide_total = mine_ref[...].astype(F32) + local.astype(F32)
    if lower:
        wide_total = wide_total + got_ref[...].astype(F32)
    total = wide_total.astype(BF)
    total_ref[...] = total
    du = dot_nt(turned_ref[...], total).astype(BF)
    half = 4 * cols
    keep_ref[:half, :] = du[:half]
    send_ref[:half, :] = du[half:]
    lane = iota((rows, LANES), 1) & (GROUP - 1)
    qkvu = jnp.concatenate([one_ref[...], two_ref[...]], axis=1).astype(F32)
    product = jnp.where(lane < 3 * HEAD, wide_total * qkvu, 0.0)
    high, low = split(product)
    ones = jnp.ones((16, LANES), BF)
    second = (dot_nt(ones, high) + dot_nt(ones, low))[:1]
    first_rows = dot_nt(wg_ref[...], total)
    first = first_rows[:1] + first_rows[1:2]
    stats = pack_stats(first, second, rows)
    keep_ref[half:, :] = stats
    send_ref[half:, :] = stats


def weight_kernel(total_ref, unit_ref, dy_ref, after_ref, grads_ref, gu_ref, gy_ref):
    step = pl.program_id(0)

    @pl.when(step == 0)
    def _():
        gu_ref[...] = jnp.zeros_like(gu_ref)
        gy_ref[...] = jnp.zeros_like(gy_ref)

    total = total_ref[...]
    gu_ref[...] += dot_tn(total, unit_ref[...])
    gy_ref[...] += dot_tn(total, dy_ref[...])

    @pl.when(step == pl.num_programs(0) - 1)
    def _():
        row = iota(gu_ref.shape, 0) & (GROUP - 1)
        grads_ref[...] = jnp.where(row < 3 * HEAD, gu_ref[...], gy_ref[...]).T.astype(BF)


def pack_stats(first, second, rows):
    row = iota((16, rows), 0)
    first_high = first.astype(BF).astype(F32)
    second_high = second.astype(BF).astype(F32)
    return jnp.where(
        row == 0,
        first_high,
        jnp.where(
            row == 1,
            first - first_high,
            jnp.where(row == 2, second_high, jnp.where(row == 3, second - second_high, 0.0)),
        ),
    ).astype(BF)


def pair_kernel(keep_ref, got_ref, after_ref, out0_ref, out1_ref, out2_ref, out3_ref):
    x = lax.axis_index("mp") // 2
    rows = keep_ref.shape[1]
    half = keep_ref.shape[0] - 16
    cols = half // 4
    stats = keep_ref[half:, :].astype(F32) + got_ref[half:, :].astype(F32)
    packed = pack_stats(stats[0:1] + stats[1:2], stats[2:3] + stats[3:4], rows).astype(F32)
    folded = jnp.concatenate(
        [packed[i : i + 1, j : j + 128] for i in range(4) for j in range(0, rows, 128)], axis=0
    ).astype(BF)
    for d, out_ref in enumerate((out0_ref, out1_ref, out2_ref, out3_ref)):
        at = pl.ds(pl.multiple_of(((x + d) % 4) * cols, cols), cols)
        both = keep_ref[at, :].astype(F32) + got_ref[at, :].astype(F32)
        out_ref[:, :rows] = both.astype(BF)
        out_ref[:, rows:] = folded


def finish_kernel(
    counts_ref, a_ref, b_ref, c_ref, d_ref, own_ref, stat_ref, gain_ref, grads_ref,
    points_ref, qkv_ref, proj_ref,
):
    rows = a_ref.shape[1] - 128
    cols = own_ref.shape[0] // 2
    width = gain_ref.shape[1]
    parts = [ref[...].astype(F32) for ref in (a_ref, b_ref, c_ref, d_ref)]
    total = (parts[0] + parts[1]) + (parts[2] + parts[3])
    folded = total[:, rows:]
    total = total[:, :rows]
    each = rows // 128
    firsts = (folded[:each] + folded[each : 2 * each]) * (1.0 / width)
    seconds = (folded[2 * each : 3 * each] + folded[3 * each : 4 * each]) * (1.0 / width)
    first = jnp.concatenate([firsts[i : i + 1] for i in range(each)], axis=1)
    second = jnp.concatenate([seconds[i : i + 1] for i in range(each)], axis=1)
    mine = iota((cols, width), 1) == iota((cols, width), 0) + lax.axis_index("mp") * cols
    gain = jnp.sum(jnp.where(mine, gain_ref[...], 0.0), axis=1, keepdims=True)
    mean = stat_ref[0:1, :]
    spread = stat_ref[4:5, :]
    normed = (own_ref[:cols, :].astype(F32) - mean) * spread
    dnorm = spread * (total * gain - first - normed * second)
    out = own_ref[cols:, :].astype(F32) + dnorm
    slot = iota((cols, rows), 1)
    points_ref[...] = jnp.where(slot < counts_ref[lax.axis_index("space"), 0, 0], out, 0.0).astype(BF)

    grads = jnp.sum(grads_ref[...].astype(F32), axis=0)
    qkv_ref[...] = jnp.concatenate(
        [grads[:, h * GROUP : h * GROUP + 3 * HEAD] for h in range(4)], axis=1
    )
    proj_ref[...] = jnp.concatenate(
        [grads[:, h * GROUP + 3 * HEAD : (h + 1) * GROUP] for h in range(4)], axis=1
    )


def whole(shape):
    return pl.BlockSpec(shape, lambda *_: (0,) * len(shape))


ANY = pl.BlockSpec(memory_space=pl.ANY)
shape = jax.ShapeDtypeStruct


SMEM = pl.BlockSpec(memory_space=pltpu.SMEM)


def call(kernel, args, grid, in_specs, out_specs, out_shape, scratch, limit, micros, aliases={}):
    return pl.pallas_call(
        kernel,
        grid=grid,
        in_specs=in_specs,
        out_specs=out_specs,
        scratch_shapes=scratch,
        out_shape=out_shape,
        input_output_aliases=aliases,
        cost_estimate=pl.CostEstimate(
            flops=int(micros * 1.1e9), bytes_accessed=0, transcendentals=0
        ),
        compiler_params=pltpu.CompilerParams(vmem_limit_bytes=int(limit * MIB)),
    )(*args)


def project(counts, points, cotangent, gain, w_qkv, w_proj):
    slots, width = points.shape
    cols = width // 8
    half = slots // 2
    points, cotangent, gain, w_qkv, w_proj = (
        pltpu.with_memory_space_constraint(a, pltpu.HBM)
        for a in (points, cotangent, gain, w_qkv, w_proj)
    )
    chunks = half // CHUNK
    outs = [
        shape((slots, PAIR), BF),
        shape((slots, PAIR), BF),
        pltpu.HBM((slots, width), BF),
        shape((2 * cols, slots), BF),
        shape((8, slots), F32),
    ]
    head = shape((half, LANES), BF)
    extra = [shape((width, LANES), BF), shape((width, LANES + 2 * PAIR), BF), shape((16, LANES), BF)]
    scratch = [
        pltpu.VMEM((half, width), BF),
        pltpu.VMEM((half, width), BF),
        pltpu.VMEM(gain.shape, F32),
        pltpu.VMEM((half, LANES), BF),
        pltpu.VMEM((half, width), BF),
        pltpu.VMEM((2 * cols, half), BF),
        pltpu.VMEM((8, half), F32),
        pltpu.SemaphoreType.DMA((2, chunks)),
        pltpu.SemaphoreType.DMA((3,)),
        pltpu.SemaphoreType.DMA((6, chunks)),
    ]
    results = call(
        project_kernel,
        (points, cotangent, gain, w_qkv, w_proj),
        (1,),
        [ANY] * 5,
        [ANY] * 6 + [whole(e.shape) for e in extra],
        outs + [head] + extra,
        [pltpu.VMEM(w_qkv.shape, BF), pltpu.VMEM(w_proj.shape, BF)] + scratch,
        32,
        4.5,
    )
    head, wide, side, wg = results[5:]
    carried = list(results[:5])
    carried[2] = pltpu.with_memory_space_constraint(carried[2], pltpu.HBM)
    outs = outs + [shape((slots, PAIR), BF)]
    again = call(
        front_kernel,
        (counts, points, cotangent, gain, wide, side, head, *carried),
        (1,),
        [SMEM] + [ANY] * 11,
        [ANY] * 5 + [whole((slots, PAIR))],
        outs,
        [pltpu.VMEM(e.shape, BF) for e in extra[:2]]
        + scratch
        + [pltpu.VMEM((slots, PAIR), BF), pltpu.SemaphoreType.DMA((1,))]
        + attend_scratch(slots, 1),
        32,
        11.0,
        {7 + i: i for i in range(5)},
    )
    return (*again, head, wide, wg)


def count_kernel(cells_ref, out_ref):
    total = jnp.sum(cells_ref[...].astype(F32), axis=1, keepdims=True).astype(jnp.int32)
    out_ref[...] = jnp.broadcast_to(total.reshape(1, 1, 1), out_ref.shape)


def count(cells, n_space):
    out = shape((n_space, 1, 128), jnp.int32)
    cells = cells.reshape(1, -1)
    return call(
        count_kernel, (cells,), (1,), [whole(cells.shape)], whole(out.shape), out, [], 1, 0.5
    )


def attend_scratch(slots, pairs):
    lanes = pairs * PAIR
    return [
        pltpu.VMEM((PATCH, lanes), BF),
        pltpu.VMEM((PATCH, lanes), BF),
        pltpu.VMEM((lanes, PATCH), BF),
        pltpu.VMEM((2 * pairs, 2 * HEAD, PATCH), BF),
        pltpu.VMEM((8, BLOCK), F32),
        pltpu.VMEM((4, PATCH, BLOCK), F32),
        pltpu.VMEM((PATCH, 4 * BLOCK), BF),
        pltpu.VMEM((PATCH, 4 * BLOCK), BF),
        pltpu.VMEM((lanes, PATCH), F32),
        pltpu.VMEM((PATCH + 2 * MARGIN, lanes), BF),
        pltpu.VMEM((slots + 2 * MARGIN, lanes), BF),
        pltpu.VMEM((PATCH + 2 * MARGIN, lanes), BF),
    ]


def attend(spanning, counts, owns, following, after):
    slots = owns[0].shape[0]
    pairs = len(owns)
    lanes = pairs * PAIR
    outs = [shape((slots, lanes), BF)] + ([shape((PATCH, lanes), BF)] if spanning else [])
    args = (*owns, following) if spanning else tuple(owns)
    return call(
        functools.partial(attend_kernel, spanning, pairs),
        (counts, *args, after),
        (1,),
        [SMEM] + [whole(a.shape) for a in args] + [ANY],
        [whole(o.shape) for o in outs],
        outs,
        attend_scratch(slots, pairs),
        24,
        7.5 * pairs,
    )


def products(mine, locals_, got, heads, wide, wg):
    slots = mine.shape[0]
    width = wide.shape[0]
    rows = 256
    half = width // 2 + 16
    outs = [shape((half, slots), BF), shape((half, slots), BF), shape((slots, LANES), BF)]
    steps = PATCH // rows

    def part(offset, more, more_specs, steps, aliases):
        down = pl.BlockSpec((rows, PAIR), lambda i: (i + offset, 0))
        full = pl.BlockSpec((rows, LANES), lambda i: (i + offset, 0))
        across = pl.BlockSpec((half, rows), lambda i: (0, i + offset))
        return call(
            functools.partial(product_kernel, bool(more)),
            (mine, *locals_, *heads, wide, wg, *more),
            (steps,),
            [full, down, down, down, down, whole(wide.shape), whole(wg.shape)] + more_specs,
            [across, across, full],
            outs,
            [pltpu.VMEM((width, LANES), BF)],
            16,
            2.0,
            aliases,
        )

    upper = part(steps, (), [], slots // rows - steps, {})
    row = pl.BlockSpec((rows, LANES), lambda i: (i, 0))
    return part(0, (got, *upper), [row] + [ANY] * 3, steps, {8 + i: i for i in range(3)})


def weights(total, unit, dy, after):
    slots, width = unit.shape
    rows = 512
    down = lambda i: (i, 0)
    return call(
        weight_kernel,
        (total, unit, dy, after),
        (slots // rows,),
        [
            pl.BlockSpec((rows, LANES), down),
            pl.BlockSpec((rows, width), down),
            pl.BlockSpec((rows, width), down),
            ANY,
        ],
        [whole((width, LANES))],
        [shape((width, LANES), BF)],
        [pltpu.VMEM((LANES, width), F32), pltpu.VMEM((LANES, width), F32)],
        24,
        4.0,
    )[0]


def pair_sum(keep, got, after):
    total, slots = keep.shape
    out = shape(((total - 16) // 4, slots + 128), BF)
    return call(
        pair_kernel,
        (keep, got, after),
        (1,),
        [whole(keep.shape)] * 2 + [ANY],
        [whole(out.shape)] * 4,
        [out] * 4,
        [],
        24,
        2.3,
    )


def finish(counts, parts, own, stat, gain, grads):
    cols, slots = own.shape
    rows = grads.shape[1]
    outs = [
        shape((cols // 2, slots), BF),
        shape((rows, 3 * GROUP), F32),
        shape((rows, GROUP), F32),
    ]
    args = (*parts, own, stat, gain, grads)
    points, qkv, proj = call(
        finish_kernel,
        (counts, *args),
        (1,),
        [SMEM] + [whole(a.shape) for a in args],
        [whole(o.shape) for o in outs],
        outs,
        [],
        24,
        2.3,
    )
    return points.T, qkv, proj.T


def on_device(points, cotangent, cell_counts, norm_gain, w_qkv, w_proj):
    slots, width = points.shape
    n_space = lax.axis_size("space")
    n_mp = lax.axis_size("mp")
    counts = lax.all_to_all(count(cell_counts, n_space), "space", 0, 0)
    gain = norm_gain.reshape(1, width)
    one, two, unit, own, stat, local_a, head, wide, wg = project(
        counts, points, cotangent, gain, w_qkv.T, w_proj
    )
    back = [(i + 1, i) for i in range(n_space - 1)]
    onward = [(i, i + 1) for i in range(n_space - 1)]
    following = lax.ppermute(head, "space", back)
    mine, spill = attend(True, counts, (one, two), following, one)
    got = lax.ppermute(spill, "space", onward)
    local_b = attend(False, counts, (two,), None, mine)[0]
    keep, send, total = products(mine, (local_a, local_b), got, (one, two), wide, wg)
    swap = [(i, i ^ 1) for i in range(n_mp)]
    other = lax.ppermute(send, "mp", swap)
    grads = weights(total, unit, cotangent, keep)
    gathered = lax.all_to_all(
        grads.reshape(n_space, width // n_space, LANES), "space", 0, 0
    )
    parts = pair_sum(keep, other, grads)
    received = [parts[0]]
    for d in range(1, n_mp // 2):
        route = [(i, (i + 2 * d) % n_mp) for i in range(n_mp)]
        received.append(lax.ppermute(parts[d], "mp", route))
    return finish(counts, received, own, stat, gain, gathered)


def solution(mesh):
    return jax.shard_map(
        on_device,
        mesh=mesh,
        in_specs=(
            P("space", None),
            P("space", None),
            P("space"),
            P(),
            P(None, "mp"),
            P("mp", None),
        ),
        out_specs=(P("space", "mp"), P("space", "mp"), P("mp", "space")),
        check_vma=False,
    )
```

```python
import functools

import jax
import jax.numpy as jnp
from jax import lax
from jax.experimental import pallas as pl
from jax.experimental.pallas import tpu as pltpu
from jax.sharding import PartitionSpec as P

H = 32
PATCH = 1024
EPS = 1e-05
MASKED = -1e30
HEAD = 16
GROUP = 64
LANES = 256
PAIR = 128
BLOCK = 256
SHIFT = 128
CHUNK = 512
MIB = 1024 * 1024
FULL = 60.5
LOG2E = 1.4426950408889634
SAFE = 40.0

BF = jnp.bfloat16
F32 = jnp.float32
NT = (((1,), (1,)), ((), ()))
TN = (((0,), (0,)), ((), ()))


def dot(a, b):
    return jnp.dot(a, b, preferred_element_type=F32)


def dot_nt(a, b):
    return lax.dot_general(a, b, NT, preferred_element_type=F32)


def dot_tn(a, b):
    return lax.dot_general(a, b, TN, preferred_element_type=F32)


def iota(shape, axis):
    return lax.broadcasted_iota(jnp.int32, shape, axis)


def onehot(mask):
    return jnp.where(mask, 1.0, 0.0).astype(BF)


def split(value):
    high = value.astype(BF)
    return high, (value - high.astype(F32)).astype(BF)


def project_rows(lead, x_hbm, dy_hbm, gain_hbm, *rest):
    if lead:
        wqkv_hbm, wproj_hbm = rest[:2]
        one_hbm, two_hbm, unit_hbm, own_hbm, stat_hbm, head_hbm = rest[2:8]
        wide_ref, side_ref, wg_ref = rest[8:11]
        wqkv_ref, wproj_ref = rest[11:13]
        rest = rest[13:]
        pairs = ((wqkv_hbm, wqkv_ref), (wproj_hbm, wproj_ref))
    else:
        wide_hbm, side_hbm = rest[:2]
        one_hbm, two_hbm, unit_hbm, own_hbm, stat_hbm = rest[7:12]
        wide_ref, side_ref = rest[12:14]
        rest = rest[14:]
        pairs = ((wide_hbm, wide_ref), (side_hbm, side_ref))
    x_ref, dy_ref, gain_ref, qkvu_ref, unit_ref, own_ref, stat_ref, row_sems, sems, out_sems = rest
    half, width = x_ref.shape
    cols = own_ref.shape[0] // 2
    chunks = half // CHUNK
    base = 0 if lead else half

    def rows_copy(i, which):
        src, dst = ((x_hbm, x_ref), (dy_hbm, dy_ref))[which]
        return pltpu.make_async_copy(
            src.at[pl.ds(base + i * CHUNK, CHUNK)],
            dst.at[pl.ds(i * CHUNK, CHUNK)],
            row_sems.at[which, i],
        )

    def out_copy(i, which):
        at = pl.ds(i * CHUNK, CHUNK)
        to = pl.ds(base + i * CHUNK, CHUNK)
        if which == 0:
            src, dst = qkvu_ref.at[at, :PAIR], one_hbm.at[to]
        elif which == 1:
            src, dst = qkvu_ref.at[at, PAIR:], two_hbm.at[to]
        elif which == 2:
            src, dst = unit_ref.at[at], unit_hbm.at[to]
        elif which == 3:
            src, dst = own_ref.at[:, at], own_hbm.at[:, to]
        elif which == 4:
            src, dst = stat_ref.at[:, at], stat_hbm.at[:, to]
        else:
            src, dst = qkvu_ref.at[at], head_hbm.at[to]
        return pltpu.make_async_copy(src, dst, out_sems.at[which, i])

    pairs = (*pairs, (gain_hbm, gain_ref))
    small = [pltpu.make_async_copy(src, dst, sems.at[i]) for i, (src, dst) in enumerate(pairs)]
    for copy in small:
        copy.start()
    for i in range(chunks):
        rows_copy(i, 0).start()
        rows_copy(i, 1).start()
    if lead:
        row = iota((width, cols), 0)
        col = iota((width, cols), 1)
        pick = onehot(row == col + lax.axis_index("mp") * cols)
        none = jnp.zeros((width, cols), BF)
        side_ref[:, LANES:] = jnp.concatenate([none, pick, pick, none], axis=1)
    for copy in small:
        copy.wait()
    gain = gain_ref[...]
    if lead:
        col = iota((3 * GROUP, LANES), 0)
        lane = iota((3 * GROUP, LANES), 1)
        head = sum(jnp.where(col >= 3 * HEAD * h, HEAD, 0) for h in range(1, 4))
        wide = dot_tn(wqkv_ref[...], onehot(lane == col + head)).astype(BF)
        wide_ref[...] = wide
        part = iota((GROUP, LANES), 0)
        lane = iota((GROUP, LANES), 1)
        head = sum(jnp.where(part >= HEAD * h, GROUP - HEAD, 0) for h in range(1, 4))
        up = onehot(lane == part + head + 3 * HEAD)
        side_ref[:, :LANES] = dot_tn(wproj_ref[...], up).astype(BF)
        gain_high, gain_low = split(jnp.broadcast_to(gain, (16, width)))
        wg_high, wg_low = split(dot(gain_high, wide) + dot(gain_low, wide))
        row = iota((16, LANES), 0)
        wg_ref[...] = jnp.where(
            row == 0, wg_high.astype(F32), jnp.where(row == 1, wg_low.astype(F32), 0.0)
        ).astype(BF)

    copies = []
    for i in range(chunks):
        rows_copy(i, 0).wait()
        rows_copy(i, 1).wait()
        at = slice(i * CHUNK, (i + 1) * CHUNK)
        x_low = x_ref[at, :]
        x = x_low.astype(F32)
        mean = jnp.mean(x, axis=-1, keepdims=True)
        center = x - mean
        spread = lax.rsqrt(jnp.mean(center * center, axis=-1, keepdims=True) + EPS)
        unit = (center * spread * gain).astype(BF)
        unit_ref[at, :] = unit
        from_dy = dot(dy_ref[at, :], side_ref[:, : LANES + PAIR])
        qkvu_ref[at, :] = (dot(unit, wide_ref[...]) + from_dy[:, :LANES]).astype(BF)
        own = dot(x_low, side_ref[:, LANES + PAIR :]) + from_dy[:, LANES:]
        own_ref[:, at] = own.T.astype(BF)
        both = jnp.where(iota((CHUNK, 128), 1) < 4, mean, spread)
        stat_ref[:, at] = both.T[:8, :]
        for which in range(6 if lead else 5):
            copies.append(out_copy(i, which))
            copies[-1].start()
    return copies


def project_kernel(*refs):
    for copy in project_rows(True, *refs):
        copy.wait()


def second_kernel(*refs):
    for copy in project_rows(False, *refs):
        copy.wait()


def place_in_row(counts_ref):
    place = lax.axis_index("space")
    n_space = counts_ref.shape[0]
    start = jnp.int32(0)
    for i in range(n_space):
        start = start + jnp.where(i < place, counts_ref[i, 0, 0], 0)
    count = counts_ref[place, 0, 0]
    head_len = (PATCH - start % PATCH) % PATCH
    tail_len = jnp.where(place == n_space - 1, 0, (PATCH - (start + count) % PATCH) % PATCH)
    n_patch = (count - head_len + PATCH - 1) // PATCH
    return count, head_len, tail_len, n_patch


MARGIN = 2 * SHIFT


def shifter(first):
    part = first & (SHIFT - 1)
    pick = onehot(iota((SHIFT, 2 * SHIFT), 1) == iota((SHIFT, 2 * SHIFT), 0) + part)

    def block(src_ref, start):
        rows = src_ref.shape[0]
        base = jnp.clip(first - part + start + MARGIN, 0, rows - MARGIN)
        return dot(pick, src_ref[pl.ds(pl.multiple_of(base, SHIFT), 2 * SHIFT), :])

    return block


def padded(dst_ref, src_ref, limit, at):
    rows, width = src_ref.shape
    cols = slice(at, at + width)
    none = jnp.zeros((MARGIN, width), BF)
    dst_ref[:MARGIN, cols] = none
    dst_ref[MARGIN + rows :, cols] = none
    kept = iota(src_ref.shape, 0) < limit
    dst_ref[MARGIN : MARGIN + rows, cols] = jnp.where(
        kept, src_ref[...].astype(F32), 0.0
    ).astype(BF)


def attend_kernel(spanning, pairs, counts_ref, *rest):
    own_refs = rest[:pairs]
    if spanning:
        next_ref = rest[pairs]
        out_ref, out_next_ref = rest[pairs + 2 : pairs + 4]
        rest = rest[pairs + 4 :]
    else:
        out_ref = rest[pairs + 1]
        rest = rest[pairs + 2 :]
    (x_ref, left_ref, flip_ref, value_ref, top_ref, exp_ref, low_ref, grad_ref, turn_ref,
     done_ref, own_pad_ref, next_pad_ref) = rest
    slots = own_refs[0].shape[0]
    lanes = pairs * PAIR
    count, head_len, tail_len, n_patch = place_in_row(counts_ref)
    scale = HEAD ** (-0.5)

    def work():
        first = head_len + (PATCH * (n_patch - 1) if spanning else 0)

        for p in range(pairs):
            padded(own_pad_ref, own_refs[p], count, p * PAIR)
        from_own = shifter(first)
        if spanning:
            padded(next_pad_ref, next_ref, tail_len, 0)
            from_next = shifter(first - count)
        for start in range(0, PATCH, SHIFT):
            piece = from_own(own_pad_ref, start)
            if spanning:
                piece = piece + from_next(next_pad_ref, start)
            x_ref[start : start + SHIFT, :] = piece.astype(BF)
        x = x_ref[...]
        src = iota((lanes, lanes), 0)
        dst = iota((lanes, lanes), 1)
        sub = dst & (GROUP - 1)
        keys = sub < 2 * HEAD
        move = onehot(
            ((sub < HEAD) & (src == dst + HEAD))
            | ((sub >= HEAD) & (sub < 3 * HEAD) & (src == dst))
        )
        lane = iota((PATCH, lanes), 1) & (GROUP - 1)
        fixed = jnp.where((lane > 3 * HEAD) & (lane < 3 * HEAD + 4), 1.0, 0.0)
        if spanning:
            valid = count - first + tail_len
            row = iota((PATCH, lanes), 0)
            fixed = jnp.where((lane == 3 * HEAD) & (row >= valid), MASKED, fixed)
        left_ref[...] = (dot(x, move) + fixed).astype(BF)
        flip = dot_nt(onehot(src == dst), x)
        flip_ref[...] = flip.astype(BF)
        square = flip * flip
        most = jnp.zeros((1, 1), F32)
        for h in range(2 * pairs):
            at = h * GROUP
            value_ref[h, :HEAD, :] = flip_ref[at + 2 * HEAD : at + 3 * HEAD, :]
            value_ref[h, HEAD:, :] = jnp.ones((HEAD, PATCH), BF)
            most_q = jnp.sum(square[at : at + HEAD], axis=0, keepdims=True)
            most_k = jnp.sum(square[at + HEAD : at + 2 * HEAD], axis=0, keepdims=True)
            both = jnp.max(most_q, axis=1, keepdims=True) * jnp.max(most_k, axis=1, keepdims=True)
            most = jnp.maximum(most, both)
        bounded = jnp.max(most) * scale * scale <= SAFE * SAFE
        turn_ref[...] = jnp.zeros_like(turn_ref)
        top_ref[...] = jnp.zeros_like(top_ref)
        row = iota((HEAD, BLOCK), 0)

        def placed(pieces, h):
            zero = jnp.zeros((GROUP, BLOCK), BF)
            group = jnp.concatenate(pieces, axis=0)
            return jnp.concatenate([group, zero] if h % 2 == 0 else [zero, group], axis=0)

        nothing = jnp.zeros((HEAD, BLOCK), BF)

        def score_right(h, here, top):
            query = flip_ref[h * GROUP : h * GROUP + HEAD, here].astype(F32) * (scale * LOG2E)
            high, low = split(query)
            if top is None:
                extra = jnp.where(row == 0, 1.0, 0.0)
            else:
                top_high = top.astype(BF).astype(F32)
                top_mid = (top - top_high).astype(BF).astype(F32)
                top_low = top - top_high - top_mid
                extra = jnp.where(
                    row == 0,
                    1.0,
                    jnp.where(
                        row == 1,
                        -top_high,
                        jnp.where(row == 2, -top_mid, jnp.where(row == 3, -top_low, 0.0)),
                    ),
                )
            return placed([high, low, nothing, extra.astype(BF)], h)

        def block(pair, step, carry):
            left = left_ref.at[:, pair * PAIR : (pair + 1) * PAIR]
            here = [
                pl.ds(pl.multiple_of((step * 2 + t // 2) * BLOCK, BLOCK), BLOCK) for t in range(4)
            ]

            @pl.when(jnp.logical_not(bounded))
            def _():
                for t in range(4):
                    scores = dot(left[...], score_right(pair * 2 + t % 2, here[t], None))
                    top_ref[t : t + 1, :] = jnp.max(scores, axis=0, keepdims=True)

            inverses = [None] * 4
            rights = [None] * 4
            spans = [
                slice((t % 2 * 2 + t // 2) * BLOCK, (t % 2 * 2 + t // 2 + 1) * BLOCK)
                for t in range(4)
            ]
            ups = [None] * 4
            queries = [None] * 4

            def stage_exp(t):
                scores = dot(left[...], score_right(pair * 2 + t % 2, here[t], top_ref[t : t + 1, :]))
                exps = jnp.exp2(scores)
                exp_ref[t] = exps
                low_ref[:, spans[t]] = exps.astype(BF)

            def stage_sum(t):
                at = (pair * 2 + t % 2) * GROUP
                result = dot(value_ref[pair * 2 + t % 2], low_ref[:, spans[t]])
                inverse = 1.0 / result[HEAD : HEAD + 1]
                inverses[t] = inverse
                attended = result[:HEAD] * inverse
                turn_ref[at + 3 * HEAD : at + 4 * HEAD, here[t]] = attended
                up = flip_ref[at + 3 * HEAD : at + 4 * HEAD, here[t]].astype(F32)
                scaled = up * scale
                delta = jnp.sum(scaled * attended, axis=0, keepdims=True)
                delta_high = delta.astype(BF).astype(F32)
                extra = jnp.where(
                    row == 1, -delta_high, jnp.where(row == 2, delta_high - delta, 0.0)
                ).astype(BF)
                rights[t] = placed([nothing, nothing, scaled.astype(BF), extra], t % 2)
                query = flip_ref[at : at + HEAD, here[t]].astype(F32)
                ups[t] = (up * inverse).astype(BF)
                queries[t] = (query * inverse).astype(BF)

            def stage_grad(t):
                dprob = dot(left[...], rights[t])
                grad_ref[:, spans[t]] = (exp_ref[t] * dprob).astype(BF)

            def stage_query(t):
                at = (pair * 2 + t % 2) * GROUP
                result = dot(flip_ref[at + HEAD : at + 2 * HEAD, :], grad_ref[:, spans[t]])
                turn_ref[at : at + HEAD, here[t]] = result * inverses[t]

            for stage in (stage_exp, stage_sum, stage_grad, stage_query):
                for t in range(4):
                    stage(t)
            for h in range(2):
                at = (pair * 2 + h) * GROUP
                both = slice(2 * h * BLOCK, 2 * (h + 1) * BLOCK)
                turn_ref[at + 2 * HEAD : at + 3 * HEAD, :] += dot_nt(
                    jnp.concatenate([ups[h], ups[h + 2]], axis=1), low_ref[:, both]
                )
                turn_ref[at + HEAD : at + 2 * HEAD, :] += dot_nt(
                    jnp.concatenate([queries[h], queries[h + 2]], axis=1), grad_ref[:, both]
                )
            return carry

        for pair in range(pairs):
            lax.fori_loop(0, PATCH // (2 * BLOCK), functools.partial(block, pair), 0)
        done_ref[:MARGIN, :] = jnp.zeros((MARGIN, lanes), BF)
        done_ref[MARGIN + PATCH :, :] = jnp.zeros((MARGIN, lanes), BF)
        done_ref[MARGIN : MARGIN + PATCH, :] = turn_ref[...].T.astype(BF)
        row = iota((SHIFT, lanes), 0)
        to_own = shifter(-first)
        for start in range(0, slots, SHIFT):
            piece = to_own(done_ref, start)
            out_ref[start : start + SHIFT, :] = jnp.where(
                row < count - start, piece, 0.0
            ).astype(BF)
        if spanning:
            to_next = shifter(count - first)
            for start in range(0, PATCH, SHIFT):
                piece = to_next(done_ref, start)
                out_next_ref[start : start + SHIFT, :] = jnp.where(
                    row < tail_len - start, piece, 0.0
                ).astype(BF)

    if spanning:
        work()
    else:
        pl.when(n_patch == 2)(work)

        @pl.when(n_patch < 2)
        def _():
            out_ref[...] = jnp.zeros_like(out_ref)


def product_kernel(lower, mine_ref, a_ref, b_ref, one_ref, two_ref, wide_ref, wg_ref, *rest):
    if lower:
        got_ref = rest[0]
        rest = rest[4:]
    keep_ref, send_ref, total_ref, turned_ref = rest
    step = pl.program_id(0)
    rows = a_ref.shape[0]
    core = lax.axis_index("mp") % 2
    cols = wide_ref.shape[0] // 8

    @pl.when(step == 0)
    def _():
        for side in range(2):
            for x in range(4):
                from_row = pl.multiple_of((2 * x + (core ^ side)) * cols, cols)
                to_row = (side * 4 + x) * cols
                turned_ref[to_row : to_row + cols, :] = wide_ref[pl.ds(from_row, cols), :]

    local = jnp.concatenate([a_ref[...], b_ref[...]], axis=1)
    wide_total = mine_ref[...].astype(F32) + local.astype(F32)
    if lower:
        wide_total = wide_total + got_ref[...].astype(F32)
    total = wide_total.astype(BF)
    total_ref[...] = total
    du = dot_nt(turned_ref[...], total).astype(BF)
    half = 4 * cols
    keep_ref[:half, :] = du[:half]
    send_ref[:half, :] = du[half:]
    lane = iota((rows, LANES), 1) & (GROUP - 1)
    qkvu = jnp.concatenate([one_ref[...], two_ref[...]], axis=1).astype(F32)
    product = jnp.where(lane < 3 * HEAD, wide_total * qkvu, 0.0)
    high, low = split(product)
    ones = jnp.ones((16, LANES), BF)
    second = (dot_nt(ones, high) + dot_nt(ones, low))[:1]
    first_rows = dot_nt(wg_ref[...], total)
    first = first_rows[:1] + first_rows[1:2]
    stats = pack_stats(first, second, rows)
    keep_ref[half:, :] = stats
    send_ref[half:, :] = stats


def weight_kernel(total_ref, unit_ref, dy_ref, after_ref, grads_ref, gu_ref, gy_ref):
    step = pl.program_id(0)

    @pl.when(step == 0)
    def _():
        gu_ref[...] = jnp.zeros_like(gu_ref)
        gy_ref[...] = jnp.zeros_like(gy_ref)

    total = total_ref[...]
    gu_ref[...] += dot_tn(total, unit_ref[...])
    gy_ref[...] += dot_tn(total, dy_ref[...])

    @pl.when(step == pl.num_programs(0) - 1)
    def _():
        row = iota(gu_ref.shape, 0) & (GROUP - 1)
        grads_ref[...] = jnp.where(row < 3 * HEAD, gu_ref[...], gy_ref[...]).T.astype(BF)


def pack_stats(first, second, rows):
    row = iota((16, rows), 0)
    first_high = first.astype(BF).astype(F32)
    second_high = second.astype(BF).astype(F32)
    return jnp.where(
        row == 0,
        first_high,
        jnp.where(
            row == 1,
            first - first_high,
            jnp.where(row == 2, second_high, jnp.where(row == 3, second - second_high, 0.0)),
        ),
    ).astype(BF)


def pair_kernel(keep_ref, got_ref, after_ref, out0_ref, out1_ref, out2_ref, out3_ref):
    x = lax.axis_index("mp") // 2
    rows = keep_ref.shape[1]
    half = keep_ref.shape[0] - 16
    cols = half // 4
    stats = keep_ref[half:, :].astype(F32) + got_ref[half:, :].astype(F32)
    packed = pack_stats(stats[0:1] + stats[1:2], stats[2:3] + stats[3:4], rows).astype(F32)
    folded = jnp.concatenate(
        [packed[i : i + 1, j : j + 128] for i in range(4) for j in range(0, rows, 128)], axis=0
    ).astype(BF)
    for d, out_ref in enumerate((out0_ref, out1_ref, out2_ref, out3_ref)):
        at = pl.ds(pl.multiple_of(((x + d) % 4) * cols, cols), cols)
        both = keep_ref[at, :].astype(F32) + got_ref[at, :].astype(F32)
        out_ref[:, :rows] = both.astype(BF)
        out_ref[:, rows:] = folded


def finish_kernel(
    counts_ref, a_ref, b_ref, c_ref, d_ref, own_ref, stat_ref, gain_ref, grads_ref,
    points_ref, qkv_ref, proj_ref,
):
    rows = a_ref.shape[1] - 128
    cols = own_ref.shape[0] // 2
    width = gain_ref.shape[1]
    parts = [ref[...].astype(F32) for ref in (a_ref, b_ref, c_ref, d_ref)]
    total = (parts[0] + parts[1]) + (parts[2] + parts[3])
    folded = total[:, rows:]
    total = total[:, :rows]
    each = rows // 128
    firsts = (folded[:each] + folded[each : 2 * each]) * (1.0 / width)
    seconds = (folded[2 * each : 3 * each] + folded[3 * each : 4 * each]) * (1.0 / width)
    first = jnp.concatenate([firsts[i : i + 1] for i in range(each)], axis=1)
    second = jnp.concatenate([seconds[i : i + 1] for i in range(each)], axis=1)
    mine = iota((cols, width), 1) == iota((cols, width), 0) + lax.axis_index("mp") * cols
    gain = jnp.sum(jnp.where(mine, gain_ref[...], 0.0), axis=1, keepdims=True)
    mean = stat_ref[0:1, :]
    spread = stat_ref[4:5, :]
    normed = (own_ref[:cols, :].astype(F32) - mean) * spread
    dnorm = spread * (total * gain - first - normed * second)
    out = own_ref[cols:, :].astype(F32) + dnorm
    slot = iota((cols, rows), 1)
    points_ref[...] = jnp.where(slot < counts_ref[lax.axis_index("space"), 0, 0], out, 0.0).astype(BF)

    grads = jnp.sum(grads_ref[...].astype(F32), axis=0)
    qkv_ref[...] = jnp.concatenate(
        [grads[:, h * GROUP : h * GROUP + 3 * HEAD] for h in range(4)], axis=1
    )
    proj_ref[...] = jnp.concatenate(
        [grads[:, h * GROUP + 3 * HEAD : (h + 1) * GROUP] for h in range(4)], axis=1
    )


def whole(shape):
    return pl.BlockSpec(shape, lambda *_: (0,) * len(shape))


ANY = pl.BlockSpec(memory_space=pl.ANY)
shape = jax.ShapeDtypeStruct


SMEM = pl.BlockSpec(memory_space=pltpu.SMEM)


def call(kernel, args, grid, in_specs, out_specs, out_shape, scratch, limit, micros, aliases={}):
    return pl.pallas_call(
        kernel,
        grid=grid,
        in_specs=in_specs,
        out_specs=out_specs,
        scratch_shapes=scratch,
        out_shape=out_shape,
        input_output_aliases=aliases,
        cost_estimate=pl.CostEstimate(
            flops=int(micros * 1.1e9), bytes_accessed=0, transcendentals=0
        ),
        compiler_params=pltpu.CompilerParams(vmem_limit_bytes=int(limit * MIB)),
    )(*args)


def project(cells, n_space, points, cotangent, gain, w_qkv, w_proj):
    slots, width = points.shape
    cols = width // 8
    half = slots // 2
    points, cotangent, gain, w_qkv, w_proj = (
        pltpu.with_memory_space_constraint(a, pltpu.HBM)
        for a in (points, cotangent, gain, w_qkv, w_proj)
    )
    chunks = half // CHUNK
    outs = [
        shape((slots, PAIR), BF),
        shape((slots, PAIR), BF),
        pltpu.HBM((slots, width), BF),
        shape((2 * cols, slots), BF),
        shape((8, slots), F32),
    ]
    head = shape((half, LANES), BF)
    extra = [shape((width, LANES), BF), shape((width, LANES + 2 * PAIR), BF), shape((16, LANES), BF)]
    scratch = [
        pltpu.VMEM((half, width), BF),
        pltpu.VMEM((half, width), BF),
        pltpu.VMEM(gain.shape, F32),
        pltpu.VMEM((half, LANES), BF),
        pltpu.VMEM((half, width), BF),
        pltpu.VMEM((2 * cols, half), BF),
        pltpu.VMEM((8, half), F32),
        pltpu.SemaphoreType.DMA((2, chunks)),
        pltpu.SemaphoreType.DMA((3,)),
        pltpu.SemaphoreType.DMA((6, chunks)),
    ]
    results = call(
        project_kernel,
        (points, cotangent, gain, w_qkv, w_proj),
        (1,),
        [ANY] * 5,
        [ANY] * 6 + [whole(e.shape) for e in extra],
        outs + [head] + extra,
        [pltpu.VMEM(w_qkv.shape, BF), pltpu.VMEM(w_proj.shape, BF)] + scratch,
        32,
        4.5,
    )
    head, wide, side, wg = results[5:]
    carried = list(results[:5])
    carried[2] = pltpu.with_memory_space_constraint(carried[2], pltpu.HBM)
    counts = lax.all_to_all(count(cells, n_space, wg), "space", 0, 0)
    again = call(
        second_kernel,
        (points, cotangent, gain, wide, side, *carried),
        (1,),
        [ANY] * 10,
        [ANY] * 5,
        outs,
        [pltpu.VMEM(e.shape, BF) for e in extra[:2]] + scratch,
        32,
        3.3,
        {5 + i: i for i in range(5)},
    )
    return (counts, *again, head, wide, wg)


def count_kernel(cells_ref, after_ref, out_ref):
    total = jnp.sum(cells_ref[...].astype(F32), axis=1, keepdims=True).astype(jnp.int32)
    out_ref[...] = jnp.broadcast_to(total.reshape(1, 1, 1), out_ref.shape)


def count(cells, n_space, after):
    out = shape((n_space, 1, 128), jnp.int32)
    cells = cells.reshape(1, -1)
    return call(
        count_kernel, (cells, after), (1,), [whole(cells.shape), ANY], whole(out.shape), out, [], 1, 0.5
    )


def attend_scratch(slots, pairs):
    lanes = pairs * PAIR
    return [
        pltpu.VMEM((PATCH, lanes), BF),
        pltpu.VMEM((PATCH, lanes), BF),
        pltpu.VMEM((lanes, PATCH), BF),
        pltpu.VMEM((2 * pairs, 2 * HEAD, PATCH), BF),
        pltpu.VMEM((8, BLOCK), F32),
        pltpu.VMEM((4, PATCH, BLOCK), F32),
        pltpu.VMEM((PATCH, 4 * BLOCK), BF),
        pltpu.VMEM((PATCH, 4 * BLOCK), BF),
        pltpu.VMEM((lanes, PATCH), F32),
        pltpu.VMEM((PATCH + 2 * MARGIN, lanes), BF),
        pltpu.VMEM((slots + 2 * MARGIN, lanes), BF),
        pltpu.VMEM((PATCH + 2 * MARGIN, lanes), BF),
    ]


def attend(spanning, counts, owns, following, after):
    slots = owns[0].shape[0]
    pairs = len(owns)
    lanes = pairs * PAIR
    outs = [shape((slots, lanes), BF)] + ([shape((PATCH, lanes), BF)] if spanning else [])
    args = (*owns, following) if spanning else tuple(owns)
    return call(
        functools.partial(attend_kernel, spanning, pairs),
        (counts, *args, after),
        (1,),
        [SMEM] + [whole(a.shape) for a in args] + [ANY],
        [whole(o.shape) for o in outs],
        outs,
        attend_scratch(slots, pairs),
        24,
        7.5 * pairs,
    )


def products(mine, locals_, got, heads, wide, wg):
    slots = mine.shape[0]
    width = wide.shape[0]
    rows = 256
    half = width // 2 + 16
    outs = [shape((half, slots), BF), shape((half, slots), BF), shape((slots, LANES), BF)]
    steps = PATCH // rows

    def part(offset, more, more_specs, steps, aliases):
        down = pl.BlockSpec((rows, PAIR), lambda i: (i + offset, 0))
        full = pl.BlockSpec((rows, LANES), lambda i: (i + offset, 0))
        across = pl.BlockSpec((half, rows), lambda i: (0, i + offset))
        return call(
            functools.partial(product_kernel, bool(more)),
            (mine, *locals_, *heads, wide, wg, *more),
            (steps,),
            [full, down, down, down, down, whole(wide.shape), whole(wg.shape)] + more_specs,
            [across, across, full],
            outs,
            [pltpu.VMEM((width, LANES), BF)],
            16,
            2.0,
            aliases,
        )

    upper = part(steps, (), [], slots // rows - steps, {})
    row = pl.BlockSpec((rows, LANES), lambda i: (i, 0))
    return part(0, (got, *upper), [row] + [ANY] * 3, steps, {8 + i: i for i in range(3)})


def weights(total, unit, dy, after):
    slots, width = unit.shape
    rows = 512
    down = lambda i: (i, 0)
    return call(
        weight_kernel,
        (total, unit, dy, after),
        (slots // rows,),
        [
            pl.BlockSpec((rows, LANES), down),
            pl.BlockSpec((rows, width), down),
            pl.BlockSpec((rows, width), down),
            ANY,
        ],
        [whole((width, LANES))],
        [shape((width, LANES), BF)],
        [pltpu.VMEM((LANES, width), F32), pltpu.VMEM((LANES, width), F32)],
        24,
        4.0,
    )[0]


def pair_sum(keep, got, after):
    total, slots = keep.shape
    out = shape(((total - 16) // 4, slots + 128), BF)
    return call(
        pair_kernel,
        (keep, got, after),
        (1,),
        [whole(keep.shape)] * 2 + [ANY],
        [whole(out.shape)] * 4,
        [out] * 4,
        [],
        24,
        2.3,
    )


def finish(counts, parts, own, stat, gain, grads):
    cols, slots = own.shape
    rows = grads.shape[1]
    outs = [
        shape((cols // 2, slots), BF),
        shape((rows, 3 * GROUP), F32),
        shape((rows, GROUP), F32),
    ]
    args = (*parts, own, stat, gain, grads)
    points, qkv, proj = call(
        finish_kernel,
        (counts, *args),
        (1,),
        [SMEM] + [whole(a.shape) for a in args],
        [whole(o.shape) for o in outs],
        outs,
        [],
        24,
        2.3,
    )
    return points.T, qkv, proj.T


def on_device(points, cotangent, cell_counts, norm_gain, w_qkv, w_proj):
    slots, width = points.shape
    n_space = lax.axis_size("space")
    n_mp = lax.axis_size("mp")
    gain = norm_gain.reshape(1, width)
    counts, one, two, unit, own, stat, head, wide, wg = project(
        cell_counts, n_space, points, cotangent, gain, w_qkv.T, w_proj
    )
    back = [(i + 1, i) for i in range(n_space - 1)]
    onward = [(i, i + 1) for i in range(n_space - 1)]
    following = lax.ppermute(head, "space", back)
    local_a = attend(False, counts, (one,), None, one)[0]
    mine, spill = attend(True, counts, (one, two), following, local_a)
    got = lax.ppermute(spill, "space", onward)
    local_b = attend(False, counts, (two,), None, mine)[0]
    keep, send, total = products(mine, (local_a, local_b), got, (one, two), wide, wg)
    swap = [(i, i ^ 1) for i in range(n_mp)]
    other = lax.ppermute(send, "mp", swap)
    grads = weights(total, unit, cotangent, keep)
    gathered = lax.all_to_all(
        grads.reshape(n_space, width // n_space, LANES), "space", 0, 0
    )
    parts = pair_sum(keep, other, grads)
    received = [parts[0]]
    for d in range(1, n_mp // 2):
        route = [(i, (i + 2 * d) % n_mp) for i in range(n_mp)]
        received.append(lax.ppermute(parts[d], "mp", route))
    return finish(counts, received, own, stat, gain, gathered)


def solution(mesh):
    return jax.shard_map(
        on_device,
        mesh=mesh,
        in_specs=(
            P("space", None),
            P("space", None),
            P("space"),
            P(),
            P(None, "mp"),
            P("mp", None),
        ),
        out_specs=(P("space", "mp"), P("space", "mp"), P("mp", "space")),
        check_vma=False,
    )
```

```python
import functools

import jax
import jax.numpy as jnp
from jax import lax
from jax.experimental import pallas as pl
from jax.experimental.pallas import tpu as pltpu
from jax.sharding import PartitionSpec as P

H = 32
PATCH = 1024
EPS = 1e-05
MASKED = -1e30
HEAD = 16
GROUP = 64
LANES = 256
PAIR = 128
BLOCK = 256
SHIFT = 128
CHUNK = 512
MIB = 1024 * 1024
FULL = 60.5
LOG2E = 1.4426950408889634
SAFE = 40.0

BF = jnp.bfloat16
F32 = jnp.float32
NT = (((1,), (1,)), ((), ()))
TN = (((0,), (0,)), ((), ()))


def dot(a, b):
    return jnp.dot(a, b, preferred_element_type=F32)


def dot_nt(a, b):
    return lax.dot_general(a, b, NT, preferred_element_type=F32)


def dot_tn(a, b):
    return lax.dot_general(a, b, TN, preferred_element_type=F32)


def iota(shape, axis):
    return lax.broadcasted_iota(jnp.int32, shape, axis)


def onehot(mask):
    return jnp.where(mask, 1.0, 0.0).astype(BF)


def split(value):
    high = value.astype(BF)
    return high, (value - high.astype(F32)).astype(BF)


def project_rows(lead, x_hbm, dy_hbm, gain_hbm, *rest):
    if lead:
        wqkv_hbm, wproj_hbm = rest[:2]
        one_hbm, two_hbm, unit_hbm, own_hbm, stat_hbm, head_hbm = rest[2:8]
        wide_ref, side_ref, wg_ref = rest[8:11]
        wqkv_ref, wproj_ref = rest[11:13]
        rest = rest[13:]
        pairs = ((wqkv_hbm, wqkv_ref), (wproj_hbm, wproj_ref))
    else:
        wide_hbm, side_hbm = rest[:2]
        one_hbm, two_hbm, unit_hbm, own_hbm, stat_hbm = rest[7:12]
        wide_ref, side_ref = rest[12:14]
        rest = rest[14:]
        pairs = ((wide_hbm, wide_ref), (side_hbm, side_ref))
    x_ref, dy_ref, gain_ref, qkvu_ref, unit_ref, own_ref, stat_ref, row_sems, sems, out_sems = rest
    half, width = x_ref.shape
    cols = own_ref.shape[0] // 2
    chunks = half // CHUNK
    base = 0 if lead else half

    def rows_copy(i, which):
        src, dst = ((x_hbm, x_ref), (dy_hbm, dy_ref))[which]
        return pltpu.make_async_copy(
            src.at[pl.ds(base + i * CHUNK, CHUNK)],
            dst.at[pl.ds(i * CHUNK, CHUNK)],
            row_sems.at[which, i],
        )

    def out_copy(i, which):
        at = pl.ds(i * CHUNK, CHUNK)
        to = pl.ds(base + i * CHUNK, CHUNK)
        if which == 0:
            src, dst = qkvu_ref.at[at, :PAIR], one_hbm.at[to]
        elif which == 1:
            src, dst = qkvu_ref.at[at, PAIR:], two_hbm.at[to]
        elif which == 2:
            src, dst = unit_ref.at[at], unit_hbm.at[to]
        elif which == 3:
            src, dst = own_ref.at[:, at], own_hbm.at[:, to]
        elif which == 4:
            src, dst = stat_ref.at[:, at], stat_hbm.at[:, to]
        else:
            src, dst = qkvu_ref.at[at], head_hbm.at[to]
        return pltpu.make_async_copy(src, dst, out_sems.at[which, i])

    pairs = (*pairs, (gain_hbm, gain_ref))
    small = [pltpu.make_async_copy(src, dst, sems.at[i]) for i, (src, dst) in enumerate(pairs)]
    for copy in small:
        copy.start()
    for i in range(chunks):
        rows_copy(i, 0).start()
        rows_copy(i, 1).start()
    if lead:
        row = iota((width, cols), 0)
        col = iota((width, cols), 1)
        pick = onehot(row == col + lax.axis_index("mp") * cols)
        none = jnp.zeros((width, cols), BF)
        side_ref[:, LANES:] = jnp.concatenate([none, pick, pick, none], axis=1)
    for copy in small:
        copy.wait()
    gain = gain_ref[...]
    if lead:
        col = iota((3 * GROUP, LANES), 0)
        lane = iota((3 * GROUP, LANES), 1)
        head = sum(jnp.where(col >= 3 * HEAD * h, HEAD, 0) for h in range(1, 4))
        wide = dot_tn(wqkv_ref[...], onehot(lane == col + head)).astype(BF)
        wide_ref[...] = wide
        part = iota((GROUP, LANES), 0)
        lane = iota((GROUP, LANES), 1)
        head = sum(jnp.where(part >= HEAD * h, GROUP - HEAD, 0) for h in range(1, 4))
        up = onehot(lane == part + head + 3 * HEAD)
        side_ref[:, :LANES] = dot_tn(wproj_ref[...], up).astype(BF)
        gain_high, gain_low = split(jnp.broadcast_to(gain, (16, width)))
        wg_high, wg_low = split(dot(gain_high, wide) + dot(gain_low, wide))
        row = iota((16, LANES), 0)
        wg_ref[...] = jnp.where(
            row == 0, wg_high.astype(F32), jnp.where(row == 1, wg_low.astype(F32), 0.0)
        ).astype(BF)

    copies = []
    for i in range(chunks):
        rows_copy(i, 0).wait()
        rows_copy(i, 1).wait()
        at = slice(i * CHUNK, (i + 1) * CHUNK)
        x_low = x_ref[at, :]
        x = x_low.astype(F32)
        mean = jnp.mean(x, axis=-1, keepdims=True)
        center = x - mean
        spread = lax.rsqrt(jnp.mean(center * center, axis=-1, keepdims=True) + EPS)
        unit = (center * spread * gain).astype(BF)
        unit_ref[at, :] = unit
        from_dy = dot(dy_ref[at, :], side_ref[:, : LANES + PAIR])
        qkvu_ref[at, :] = (dot(unit, wide_ref[...]) + from_dy[:, :LANES]).astype(BF)
        own = dot(x_low, side_ref[:, LANES + PAIR :]) + from_dy[:, LANES:]
        own_ref[:, at] = own.T.astype(BF)
        both = jnp.where(iota((CHUNK, 128), 1) < 4, mean, spread)
        stat_ref[:, at] = both.T[:8, :]
        for which in range(6 if lead else 5):
            copies.append(out_copy(i, which))
            copies[-1].start()
    return copies


def project_kernel(*refs):
    for copy in project_rows(True, *refs):
        copy.wait()


def front_kernel(
    counts_ref, x_hbm, dy_hbm, gain_hbm, wide_hbm, side_hbm, head_hbm, *rest
):
    carried, outs, local_ref = rest[:5], rest[5:10], rest[10]
    (wide_ref, side_ref, *project_scratch) = rest[11:23]
    first_ref, first_sem = rest[23:25]
    half = head_hbm.shape[0]
    lower = pltpu.make_async_copy(head_hbm.at[:, :PAIR], first_ref.at[pl.ds(0, half)], first_sem.at[0])
    lower.start()
    copies = project_rows(
        False, x_hbm, dy_hbm, gain_hbm, wide_hbm, side_hbm, *carried, *outs,
        wide_ref, side_ref, *project_scratch,
    )
    qkvu_ref = project_scratch[3]
    first_ref[half:, :] = qkvu_ref[:, :PAIR]
    lower.wait()
    attend_kernel(False, 1, counts_ref, first_ref, None, local_ref, *rest[25:])
    for copy in copies:
        copy.wait()


def place_in_row(counts_ref):
    place = lax.axis_index("space")
    n_space = counts_ref.shape[0]
    start = jnp.int32(0)
    for i in range(n_space):
        start = start + jnp.where(i < place, counts_ref[i, 0, 0], 0)
    count = counts_ref[place, 0, 0]
    head_len = (PATCH - start % PATCH) % PATCH
    tail_len = jnp.where(place == n_space - 1, 0, (PATCH - (start + count) % PATCH) % PATCH)
    n_patch = (count - head_len + PATCH - 1) // PATCH
    return count, head_len, tail_len, n_patch


MARGIN = 2 * SHIFT


def shifter(first):
    part = first & (SHIFT - 1)
    pick = onehot(iota((SHIFT, 2 * SHIFT), 1) == iota((SHIFT, 2 * SHIFT), 0) + part)

    def block(src_ref, start):
        rows = src_ref.shape[0]
        base = jnp.clip(first - part + start + MARGIN, 0, rows - MARGIN)
        return dot(pick, src_ref[pl.ds(pl.multiple_of(base, SHIFT), 2 * SHIFT), :])

    return block


def padded(dst_ref, src_ref, limit, at):
    rows, width = src_ref.shape
    cols = slice(at, at + width)
    none = jnp.zeros((MARGIN, width), BF)
    dst_ref[:MARGIN, cols] = none
    dst_ref[MARGIN + rows :, cols] = none
    kept = iota(src_ref.shape, 0) < limit
    dst_ref[MARGIN : MARGIN + rows, cols] = jnp.where(
        kept, src_ref[...].astype(F32), 0.0
    ).astype(BF)


def attend_kernel(spanning, pairs, counts_ref, *rest):
    own_refs = rest[:pairs]
    if spanning:
        next_ref = rest[pairs]
        out_ref, out_next_ref = rest[pairs + 2 : pairs + 4]
        rest = rest[pairs + 4 :]
    else:
        out_ref = rest[pairs + 1]
        rest = rest[pairs + 2 :]
    (x_ref, left_ref, flip_ref, value_ref, top_ref, exp_ref, low_ref, grad_ref, turn_ref,
     done_ref, own_pad_ref, next_pad_ref) = rest
    slots = own_refs[0].shape[0]
    lanes = pairs * PAIR
    count, head_len, tail_len, n_patch = place_in_row(counts_ref)
    scale = HEAD ** (-0.5)

    def work():
        first = head_len + (PATCH * (n_patch - 1) if spanning else 0)

        for p in range(pairs):
            padded(own_pad_ref, own_refs[p], count, p * PAIR)
        from_own = shifter(first)
        if spanning:
            padded(next_pad_ref, next_ref, tail_len, 0)
            from_next = shifter(first - count)
        for start in range(0, PATCH, SHIFT):
            piece = from_own(own_pad_ref, start)
            if spanning:
                piece = piece + from_next(next_pad_ref, start)
            x_ref[start : start + SHIFT, :] = piece.astype(BF)
        x = x_ref[...]
        src = iota((lanes, lanes), 0)
        dst = iota((lanes, lanes), 1)
        sub = dst & (GROUP - 1)
        keys = sub < 2 * HEAD
        move = onehot(
            ((sub < HEAD) & (src == dst + HEAD))
            | ((sub >= HEAD) & (sub < 3 * HEAD) & (src == dst))
        )
        lane = iota((PATCH, lanes), 1) & (GROUP - 1)
        fixed = jnp.where((lane > 3 * HEAD) & (lane < 3 * HEAD + 4), 1.0, 0.0)
        if spanning:
            valid = count - first + tail_len
            row = iota((PATCH, lanes), 0)
            fixed = jnp.where((lane == 3 * HEAD) & (row >= valid), MASKED, fixed)
        left_ref[...] = (dot(x, move) + fixed).astype(BF)
        flip = dot_nt(onehot(src == dst), x)
        flip_ref[...] = flip.astype(BF)
        square = flip * flip
        most = jnp.zeros((1, 1), F32)
        for h in range(2 * pairs):
            at = h * GROUP
            value_ref[h, :HEAD, :] = flip_ref[at + 2 * HEAD : at + 3 * HEAD, :]
            value_ref[h, HEAD:, :] = jnp.ones((HEAD, PATCH), BF)
            most_q = jnp.sum(square[at : at + HEAD], axis=0, keepdims=True)
            most_k = jnp.sum(square[at + HEAD : at + 2 * HEAD], axis=0, keepdims=True)
            both = jnp.max(most_q, axis=1, keepdims=True) * jnp.max(most_k, axis=1, keepdims=True)
            most = jnp.maximum(most, both)
        bounded = jnp.max(most) * scale * scale <= SAFE * SAFE
        turn_ref[...] = jnp.zeros_like(turn_ref)
        top_ref[...] = jnp.zeros_like(top_ref)
        row = iota((HEAD, BLOCK), 0)

        def placed(pieces, h):
            zero = jnp.zeros((GROUP, BLOCK), BF)
            group = jnp.concatenate(pieces, axis=0)
            return jnp.concatenate([group, zero] if h % 2 == 0 else [zero, group], axis=0)

        nothing = jnp.zeros((HEAD, BLOCK), BF)

        def score_right(h, here, top):
            query = flip_ref[h * GROUP : h * GROUP + HEAD, here].astype(F32) * (scale * LOG2E)
            high, low = split(query)
            if top is None:
                extra = jnp.where(row == 0, 1.0, 0.0)
            else:
                top_high = top.astype(BF).astype(F32)
                top_mid = (top - top_high).astype(BF).astype(F32)
                top_low = top - top_high - top_mid
                extra = jnp.where(
                    row == 0,
                    1.0,
                    jnp.where(
                        row == 1,
                        -top_high,
                        jnp.where(row == 2, -top_mid, jnp.where(row == 3, -top_low, 0.0)),
                    ),
                )
            return placed([high, low, nothing, extra.astype(BF)], h)

        def block(pair, step, carry):
            left = left_ref.at[:, pair * PAIR : (pair + 1) * PAIR]
            here = [
                pl.ds(pl.multiple_of((step * 2 + t // 2) * BLOCK, BLOCK), BLOCK) for t in range(4)
            ]

            @pl.when(jnp.logical_not(bounded))
            def _():
                for t in range(4):
                    scores = dot(left[...], score_right(pair * 2 + t % 2, here[t], None))
                    top_ref[t : t + 1, :] = jnp.max(scores, axis=0, keepdims=True)

            inverses = [None] * 4
            rights = [None] * 4
            spans = [
                slice((t % 2 * 2 + t // 2) * BLOCK, (t % 2 * 2 + t // 2 + 1) * BLOCK)
                for t in range(4)
            ]
            ups = [None] * 4
            queries = [None] * 4

            def stage_exp(t):
                scores = dot(left[...], score_right(pair * 2 + t % 2, here[t], top_ref[t : t + 1, :]))
                exps = jnp.exp2(scores)
                exp_ref[t] = exps
                low_ref[:, spans[t]] = exps.astype(BF)

            def stage_sum(t):
                at = (pair * 2 + t % 2) * GROUP
                result = dot(value_ref[pair * 2 + t % 2], low_ref[:, spans[t]])
                inverse = 1.0 / result[HEAD : HEAD + 1]
                inverses[t] = inverse
                attended = result[:HEAD] * inverse
                turn_ref[at + 3 * HEAD : at + 4 * HEAD, here[t]] = attended
                up = flip_ref[at + 3 * HEAD : at + 4 * HEAD, here[t]].astype(F32)
                scaled = up * scale
                delta = jnp.sum(scaled * attended, axis=0, keepdims=True)
                delta_high = delta.astype(BF).astype(F32)
                extra = jnp.where(
                    row == 1, -delta_high, jnp.where(row == 2, delta_high - delta, 0.0)
                ).astype(BF)
                rights[t] = placed([nothing, nothing, scaled.astype(BF), extra], t % 2)
                query = flip_ref[at : at + HEAD, here[t]].astype(F32)
                ups[t] = (up * inverse).astype(BF)
                queries[t] = (query * inverse).astype(BF)

            def stage_grad(t):
                dprob = dot(left[...], rights[t])
                grad_ref[:, spans[t]] = (exp_ref[t] * dprob).astype(BF)

            def stage_query(t):
                at = (pair * 2 + t % 2) * GROUP
                result = dot(flip_ref[at + HEAD : at + 2 * HEAD, :], grad_ref[:, spans[t]])
                turn_ref[at : at + HEAD, here[t]] = result * inverses[t]

            for stage in (stage_exp, stage_sum, stage_grad, stage_query):
                for t in range(4):
                    stage(t)
            for h in range(2):
                at = (pair * 2 + h) * GROUP
                both = slice(2 * h * BLOCK, 2 * (h + 1) * BLOCK)
                turn_ref[at + 2 * HEAD : at + 3 * HEAD, :] += dot_nt(
                    jnp.concatenate([ups[h], ups[h + 2]], axis=1), low_ref[:, both]
                )
                turn_ref[at + HEAD : at + 2 * HEAD, :] += dot_nt(
                    jnp.concatenate([queries[h], queries[h + 2]], axis=1), grad_ref[:, both]
                )
            return carry

        for pair in range(pairs):
            lax.fori_loop(0, PATCH // (2 * BLOCK), functools.partial(block, pair), 0)
        done_ref[:MARGIN, :] = jnp.zeros((MARGIN, lanes), BF)
        done_ref[MARGIN + PATCH :, :] = jnp.zeros((MARGIN, lanes), BF)
        done_ref[MARGIN : MARGIN + PATCH, :] = turn_ref[...].T.astype(BF)
        row = iota((SHIFT, lanes), 0)
        to_own = shifter(-first)
        for start in range(0, slots, SHIFT):
            piece = to_own(done_ref, start)
            out_ref[start : start + SHIFT, :] = jnp.where(
                row < count - start, piece, 0.0
            ).astype(BF)
        if spanning:
            to_next = shifter(count - first)
            for start in range(0, PATCH, SHIFT):
                piece = to_next(done_ref, start)
                out_next_ref[start : start + SHIFT, :] = jnp.where(
                    row < tail_len - start, piece, 0.0
                ).astype(BF)

    if spanning:
        work()
    else:
        pl.when(n_patch == 2)(work)

        @pl.when(n_patch < 2)
        def _():
            out_ref[...] = jnp.zeros_like(out_ref)


def product_kernel(lower, mine_ref, a_ref, b_ref, one_ref, two_ref, wide_ref, wg_ref, *rest):
    if lower:
        got_ref = rest[0]
        rest = rest[4:]
    keep_ref, send_ref, total_ref, turned_ref = rest
    step = pl.program_id(0)
    rows = a_ref.shape[0]
    core = lax.axis_index("mp") % 2
    cols = wide_ref.shape[0] // 8

    @pl.when(step == 0)
    def _():
        for side in range(2):
            for x in range(4):
                from_row = pl.multiple_of((2 * x + (core ^ side)) * cols, cols)
                to_row = (side * 4 + x) * cols
                turned_ref[to_row : to_row + cols, :] = wide_ref[pl.ds(from_row, cols), :]

    local = jnp.concatenate([a_ref[...], b_ref[...]], axis=1)
    wide_total = mine_ref[...].astype(F32) + local.astype(F32)
    if lower:
        wide_total = wide_total + got_ref[...].astype(F32)
    total = wide_total.astype(BF)
    total_ref[...] = total
    du = dot_nt(turned_ref[...], total).astype(BF)
    half = 4 * cols
    keep_ref[:half, :] = du[:half]
    send_ref[:half, :] = du[half:]
    lane = iota((rows, LANES), 1) & (GROUP - 1)
    qkvu = jnp.concatenate([one_ref[...], two_ref[...]], axis=1).astype(F32)
    product = jnp.where(lane < 3 * HEAD, wide_total * qkvu, 0.0)
    high, low = split(product)
    ones = jnp.ones((16, LANES), BF)
    second = (dot_nt(ones, high) + dot_nt(ones, low))[:1]
    first_rows = dot_nt(wg_ref[...], total)
    first = first_rows[:1] + first_rows[1:2]
    stats = pack_stats(first, second, rows)
    keep_ref[half:, :] = stats
    send_ref[half:, :] = stats


def weight_kernel(total_ref, unit_ref, dy_ref, after_ref, grads_ref, gu_ref, gy_ref):
    step = pl.program_id(0)

    @pl.when(step == 0)
    def _():
        gu_ref[...] = jnp.zeros_like(gu_ref)
        gy_ref[...] = jnp.zeros_like(gy_ref)

    total = total_ref[...]
    gu_ref[...] += dot_tn(total, unit_ref[...])
    gy_ref[...] += dot_tn(total, dy_ref[...])

    @pl.when(step == pl.num_programs(0) - 1)
    def _():
        row = iota(gu_ref.shape, 0) & (GROUP - 1)
        grads_ref[...] = jnp.where(row < 3 * HEAD, gu_ref[...], gy_ref[...]).T.astype(BF)


def pack_stats(first, second, rows):
    row = iota((16, rows), 0)
    first_high = first.astype(BF).astype(F32)
    second_high = second.astype(BF).astype(F32)
    return jnp.where(
        row == 0,
        first_high,
        jnp.where(
            row == 1,
            first - first_high,
            jnp.where(row == 2, second_high, jnp.where(row == 3, second - second_high, 0.0)),
        ),
    ).astype(BF)


def pair_kernel(keep_ref, got_ref, after_ref, out0_ref, out1_ref, out2_ref, out3_ref):
    x = lax.axis_index("mp") // 2
    rows = keep_ref.shape[1]
    half = keep_ref.shape[0] - 16
    cols = half // 4
    stats = keep_ref[half:, :].astype(F32) + got_ref[half:, :].astype(F32)
    packed = pack_stats(stats[0:1] + stats[1:2], stats[2:3] + stats[3:4], rows).astype(F32)
    folded = jnp.concatenate(
        [packed[i : i + 1, j : j + 128] for i in range(4) for j in range(0, rows, 128)], axis=0
    ).astype(BF)
    for d, out_ref in enumerate((out0_ref, out1_ref, out2_ref, out3_ref)):
        at = pl.ds(pl.multiple_of(((x + d) % 4) * cols, cols), cols)
        both = keep_ref[at, :].astype(F32) + got_ref[at, :].astype(F32)
        out_ref[:, :rows] = both.astype(BF)
        out_ref[:, rows:] = folded


def finish_kernel(
    counts_ref, a_ref, b_ref, c_ref, d_ref, own_ref, stat_ref, gain_ref, grads_ref,
    points_ref, qkv_ref, proj_ref,
):
    rows = a_ref.shape[1] - 128
    cols = own_ref.shape[0] // 2
    width = gain_ref.shape[1]
    parts = [ref[...].astype(F32) for ref in (a_ref, b_ref, c_ref, d_ref)]
    total = (parts[0] + parts[1]) + (parts[2] + parts[3])
    folded = total[:, rows:]
    total = total[:, :rows]
    each = rows // 128
    firsts = (folded[:each] + folded[each : 2 * each]) * (1.0 / width)
    seconds = (folded[2 * each : 3 * each] + folded[3 * each : 4 * each]) * (1.0 / width)
    first = jnp.concatenate([firsts[i : i + 1] for i in range(each)], axis=1)
    second = jnp.concatenate([seconds[i : i + 1] for i in range(each)], axis=1)
    mine = iota((cols, width), 1) == iota((cols, width), 0) + lax.axis_index("mp") * cols
    gain = jnp.sum(jnp.where(mine, gain_ref[...], 0.0), axis=1, keepdims=True)
    mean = stat_ref[0:1, :]
    spread = stat_ref[4:5, :]
    normed = (own_ref[:cols, :].astype(F32) - mean) * spread
    dnorm = spread * (total * gain - first - normed * second)
    out = own_ref[cols:, :].astype(F32) + dnorm
    slot = iota((cols, rows), 1)
    points_ref[...] = jnp.where(slot < counts_ref[lax.axis_index("space"), 0, 0], out, 0.0).astype(BF)

    grads = jnp.sum(grads_ref[...].astype(F32), axis=0)
    qkv_ref[...] = jnp.concatenate(
        [grads[:, h * GROUP : h * GROUP + 3 * HEAD] for h in range(4)], axis=1
    )
    proj_ref[...] = jnp.concatenate(
        [grads[:, h * GROUP + 3 * HEAD : (h + 1) * GROUP] for h in range(4)], axis=1
    )


def whole(shape):
    return pl.BlockSpec(shape, lambda *_: (0,) * len(shape))


ANY = pl.BlockSpec(memory_space=pl.ANY)
shape = jax.ShapeDtypeStruct


SMEM = pl.BlockSpec(memory_space=pltpu.SMEM)


def call(kernel, args, grid, in_specs, out_specs, out_shape, scratch, limit, micros, aliases={}):
    return pl.pallas_call(
        kernel,
        grid=grid,
        in_specs=in_specs,
        out_specs=out_specs,
        scratch_shapes=scratch,
        out_shape=out_shape,
        input_output_aliases=aliases,
        cost_estimate=pl.CostEstimate(
            flops=int(micros * 1.1e9), bytes_accessed=0, transcendentals=0
        ),
        compiler_params=pltpu.CompilerParams(vmem_limit_bytes=int(limit * MIB)),
    )(*args)


def project(counts, points, cotangent, gain, w_qkv, w_proj):
    slots, width = points.shape
    cols = width // 8
    half = slots // 2
    points, cotangent, gain, w_qkv, w_proj = (
        pltpu.with_memory_space_constraint(a, pltpu.HBM)
        for a in (points, cotangent, gain, w_qkv, w_proj)
    )
    chunks = half // CHUNK
    outs = [
        shape((slots, PAIR), BF),
        shape((slots, PAIR), BF),
        pltpu.HBM((slots, width), BF),
        shape((2 * cols, slots), BF),
        shape((8, slots), F32),
    ]
    head = shape((half, LANES), BF)
    extra = [shape((width, LANES), BF), shape((width, LANES + 2 * PAIR), BF), shape((16, LANES), BF)]
    scratch = [
        pltpu.VMEM((half, width), BF),
        pltpu.VMEM((half, width), BF),
        pltpu.VMEM(gain.shape, F32),
        pltpu.VMEM((half, LANES), BF),
        pltpu.VMEM((half, width), BF),
        pltpu.VMEM((2 * cols, half), BF),
        pltpu.VMEM((8, half), F32),
        pltpu.SemaphoreType.DMA((2, chunks)),
        pltpu.SemaphoreType.DMA((3,)),
        pltpu.SemaphoreType.DMA((6, chunks)),
    ]
    results = call(
        project_kernel,
        (points, cotangent, gain, w_qkv, w_proj),
        (1,),
        [ANY] * 5,
        [ANY] * 6 + [whole(e.shape) for e in extra],
        outs + [head] + extra,
        [pltpu.VMEM(w_qkv.shape, BF), pltpu.VMEM(w_proj.shape, BF)] + scratch,
        32,
        4.5,
    )
    head, wide, side, wg = results[5:]
    carried = list(results[:5])
    carried[2] = pltpu.with_memory_space_constraint(carried[2], pltpu.HBM)
    outs = outs + [shape((slots, PAIR), BF)]
    again = call(
        front_kernel,
        (counts, points, cotangent, gain, wide, side, head, *carried),
        (1,),
        [SMEM] + [ANY] * 11,
        [ANY] * 5 + [whole((slots, PAIR))],
        outs,
        [pltpu.VMEM(e.shape, BF) for e in extra[:2]]
        + scratch
        + [pltpu.VMEM((slots, PAIR), BF), pltpu.SemaphoreType.DMA((1,))]
        + attend_scratch(slots, 1),
        32,
        11.0,
        {7 + i: i for i in range(5)},
    )
    return (*again, head, wide, wg)


def count_kernel(cells_ref, out_ref):
    total = jnp.sum(cells_ref[...].astype(F32), axis=1, keepdims=True).astype(jnp.int32)
    out_ref[...] = jnp.broadcast_to(total.reshape(1, 1, 1), out_ref.shape)


def count(cells, n_space):
    out = shape((n_space, 1, 128), jnp.int32)
    cells = cells.reshape(1, -1)
    return call(
        count_kernel, (cells,), (1,), [whole(cells.shape)], whole(out.shape), out, [], 1, 0.5
    )


def attend_scratch(slots, pairs):
    lanes = pairs * PAIR
    return [
        pltpu.VMEM((PATCH, lanes), BF),
        pltpu.VMEM((PATCH, lanes), BF),
        pltpu.VMEM((lanes, PATCH), BF),
        pltpu.VMEM((2 * pairs, 2 * HEAD, PATCH), BF),
        pltpu.VMEM((8, BLOCK), F32),
        pltpu.VMEM((4, PATCH, BLOCK), F32),
        pltpu.VMEM((PATCH, 4 * BLOCK), BF),
        pltpu.VMEM((PATCH, 4 * BLOCK), BF),
        pltpu.VMEM((lanes, PATCH), F32),
        pltpu.VMEM((PATCH + 2 * MARGIN, lanes), BF),
        pltpu.VMEM((slots + 2 * MARGIN, lanes), BF),
        pltpu.VMEM((PATCH + 2 * MARGIN, lanes), BF),
    ]


def attend(spanning, counts, owns, following, after):
    slots = owns[0].shape[0]
    pairs = len(owns)
    lanes = pairs * PAIR
    outs = [shape((slots, lanes), BF)] + ([shape((PATCH, lanes), BF)] if spanning else [])
    args = (*owns, following) if spanning else tuple(owns)
    return call(
        functools.partial(attend_kernel, spanning, pairs),
        (counts, *args, after),
        (1,),
        [SMEM] + [whole(a.shape) for a in args] + [ANY],
        [whole(o.shape) for o in outs],
        outs,
        attend_scratch(slots, pairs),
        24,
        7.5 * pairs,
    )


def products(mine, locals_, got, heads, wide, wg):
    slots = mine.shape[0]
    width = wide.shape[0]
    rows = 512
    half = width // 2 + 16
    outs = [shape((half, slots), BF), shape((half, slots), BF), shape((slots, LANES), BF)]
    steps = PATCH // rows

    def part(offset, more, more_specs, steps, aliases):
        down = pl.BlockSpec((rows, PAIR), lambda i: (i + offset, 0))
        full = pl.BlockSpec((rows, LANES), lambda i: (i + offset, 0))
        across = pl.BlockSpec((half, rows), lambda i: (0, i + offset))
        return call(
            functools.partial(product_kernel, bool(more)),
            (mine, *locals_, *heads, wide, wg, *more),
            (steps,),
            [full, down, down, down, down, whole(wide.shape), whole(wg.shape)] + more_specs,
            [across, across, full],
            outs,
            [pltpu.VMEM((width, LANES), BF)],
            16,
            2.0,
            aliases,
        )

    upper = part(steps, (), [], slots // rows - steps, {})
    row = pl.BlockSpec((rows, LANES), lambda i: (i, 0))
    return part(0, (got, *upper), [row] + [ANY] * 3, steps, {8 + i: i for i in range(3)})


def weights(total, unit, dy, after):
    slots, width = unit.shape
    rows = 1024
    down = lambda i: (i, 0)
    return call(
        weight_kernel,
        (total, unit, dy, after),
        (slots // rows,),
        [
            pl.BlockSpec((rows, LANES), down),
            pl.BlockSpec((rows, width), down),
            pl.BlockSpec((rows, width), down),
            ANY,
        ],
        [whole((width, LANES))],
        [shape((width, LANES), BF)],
        [pltpu.VMEM((LANES, width), F32), pltpu.VMEM((LANES, width), F32)],
        24,
        4.0,
    )[0]


def pair_sum(keep, got, after):
    total, slots = keep.shape
    out = shape(((total - 16) // 4, slots + 128), BF)
    return call(
        pair_kernel,
        (keep, got, after),
        (1,),
        [whole(keep.shape)] * 2 + [ANY],
        [whole(out.shape)] * 4,
        [out] * 4,
        [],
        24,
        2.3,
    )


def finish(counts, parts, own, stat, gain, grads):
    cols, slots = own.shape
    rows = grads.shape[1]
    outs = [
        shape((cols // 2, slots), BF),
        shape((rows, 3 * GROUP), F32),
        shape((rows, GROUP), F32),
    ]
    args = (*parts, own, stat, gain, grads)
    points, qkv, proj = call(
        finish_kernel,
        (counts, *args),
        (1,),
        [SMEM] + [whole(a.shape) for a in args],
        [whole(o.shape) for o in outs],
        outs,
        [],
        24,
        2.3,
    )
    return points.T, qkv, proj.T


def on_device(points, cotangent, cell_counts, norm_gain, w_qkv, w_proj):
    slots, width = points.shape
    n_space = lax.axis_size("space")
    n_mp = lax.axis_size("mp")
    counts = lax.all_to_all(count(cell_counts, n_space), "space", 0, 0)
    gain = norm_gain.reshape(1, width)
    one, two, unit, own, stat, local_a, head, wide, wg = project(
        counts, points, cotangent, gain, w_qkv.T, w_proj
    )
    back = [(i + 1, i) for i in range(n_space - 1)]
    onward = [(i, i + 1) for i in range(n_space - 1)]
    following = lax.ppermute(head, "space", back)
    mine, spill = attend(True, counts, (one, two), following, one)
    got = lax.ppermute(spill, "space", onward)
    local_b = attend(False, counts, (two,), None, mine)[0]
    keep, send, total = products(mine, (local_a, local_b), got, (one, two), wide, wg)
    swap = [(i, i ^ 1) for i in range(n_mp)]
    other = lax.ppermute(send, "mp", swap)
    grads = weights(total, unit, cotangent, keep)
    gathered = lax.all_to_all(
        grads.reshape(n_space, width // n_space, LANES), "space", 0, 0
    )
    parts = pair_sum(keep, other, grads)
    received = [parts[0]]
    for d in range(1, n_mp // 2):
        route = [(i, (i + 2 * d) % n_mp) for i in range(n_mp)]
        received.append(lax.ppermute(parts[d], "mp", route))
    return finish(counts, received, own, stat, gain, gathered)


def solution(mesh):
    return jax.shard_map(
        on_device,
        mesh=mesh,
        in_specs=(
            P("space", None),
            P("space", None),
            P("space"),
            P(),
            P(None, "mp"),
            P("mp", None),
        ),
        out_specs=(P("space", "mp"), P("space", "mp"), P("mp", "space")),
        check_vma=False,
    )
```
